32 devices in a mesh: dp: 8 (over z, x), head: 4 (over y, core).
Axes of the slice: x: 2, y: 2, z: 4, core: 2. Of those that a mesh axis runs over, the one named last changes fastest.
Arguments:
- tokens: bfloat16 [131072, 128], P(('dp', 'head')), may hold values from -6 to 6
- cotangent: bfloat16 [131072, 128], P(('dp', 'head')), may hold values from -6 to 6
- lengths: int32 [32, 8], P('dp'), may hold values from 1 to 1024, 4096 in all within a row
- qkv_master: float32 [128, 384], P('dp', 'head'), may hold values from -0.61871843 to 0.61871843
- out_master: float32 [128, 128], P(('dp', 'head')), may hold values from -3 to 3
- up_master: float32 [128, 512], P('dp', 'head'), may hold values from -1.14904852 to 1.14904852
- down_master: float32 [128, 512], P('dp', 'head'), may hold values from -0.5745243 to 0.5745243
- norm_master: float32 [128, 4], P(('dp', 'head')), may hold values from -1.2 to 2.8
- qkv_first: float32 [128, 384], P('dp', 'head'), may hold values from -0.0078125 to 0.0078125
- out_first: float32 [128, 128], P(('dp', 'head')), may hold values from -0.0078125 to 0.0078125
- up_first: float32 [128, 512], P('dp', 'head'), may hold values from -0.0078125 to 0.0078125
- down_first: float32 [128, 512], P('dp', 'head'), may hold values from -0.0078125 to 0.0078125
- norm_first: float32 [128, 4], P(('dp', 'head')), may hold values from -0.0078125 to 0.0078125
- qkv_second: float32 [128, 384], P('dp', 'head'), may hold values from 1.5853287e-07 to 2.536526e-06
- out_second: float32 [128, 128], P(('dp', 'head')), may hold values from 1.5853287e-07 to 2.536526e-06
- up_second: float32 [128, 512], P('dp', 'head'), may hold values from 1.5853287e-07 to 2.536526e-06
- down_second: float32 [128, 512], P('dp', 'head'), may hold values from 1.5853287e-07 to 2.536526e-06
- norm_second: float32 [128, 4], P(('dp', 'head')), may hold values from 1.5853287e-07 to 2.536526e-06
Outputs:
- mixed: bfloat16 [131072, 128], P(('dp', 'head'))
- input_grad: bfloat16 [131072, 128], P(('dp', 'head'))
- grad_norm: float32 [], replicated
- qkv_new: float32 [128, 384], P('dp', 'head')
- qkv_first_new: float32 [128, 384], P('dp', 'head')
- qkv_second_new: float32 [128, 384], P('dp', 'head')
- out_new: float32 [128, 128], P(('dp', 'head'))
- out_first_new: float32 [128, 128], P(('dp', 'head'))
- out_second_new: float32 [128, 128], P(('dp', 'head'))
- up_new: float32 [128, 512], P('dp', 'head')
- up_first_new: float32 [128, 512], P('dp', 'head')
- up_second_new: float32 [128, 512], P('dp', 'head')
- down_new: float32 [128, 512], P('dp', 'head')
- down_first_new: float32 [128, 512], P('dp', 'head')
- down_second_new: float32 [128, 512], P('dp', 'head')
- norm_new: float32 [128, 4], P(('dp', 'head'))
- norm_first_new: float32 [128, 4], P(('dp', 'head'))
- norm_second_new: float32 [128, 4], P(('dp', 'head'))
- qkv_grad: float32 [128, 384], P('dp', 'head')
- out_grad: float32 [128, 128], P(('dp', 'head'))
- up_grad: float32 [128, 512], P('dp', 'head')
- down_grad: float32 [128, 512], P('dp', 'head')
- norm_grad: float32 [128, 4], P(('dp', 'head'))
- qkv_copy: bfloat16 [128, 384], P('dp', 'head')
- out_copy: bfloat16 [128, 128], P(('dp', 'head'))
- up_copy: bfloat16 [128, 512], P('dp', 'head')
- down_copy: bfloat16 [128, 512], P('dp', 'head')
- norm_copy: bfloat16 [128, 4], P(('dp', 'head'))
The draws below stay inside these ranges and needn't reach their ends.
Inputs may be any that keep to these rules, and one draw needn't show every extreme that they name: `lengths`: each packed row holds 8 whole windows that fill it; the longest is 1024 tokens.
All inputs are finite; a program needn't handle non-finite values.
Results may differ from the reference program's by a relative error of at most 0.023.
Values may be sent and summed in bfloat16 or wider, within the bound.
A program may use at most 192 MiB of HBM per device.

```python
import math
import jax
import jax.numpy as jnp
import numpy as np
from jax import lax

D = 128
HEADS = 4
HD = 32
FF = 512
ROW_LEN = 4096
MAX_LEN = 1024
SEGS = 8
BLOCK = 512
STEP = 5
TOKENS = 131072
ROWS = 32


def rough(key, shape, lower, upper):
    return jax.random.uniform(key, shape, jnp.float32, lower, upper)


def column_rise(count, top):
    place = jnp.arange(count, dtype=jnp.float32) / (count - 1)
    return top ** (place - 0.5)


def draw_qkv_master(key, part):
    key = jax.random.fold_in(key, 11)
    first_key, second_key = jax.random.split(key)
    base = jax.random.truncated_normal(first_key, -4.0, 4.0, (D, 3 * D), jnp.float32)
    top = 3.0
    heads = (jnp.arange(3 * D) // (3 * HD)).astype(jnp.float32) / (HEADS - 1)
    lift = top ** (0.25 * (heads - 0.5))
    return base * rough(second_key, (D, 3 * D), 0.7, 1.4) * lift[None, :] * D ** (-0.5)


def draw_up_master(key, part):
    key = jax.random.fold_in(key, 23)
    first_key, second_key = jax.random.split(key)
    base = jax.random.truncated_normal(first_key, -4.0, 4.0, (D, FF), jnp.float32)
    top = 3.0
    return base * rough(second_key, (D, FF), 0.7, 1.4) * column_rise(FF, top)[None, :] * D ** (-0.5)


def draw_down_master(key, part):
    key = jax.random.fold_in(key, 37)
    first_key, second_key = jax.random.split(key)
    base = jax.random.truncated_normal(first_key, -4.0, 4.0, (D, FF), jnp.float32)
    top = 3.0
    return base * rough(second_key, (D, FF), 0.7, 1.4) * column_rise(FF, top)[None, :] * FF ** (-0.5)


def draw_norm_master(key, part):
    key = jax.random.fold_in(key, 41)
    first_key, second_key = jax.random.split(key)
    shifts = jax.random.truncated_normal(first_key, -4.0, 4.0, (D, 2), jnp.float32) * 0.3
    top = 3.0
    gains = column_rise(D, top)[:, None] * rough(second_key, (D, 2), 0.8, 1.25)
    return jnp.stack([gains[:, 0], shifts[:, 0], gains[:, 1], shifts[:, 1]], axis=1)


def block_scale(rng, shape, shards, least, top_value):
    level = 1.0
    for position, blocks in shards:
        steps = jax.random.uniform(jax.random.fold_in(jax.random.fold_in(rng, 6), position), (blocks,), jnp.float32, least / len(shards), top_value / len(shards))
        level = level * jnp.repeat(jnp.exp(steps), shape[position] // blocks).reshape((-1,) + (1,) * (len(shape) - 1 - position))
    return level


def split_up(count, total, bound, lean):
    portions = [(1 << 20) // math.isqrt(grade ** lean) + 1 for grade in range(2, count + 1)]
    surplus, holding = total - bound - (count - 1), [1] * (count - 1)
    while surplus > 0:
        candidates = [i for i in range(count - 1) if holding[i] < bound]
        mass, left = sum([portions[i] for i in candidates]), surplus
        for i in candidates:
            more = min(bound - holding[i], max(1, left * portions[i] // mass), surplus)
            holding[i] = holding[i] + more
            surplus = surplus - more
    return np.array([bound] + holding)


def uneven(stream_key, count, total, limit, skew):
    if count == 2:
        one = jax.random.randint(stream_key, (), max(1, total - limit), min(limit, total - 1) + 1)
        return jnp.stack([one, total - one])
    tallies = jnp.asarray(split_up(count, total, limit, skew), jnp.int32)
    twos = (count - 1) // 2
    giver, receiver = tallies[1:1 + 2 * twos:2], tallies[2:2 + 2 * twos:2]
    room = jnp.minimum(giver - 1, limit - receiver)
    shifted = jax.random.randint(jax.random.fold_in(stream_key, 1), (twos,), 0, 1 << 20) % (room + 1)
    tallies = tallies.at[1:1 + 2 * twos:2].set(giver - shifted).at[2:2 + 2 * twos:2].set(receiver + shifted)
    return tallies[jax.random.permutation(jax.random.fold_in(stream_key, 2), count)]


def bell_draw(own_key, dims, scale, reach, cuts=(), kind=jnp.bfloat16):
    result = scale * jax.random.normal(own_key, dims, jnp.float32)
    if cuts:
        result = result * block_scale(own_key, dims, cuts, -0.22, 0.18)
    return jnp.clip(result, -reach, reach).astype(kind)


def setup_inputs(seed: int = 0) -> dict:
    arg_keys = jax.random.split(jax.random.key(seed), 19)
    tokens = bell_draw(arg_keys[0], (TOKENS, D), 1.0, 6.0, ((0, 32),))
    cotangent = bell_draw(arg_keys[1], (TOKENS, D), 1.0, 6.0, ((0, 32),))
    lengths = jax.vmap(lambda own: uneven(own, SEGS, ROW_LEN, MAX_LEN, 1))(jax.random.split(arg_keys[2], ROWS)).reshape((ROWS, SEGS)).astype(jnp.int32)
    qkv_master = draw_qkv_master(jax.random.fold_in(arg_keys[18], 71), 0)
    out_master = bell_draw(arg_keys[4], (D, D), 4 ** -0.5, 3.0, ((0, 32),), jnp.float32)
    up_master = draw_up_master(jax.random.fold_in(arg_keys[18], 71), 0)
    down_master = draw_down_master(jax.random.fold_in(arg_keys[18], 71), 0)
    norm_master = draw_norm_master(jax.random.fold_in(arg_keys[18], 71), 0)
    qkv_first = bell_draw(arg_keys[8], (D, 3 * D), ((16 * (4 * D * D + 2 * D * FF + 4 * D)) ** -0.5), 0.0078125, ((0, 8), (1, 4)), jnp.float32)
    out_first = bell_draw(arg_keys[9], (D, D), ((16 * (4 * D * D + 2 * D * FF + 4 * D)) ** -0.5), 0.0078125, ((0, 32),), jnp.float32)
    up_first = bell_draw(arg_keys[10], (D, FF), ((16 * (4 * D * D + 2 * D * FF + 4 * D)) ** -0.5), 0.0078125, ((0, 8), (1, 4)), jnp.float32)
    down_first = bell_draw(arg_keys[11], (D, FF), ((16 * (4 * D * D + 2 * D * FF + 4 * D)) ** -0.5), 0.0078125, ((0, 8), (1, 4)), jnp.float32)
    norm_first = bell_draw(arg_keys[12], (D, 4), ((16 * (4 * D * D + 2 * D * FF + 4 * D)) ** -0.5), 0.0078125, ((0, 32),), jnp.float32)
    qkv_second = jnp.clip(jnp.exp(math.log(2.536525926188915e-06) - 2.7725887 * jax.random.uniform(arg_keys[13], (D, 3 * D), jnp.float32) ** block_scale(arg_keys[13], (D, 3 * D), ((0, 8), (1, 4)), -0.2, 0.2)), 1.585328703868072e-07, 2.536525926188915e-06)
    out_second = jnp.clip(jnp.exp(math.log(2.536525926188915e-06) - 2.7725887 * jax.random.uniform(arg_keys[14], (D, D), jnp.float32) ** block_scale(arg_keys[14], (D, D), ((0, 32),), -0.2, 0.2)), 1.585328703868072e-07, 2.536525926188915e-06)
    up_second = jnp.clip(jnp.exp(math.log(2.536525926188915e-06) - 2.7725887 * jax.random.uniform(arg_keys[15], (D, FF), jnp.float32) ** block_scale(arg_keys[15], (D, FF), ((0, 8), (1, 4)), -0.2, 0.2)), 1.585328703868072e-07, 2.536525926188915e-06)
    down_second = jnp.clip(jnp.exp(math.log(2.536525926188915e-06) - 2.7725887 * jax.random.uniform(arg_keys[16], (D, FF), jnp.float32) ** block_scale(arg_keys[16], (D, FF), ((0, 8), (1, 4)), -0.2, 0.2)), 1.585328703868072e-07, 2.536525926188915e-06)
    norm_second = jnp.clip(jnp.exp(math.log(2.536525926188915e-06) - 2.7725887 * jax.random.uniform(arg_keys[17], (D, 4), jnp.float32) ** block_scale(arg_keys[17], (D, 4), ((0, 32),), -0.2, 0.2)), 1.585328703868072e-07, 2.536525926188915e-06)
    return dict(tokens=tokens, cotangent=cotangent, lengths=lengths, qkv_master=qkv_master, out_master=out_master, up_master=up_master, down_master=down_master, norm_master=norm_master, qkv_first=qkv_first, out_first=out_first, up_first=up_first, down_first=down_first, norm_first=norm_first, qkv_second=qkv_second, out_second=out_second, up_second=up_second, down_second=down_second, norm_second=norm_second)


@jax.custom_vjp
def low(v):
    return lax.optimization_barrier(v.astype(jnp.bfloat16)).astype(jnp.float32)

@jax.custom_vjp
def low_back(v):
    return v

def low_keep(v):
    return (low(v), None)

def low_pass(kept, grad):
    return (grad,)

def back_keep(v):
    return (v, None)

def back_low(kept, grad):
    return (low(grad),)
low.defvjp(low_keep, low_pass)
low_back.defvjp(back_keep, back_low)
NORM_EPS = 1e-05
CLIP_NORM = 0.25
BETA_ONE = 0.5
BETA_TWO = 0.5
ADAM_EPS = 1e-08
DECAY = 0.1
MASKED = -1e+30
HIGHEST = lax.Precision.HIGHEST

def matmul_high(left, right):
    return jnp.dot(left, right, precision=HIGHEST, preferred_element_type=jnp.float32)

def layer_norm(value, gain, shift):
    mean = lax.optimization_barrier(jnp.mean(value, axis=-1, keepdims=True))
    centred = value - mean
    spread = lax.optimization_barrier(jnp.mean(centred * centred, axis=-1, keepdims=True))
    return centred * lax.rsqrt(spread + NORM_EPS) * gain + shift

def segment_ids(lengths):
    ends = jnp.cumsum(lengths, axis=1).astype(jnp.int32)
    place = jnp.arange(ROW_LEN, dtype=jnp.int32)
    inside = lax.optimization_barrier(jnp.sum((place[None, :, None] >= ends[:, None, :]).astype(jnp.int32), axis=2)).astype(jnp.int32)
    offset = (jnp.arange(lengths.shape[0], dtype=jnp.int32) * lengths.shape[1]).astype(jnp.int32)
    return (inside + offset[:, None]).astype(jnp.int32)

def attend(query, keys, values, segment):
    scale = HD ** (-0.5)
    span = MAX_LEN + BLOCK
    pad_keys = jnp.concatenate([jnp.zeros((MAX_LEN, HEADS, HD), jnp.float32), keys], axis=0)
    pad_values = jnp.concatenate([jnp.zeros((MAX_LEN, HEADS, HD), jnp.float32), values], axis=0)
    pad_segment = jnp.concatenate([jnp.full((MAX_LEN,), -1, jnp.int32), segment.astype(jnp.int32)]).astype(jnp.int32)

    def block(start):
        query_block = lax.dynamic_slice_in_dim(query, start, BLOCK, 0)
        key_block = lax.dynamic_slice_in_dim(pad_keys, start, span, 0)
        value_block = lax.dynamic_slice_in_dim(pad_values, start, span, 0)
        query_seg = lax.dynamic_slice_in_dim(segment, start, BLOCK, 0)
        key_seg = lax.dynamic_slice_in_dim(pad_segment, start, span, 0)
        query_place = start + jnp.arange(BLOCK, dtype=jnp.int32)
        key_place = start - MAX_LEN + jnp.arange(span, dtype=jnp.int32)
        allowed = (query_seg[:, None] == key_seg[None, :]) & (key_place[None, :] <= query_place[:, None])
        scores = low_back(jnp.einsum('qhd,khd->hqk', query_block, key_block, precision=HIGHEST) * scale)
        scores = jnp.where(allowed[None], scores, MASKED)
        top = lax.optimization_barrier(jnp.max(scores, axis=-1, keepdims=True))
        weights = jnp.exp(scores - top)
        probs = weights / lax.optimization_barrier(jnp.sum(weights, axis=-1, keepdims=True))
        return jnp.einsum('hqk,khd->qhd', low(probs), value_block, precision=HIGHEST)
    starts = (jnp.arange(ROW_LEN // BLOCK, dtype=jnp.int32) * BLOCK).astype(jnp.int32)
    return lax.map(jax.checkpoint(block), starts).reshape(ROW_LEN, HEADS, HD)

def forward(params, row_in, segment):
    w_qkv, w_out, w_up, w_down, norms = [low(weight) for weight in params]
    first = low(layer_norm(row_in, norms[:, 0], norms[:, 1]))
    packed = low(low_back(matmul_high(first, w_qkv))).reshape(ROW_LEN, HEADS, 3, HD)
    attended = attend(packed[:, :, 0], packed[:, :, 1], packed[:, :, 2], segment)
    heads = low(low_back(attended.reshape(ROW_LEN, D)))
    resid = row_in + low_back(matmul_high(heads, w_out))
    second = low(layer_norm(resid, norms[:, 2], norms[:, 3]))
    hidden_pre = low_back(matmul_high(second, w_up))
    hidden = low(jax.nn.gelu(hidden_pre, approximate=False))
    return resid + matmul_high(hidden, w_down.T)

def adam(weight, first, second, grad, factor, rate, decay):
    clipped = grad * factor
    first_new = BETA_ONE * first + (1.0 - BETA_ONE) * clipped
    second_new = BETA_TWO * second + (1.0 - BETA_TWO) * clipped * clipped
    direction = first_new / (1.0 - BETA_ONE ** STEP) / (jnp.sqrt(second_new / (1.0 - BETA_TWO ** STEP)) + ADAM_EPS)
    return (weight - rate * (direction + decay * weight), first_new, second_new)

def reference(tokens, cotangent, lengths, qkv_master, out_master, up_master, down_master, norm_master, qkv_first, out_first, up_first, down_first, norm_first, qkv_second, out_second, up_second, down_second, norm_second):
    params = (qkv_master, out_master, up_master, down_master, norm_master)
    segments = segment_ids(lengths)
    rows_in = tokens.astype(jnp.float32).reshape(ROWS, ROW_LEN, D)
    rows_back = cotangent.astype(jnp.float32).reshape(ROWS, ROW_LEN, D)

    def one_row(totals, item):
        row_in, row_back, segment = item
        output, pull = jax.vjp(lambda weights, value: forward(weights, value, segment), params, row_in)
        grads, row_grad = pull(row_back)
        totals = jax.tree.map(jnp.add, totals, grads)
        return (totals, (output.astype(jnp.bfloat16), row_grad.astype(jnp.bfloat16)))
    zeros = tuple((jnp.zeros_like(weight) for weight in params))
    grads, (mixed, input_grad) = lax.scan(one_row, zeros, (rows_in, rows_back, segments))
    square = jnp.float32(0.0)
    for grad in grads:
        square = square + jnp.sum(grad * grad)
    grad_norm = jnp.sqrt(square)
    factor = jnp.minimum(1.0, CLIP_NORM / grad_norm)
    qkv_new, qkv_first_new, qkv_second_new = adam(qkv_master, qkv_first, qkv_second, grads[0], factor, 0.1, DECAY)
    out_new, out_first_new, out_second_new = adam(out_master, out_first, out_second, grads[1], factor, 0.5, DECAY)
    up_new, up_first_new, up_second_new = adam(up_master, up_first, up_second, grads[2], factor, 0.1, DECAY)
    down_new, down_first_new, down_second_new = adam(down_master, down_first, down_second, grads[3], factor, 0.1, DECAY)
    norm_new, norm_first_new, norm_second_new = adam(norm_master, norm_first, norm_second, grads[4], factor, 0.5, 0.0)
    return (mixed.reshape(TOKENS, D), input_grad.reshape(TOKENS, D), grad_norm, qkv_new, qkv_first_new, qkv_second_new, out_new, out_first_new, out_second_new, up_new, up_first_new, up_second_new, down_new, down_first_new, down_second_new, norm_new, norm_first_new, norm_second_new, grads[0], grads[1], grads[2], grads[3], grads[4], qkv_new.astype(jnp.bfloat16), out_new.astype(jnp.bfloat16), up_new.astype(jnp.bfloat16), down_new.astype(jnp.bfloat16), norm_new.astype(jnp.bfloat16))
```

```python
import functools
import math

import jax
import jax.numpy as jnp
from jax import lax
from jax.experimental import pallas as pl
from jax.experimental.pallas import tpu as pltpu
from jax.sharding import PartitionSpec as P

MAX_LEN = 1024
STEP = 5
NORM_EPS = 1e-05
CLIP_NORM = 0.25
BETA_ONE = 0.5
BETA_TWO = 0.5
ADAM_EPS = 1e-08
DECAY = 0.1
HEADS = 4
HD = 32
D = 128
FF = 512
B = 256
CAP = 50
BIG = 2.0**100
LIMIT = 88.0
MASKED = -1e30
LN2 = math.log(2.0)
QSCALE = HD**-0.5 / LN2
f32 = jnp.float32
bf16 = jnp.bfloat16
MESH = pl.DeviceIdType.MESH


def mm(a, b):
    return lax.dot_general(a, b, (((1,), (0,)), ((), ())), preferred_element_type=f32)


def mm_nt(a, b):
    return lax.dot_general(a, b, (((1,), (1,)), ((), ())), preferred_element_type=f32)


def stats(value):
    mean = jnp.mean(value, axis=0, keepdims=True)
    centred = value - mean
    spread = jnp.mean(centred * centred, axis=0, keepdims=True)
    rate = lax.rsqrt(spread + NORM_EPS)
    return centred * rate, rate


def norm_back(grad, normed, rate, gain):
    scaled = grad * gain
    inner = jnp.mean(scaled, axis=0, keepdims=True)
    along = jnp.mean(scaled * normed, axis=0, keepdims=True)
    return rate * (scaled - inner - normed * along)


def split3(value):
    one = value.astype(bf16).astype(f32)
    two = (value - one).astype(bf16).astype(f32)
    return one, two, value - one - two


def lane_fold(value):
    out = value[:, :128]
    for j in range(1, value.shape[1] // 128):
        out = out + value[:, j * 128 : (j + 1) * 128]
    return out


def layer_kernel(
    rd,
    ro,
    lengths,
    w_ref,
    tokens,
    cot,
    mixed,
    igrad,
    grads,
    uq,
    uk,
    us,
    bounds,
    wqkv_t,
    wqkv,
    wout,
    wout_t,
    wup,
    wup_t,
    wdown,
    wdown_t,
    gains,
    stage,
    qf,
    kf,
    vf,
    kt,
    vt,
    dof,
    probs,
    ds,
    acc,
    dk_acc,
    dv_acc,
    resid_grad,
    first,
    causal,
    qn,
    kn,
    g_qkv,
    g_out,
    g_up,
    g_down,
    g_norm,
    g_stage,
):
    n_head, n_dp = w_ref.shape[:2]
    tiles = tokens.shape[0] // B
    row = lax.rem(lax.axis_index("head"), n_head)

    for h in range(n_head):
        qkv_h = jnp.concatenate([w_ref[h, d].astype(f32) for d in range(n_dp)], axis=0)
        stage[...] = qkv_h
        rp = w_ref.shape[2]
        pick = lambda lo, n: jnp.concatenate(
            [stage[d * rp + lo : d * rp + lo + n] for d in range(n_dp)], axis=0
        )
        q = pick(0, rd)
        wqkv_t[h] = q.T[: 3 * HD].astype(bf16)
        wqkv[:, h * 128 : (h + 1) * 128] = q.astype(bf16)
        u = pick(rd, rd)
        wup[:, h * 128 : (h + 1) * 128] = u.astype(bf16)
        wup_t[h * 128 : (h + 1) * 128] = u.T.astype(bf16)
        u = pick(2 * rd, rd)
        wdown[:, h * 128 : (h + 1) * 128] = u.astype(bf16)
        wdown_t[h * 128 : (h + 1) * 128] = u.T.astype(bf16)
        for d in range(n_dp):
            at = (d * n_head + h) * ro
            g_out[at : at + ro] = stage[d * rp + 3 * rd : d * rp + 3 * rd + ro]
            gains[at : at + ro] = stage[d * rp + 3 * rd + ro : d * rp + 3 * rd + 2 * ro]
    wo = g_out[...]
    wout[...] = wo.astype(bf16)
    wout_t[...] = wo.T.astype(bf16)
    gain1, shift1 = gains[:, 0:1], gains[:, 1:2]
    gain2, shift2 = gains[:, 2:3], gains[:, 3:4]

    starts, ends = [], []
    at = jnp.int32(0)
    for s in range(lengths.shape[1]):
        starts.append(at)
        at = at + lengths[row, s]
        ends.append(at)
    place = lax.broadcasted_iota(jnp.int32, (8, B), 0)
    start_v = jnp.zeros((8, B), jnp.int32)
    end_v = jnp.zeros((8, B), jnp.int32)
    for s in range(8):
        start_v = jnp.where(place == s, starts[s], start_v)
        end_v = jnp.where(place == s, ends[s], end_v)
    uq[0] = 0
    uk[0] = 0
    us[0] = 0

    def list_q(i, n):
        low = jnp.int32(0)
        for s in range(1, 8):
            low = jnp.where(starts[s] <= i * B, starts[s], low)

        def list_k(j, n):
            uq[n] = i
            uk[n] = j
            us[n] = jnp.minimum(n, CAP + 1)
            return n + 1

        return lax.fori_loop(lax.div(low, B), i + 1, list_k, n)

    units = lax.fori_loop(0, tiles, list_q, jnp.int32(1))
    uq[units] = 0
    uk[units] = 0
    us[units] = 0

    key_i = lax.broadcasted_iota(jnp.int32, (B, B), 0)
    query_i = lax.broadcasted_iota(jnp.int32, (B, B), 1)
    allowed = key_i <= query_i
    causal[0] = jnp.full((B, B), jnp.inf, bf16)
    causal[1] = jnp.where(allowed, jnp.inf, 0.0).astype(bf16)
    probs[0] = jnp.zeros_like(probs[0])
    ds[...] = jnp.zeros_like(ds)
    qn[...] = jnp.zeros_like(qn)
    kn[...] = jnp.zeros_like(kn)
    for ref in (acc, dk_acc, dv_acc, g_qkv, g_out, g_up, g_down, g_norm):
        ref[...] = jnp.zeros_like(ref)

    def project(i, carry):
        x = tokens[pl.ds(pl.multiple_of(i * B, B), B), :].astype(f32).T
        n1, _ = stats(x)
        f = (n1 * gain1 + shift1).astype(bf16)
        first[i] = f
        where_t = i * B + lax.broadcasted_iota(jnp.int32, (8, B), 1)
        inside = ((where_t >= start_v) & (where_t < end_v)).astype(f32)
        penalty = (1.0 - inside) * -BIG
        zeros8 = jnp.zeros((8, B), f32)
        ones8 = jnp.ones((8, B), f32)
        zeros16 = jnp.zeros((16, B), f32)
        for h in range(HEADS):
            packed = mm(wqkv_t[h], f).astype(bf16)
            pf = packed.astype(f32)
            q = (pf[:HD] * QSCALE).astype(bf16).astype(f32)
            k = pf[HD : 2 * HD]
            v = pf[2 * HD :]
            qn[h] = jnp.maximum(qn[h], jnp.sum(q * q, axis=0, keepdims=True))
            kn[h] = jnp.maximum(kn[h], jnp.sum(k * k, axis=0, keepdims=True))
            qf[h, i] = jnp.concatenate([q, penalty, zeros8, zeros16], axis=0).astype(bf16)
            kf[h, i] = packed[HD : 2 * HD]
            vf[h, i] = jnp.concatenate([v, ones8, zeros8], axis=0).astype(bf16)
            kt[h, i] = jnp.concatenate([k, inside, ones8, zeros16], axis=0).T.astype(bf16)
            vt[h, i] = jnp.concatenate([v, ones8, zeros8, zeros16], axis=0).T.astype(bf16)
        return carry

    lax.fori_loop(0, tiles, project, 0)

    bound = jnp.float32(0.0)
    for h in range(HEADS):
        bound = jnp.maximum(bound, jnp.max(qn[h]) * jnp.max(kn[h]))

    def scores(h, i, j):
        return mm(kt[h, j], qf[h, i])

    @pl.when(jnp.logical_not(bound <= LIMIT * LIMIT))
    def _():
        bounds[...] = jnp.full_like(bounds, MASKED)

        def top(t, carry):
            i, j = uq[t], uk[t]
            masked = jnp.where(allowed | (i != j), 0.0, MASKED)
            for h in range(HEADS):
                s = scores(h, i, j) + masked
                bounds[h, i] = jnp.maximum(bounds[h, i], jnp.max(s, axis=0, keepdims=True))
            return carry

        lax.fori_loop(1, units, top, 0)

        def shift(i, carry):
            for h in range(HEADS):
                one, two, three = split3(-bounds[h, i])
                r = lax.broadcasted_iota(jnp.int32, (16, B), 0)
                old = qf[h, i, HD : HD + 16].astype(f32)
                new = jnp.where(r == 8, one, jnp.where(r == 9, two, jnp.where(r == 10, three, old)))
                qf[h, i, HD : HD + 16] = new.astype(bf16)
            return carry

        lax.fori_loop(0, tiles, shift, 0)

    def weigh(t, slot):
        i, j = uq[t], uk[t]
        cut = causal[jnp.where(i == j, 1, 0)]
        for h in range(HEADS):
            probs[slot, h] = jnp.minimum(jnp.exp2(scores(h, i, j)).astype(bf16), cut)

    def forward(t, carry):
        i, j, slot = uq[t - 1], uk[t - 1], jnp.minimum(t - 1, CAP + 1)
        for h in range(HEADS):
            acc[h, i] += mm(vf[h, j, : HD + 8], probs[slot, h])
        weigh(t, jnp.minimum(t, CAP + 1))
        return carry

    lax.fori_loop(1, units + 1, forward, 0)

    def feed(i, carry):
        at = pl.ds(pl.multiple_of(i * B, B), B)
        outs, inv = [], []
        for h in range(HEADS):
            r = 1.0 / acc[h, i, HD : HD + 1]
            inv.append(r)
            outs.append(acc[h, i, :HD] * r)
        heads = jnp.concatenate(outs, axis=0).astype(bf16)
        x = tokens[at, :].astype(f32).T
        resid = x + mm(wout_t[...], heads)
        n2, rate2 = stats(resid)
        second = (n2 * gain2 + shift2).astype(bf16)
        c32 = cot[at, :].astype(f32).T
        c16 = c32.astype(bf16)
        pre = mm(wup_t[...], second)
        back = mm(wdown_t[...], c16)
        cdf = 0.5 * (1.0 + lax.erf(pre * (0.5**0.5)))
        pdf = jnp.exp(-0.5 * pre * pre) * (1.0 / math.sqrt(2.0 * math.pi))
        hidden = (pre * cdf).astype(bf16)
        pre_grad = (back * (cdf + pre * pdf)).astype(bf16)
        mixed[at, :] = (resid + mm(wdown[...], hidden)).T.astype(bf16)
        g_down[...] += mm_nt(c16, hidden)
        g_up[...] += mm_nt(second, pre_grad)
        second_in = mm(wup[...], pre_grad)
        g_norm[2] += lane_fold(second_in * n2)
        g_norm[3] += lane_fold(second_in)
        rg = c32 + norm_back(second_in, n2, rate2, gain2)
        resid_grad[i] = rg
        low = rg.astype(bf16)
        g_out[...] += mm_nt(heads, low)
        hg = mm(wout[...], low).astype(bf16).astype(f32)
        zeros16 = jnp.zeros((16, B), f32)
        r8 = lax.broadcasted_iota(jnp.int32, (16, B), 0)
        for h in range(HEADS):
            do = (hg[h * HD : (h + 1) * HD] * inv[h]).astype(bf16).astype(f32)
            delta = jnp.sum(do * outs[h], axis=0, keepdims=True)
            one, two, three = split3(-delta)
            extra = jnp.where(r8 == 0, one, jnp.where(r8 == 1, two, jnp.where(r8 == 2, three, 0.0)))
            dof[h, i] = jnp.concatenate([do, extra, zeros16], axis=0).astype(bf16)
        return carry

    lax.fori_loop(0, tiles, feed, 0)
    acc[...] = jnp.zeros_like(acc)

    def backward(t, carry):
        i, j = uq[t - 1], uk[t - 1]
        old = lax.rem(t - 1, 2)
        for h in range(HEADS):
            sg = ds[old, h]
            acc[h, i, :HD] += mm(kf[h, j], sg)
            dk_acc[h, j] += mm_nt(qf[h, i, :HD], sg)
        i, j, slot = uq[t], uk[t], us[t]
        pl.when(slot > CAP)(lambda: weigh(t, slot))
        new = lax.rem(t, 2)
        for h in range(HEADS):
            p = probs[slot, h]
            pg = mm(vt[h, j], dof[h, i])
            ds[new, h] = (p.astype(f32) * pg).astype(bf16)
            dv_acc[h, j] += mm_nt(dof[h, i, :HD], p)
        return carry

    lax.fori_loop(1, units + 1, backward, 0)

    def finish(i, carry):
        at = pl.ds(pl.multiple_of(i * B, B), B)
        rows = []
        for h in range(HEADS):
            rows += [acc[h, i, :HD] * HD**-0.5, dk_acc[h, i] * LN2, dv_acc[h, i], jnp.zeros((HD, B), f32)]
        packed_grad = jnp.concatenate(rows, axis=0).astype(bf16)
        g_qkv[...] += mm_nt(first[i], packed_grad)
        first_in = mm(wqkv[...], packed_grad)
        x = tokens[at, :].astype(f32).T
        n1, rate1 = stats(x)
        g_norm[0] += lane_fold(first_in * n1)
        g_norm[1] += lane_fold(first_in)
        out = resid_grad[i] + norm_back(first_in, n1, rate1, gain1)
        igrad[at, :] = out.T.astype(bf16)
        return carry

    lax.fori_loop(0, tiles, finish, 0)

    lane = lax.broadcasted_iota(jnp.int32, (D, 128), 1)
    norm = jnp.zeros((D, 128), f32)
    for c in range(4):
        norm = jnp.where(lane == c, jnp.sum(g_norm[c], axis=1, keepdims=True), norm)
    gains[...] = norm
    g_stage[...] = jnp.zeros_like(g_stage)
    for h in range(n_head):
        cols = slice(h * 128, (h + 1) * 128)
        for d in range(n_dp):
            rows = slice(d * rd, (d + 1) * rd)
            at = (d * n_head + h) * ro
            g_stage[0:rd] = g_qkv[rows, cols]
            g_stage[rd : 2 * rd] = g_up[rows, cols]
            g_stage[2 * rd : 3 * rd] = g_down[rows, cols]
            g_stage[3 * rd : 3 * rd + ro] = g_out[at : at + ro]
            g_stage[3 * rd + ro : 3 * rd + 2 * ro] = gains[at : at + ro]
            grads[h, d] = g_stage[...].astype(bf16)


def layer(lengths, weights, tokens, cot, rd, ro):
    n_head, n_dp, rp = weights.shape[:3]
    tiles = tokens.shape[0] // B
    listed = tiles * (MAX_LEN // B + 1) + 2
    vmem = lambda shape, dtype: pltpu.VMEM(shape, dtype)
    scratch = [
        pltpu.SMEM((listed,), jnp.int32),
        pltpu.SMEM((listed,), jnp.int32),
        pltpu.SMEM((listed,), jnp.int32),
        vmem((HEADS, tiles, 1, B), f32),
        vmem((HEADS, 3 * HD, D), bf16),
        vmem((D, HEADS * 128), bf16),
        vmem((D, D), bf16),
        vmem((D, D), bf16),
        vmem((D, FF), bf16),
        vmem((FF, D), bf16),
        vmem((D, FF), bf16),
        vmem((FF, D), bf16),
        vmem((D, 128), f32),
        vmem((n_dp * rp, 128), f32),
        vmem((HEADS, tiles, 64, B), bf16),
        vmem((HEADS, tiles, HD, B), bf16),
        vmem((HEADS, tiles, 48, B), bf16),
        vmem((HEADS, tiles, B, 64), bf16),
        vmem((HEADS, tiles, B, 64), bf16),
        vmem((HEADS, tiles, 64, B), bf16),
        vmem((CAP + 2, HEADS, B, B), bf16),
        vmem((2, HEADS, B, B), bf16),
        vmem((HEADS, tiles, HD + 8, B), f32),
        vmem((HEADS, tiles, HD, B), f32),
        vmem((HEADS, tiles, HD, B), f32),
        vmem((tiles, D, B), f32),
        vmem((tiles, D, B), bf16),
        vmem((2, B, B), bf16),
        vmem((HEADS, 1, B), f32),
        vmem((HEADS, 1, B), f32),
        vmem((D, HEADS * 128), f32),
        vmem((D, D), f32),
        vmem((D, FF), f32),
        vmem((D, FF), f32),
        vmem((4, D, 128), f32),
        vmem((rp, 128), f32),
    ]
    whole = pl.BlockSpec(memory_space=pltpu.VMEM)
    return pl.pallas_call(
        functools.partial(layer_kernel, rd, ro),
        out_shape=(
            jax.ShapeDtypeStruct(tokens.shape, bf16),
            jax.ShapeDtypeStruct(tokens.shape, bf16),
            jax.ShapeDtypeStruct((n_head, n_dp, rp, 128), bf16),
        ),
        in_specs=[pl.BlockSpec(memory_space=pltpu.SMEM), whole, whole, whole],
        out_specs=(whole, whole, whole),
        scratch_shapes=scratch,
        compiler_params=pltpu.CompilerParams(vmem_limit_bytes=62 * 1024 * 1024),
    )(lengths, weights, tokens, cot)


def factors(n_dp, n_head):
    dp, left = [], n_dp
    while left > 1:
        size = 4 if left % 4 == 0 else left
        dp.append(size)
        left //= size
    head = [2, 2] if n_head == 4 and n_dp == 8 else [n_head]
    out = []
    for axis, sizes in (("head", head), ("dp", dp)):
        stride = math.prod(sizes)
        for size in sizes:
            stride //= size
            out.append((axis, stride, size))
    return out


def digit(axis, stride, size):
    return lax.rem(lax.div(lax.axis_index(axis), stride), size)


def peer(axis, stride, size, offset):
    mine = digit(axis, stride, size)
    theirs = lax.rem(mine + offset, size)
    return {axis: lax.axis_index(axis) + (theirs - mine) * stride}, theirs


def greet(peers):
    barrier = pltpu.get_barrier_semaphore()
    for device in peers:
        pl.semaphore_signal(barrier, inc=1, device_id=device, device_id_type=MESH)
    pl.semaphore_wait(barrier, len(peers))


def gather_kernel(axes, qkv, out, up, down, norm, w_ref, stage, send, recv):
    rd, ro = qkv.shape[0], out.shape[0]
    greet([peer(*axis, o)[0] for axis in axes for o in range(1, axis[2])])
    stage[...] = jnp.zeros_like(stage)
    stage[0:rd, : qkv.shape[1]] = qkv[...]
    stage[rd : 2 * rd, : up.shape[1]] = up[...]
    stage[2 * rd : 3 * rd, : down.shape[1]] = down[...]
    stage[3 * rd : 3 * rd + ro] = out[...]
    stage[3 * rd + ro : 3 * rd + 2 * ro, : norm.shape[1]] = norm[...]
    mine = [digit(*axis) for axis in axes]
    w_ref[tuple(mine)] = stage[...].astype(bf16)
    have = list(mine)
    n = 0
    for a in reversed(range(len(axes))):
        copies = []
        for o in range(1, axes[a][2]):
            device, _ = peer(*axes[a], o)
            block = w_ref.at[tuple(have)]
            _, source = peer(*axes[a], axes[a][2] - o)
            there = list(have)
            there[a] = source
            copies.append(
                (
                    pltpu.make_async_remote_copy(
                        src_ref=block,
                        dst_ref=block,
                        send_sem=send.at[n],
                        recv_sem=recv.at[n],
                        device_id=device,
                        device_id_type=MESH,
                    ),
                    pltpu.make_async_remote_copy(
                        src_ref=w_ref.at[tuple(there)],
                        dst_ref=w_ref.at[tuple(there)],
                        send_sem=send.at[n],
                        recv_sem=recv.at[n],
                        device_id=device,
                        device_id_type=MESH,
                    ),
                )
            )
            n += 1
        for out_copy, _ in copies:
            out_copy.start()
        for out_copy, in_copy in copies:
            in_copy.wait_recv()
            out_copy.wait_send()
        have[a] = slice(None)


def gather(axes, rows, masters):
    copies = sum(size - 1 for _, _, size in axes)
    whole = pl.BlockSpec(memory_space=pltpu.VMEM)
    shape = tuple(size for _, _, size in axes) + (rows, 128)
    return pl.pallas_call(
        functools.partial(gather_kernel, axes),
        out_shape=jax.ShapeDtypeStruct(shape, bf16),
        in_specs=[whole] * 5,
        out_specs=whole,
        scratch_shapes=[
            pltpu.VMEM((rows, 128), f32),
            pltpu.SemaphoreType.DMA((copies,)),
            pltpu.SemaphoreType.DMA((copies,)),
        ],
        compiler_params=pltpu.CompilerParams(
            collective_id=0, has_side_effects=True, vmem_limit_bytes=32 * 1024 * 1024
        ),
    )(*masters)


def scatter_kernel(axes, groups, g_ref, red_ref, sq_ref, *scratch):
    stages = len(axes)
    arrived = scratch[:stages]
    partial = scratch[stages : 2 * stages - 1]
    squares, (send, recv) = scratch[2 * stages - 1 : -2], scratch[-2:]
    greet([peer(*group, o)[0] for group in groups for o in range(1, group[2])])
    current = g_ref
    n = 0
    for s, a in enumerate(reversed(range(len(axes)))):
        order = current.shape[:-2]
        lead = (slice(None),) * (len(order) - 1)
        copies = []
        for o in range(1, axes[a][2]):
            device, theirs = peer(*axes[a], o)
            copies.append(
                pltpu.make_async_remote_copy(
                    src_ref=current.at[lead + (theirs,)],
                    dst_ref=arrived[s].at[o - 1],
                    send_sem=send.at[n],
                    recv_sem=recv.at[n],
                    device_id=device,
                    device_id_type=MESH,
                )
            )
            n += 1
        for copy in copies:
            copy.start()
        total = current[lead + (digit(*axes[a]),)].astype(f32)
        for o, copy in enumerate(copies):
            copy.wait_recv()
            total = total + arrived[s][o].astype(f32)
        for copy in copies:
            copy.wait_send()
        if s < stages - 1:
            partial[s][...] = total.astype(bf16)
            current = partial[s]
    red_ref[...] = total
    square = total * total
    fold = square[0:8]
    for r in range(8, square.shape[0], 8):
        fold = fold + square[r : r + 8]
    for group, ref in zip(groups, squares):
        mine = digit(*group)
        ref[mine] = fold
        copies = []
        for o in range(1, group[2]):
            device, _ = peer(*group, o)
            _, source = peer(*group, group[2] - o)
            make = lambda at, device=device, n=n: pltpu.make_async_remote_copy(
                src_ref=ref.at[at],
                dst_ref=ref.at[at],
                send_sem=send.at[n],
                recv_sem=recv.at[n],
                device_id=device,
                device_id_type=MESH,
            )
            copies.append((make(mine), make(source)))
            n += 1
        for out_copy, _ in copies:
            out_copy.start()
        for out_copy, in_copy in copies:
            in_copy.wait_recv()
            out_copy.wait_send()
        fold = ref[0]
        for j in range(1, group[2]):
            fold = fold + ref[j]
    sq_ref[...] = fold


def scatter(axes, groups, grads):
    sizes = [size for _, _, size in axes]
    block = grads.shape[-2:]
    arrived, partial = [], []
    for a in reversed(range(len(axes))):
        arrived.append(pltpu.VMEM((sizes[a] - 1,) + tuple(sizes[:a]) + block, bf16))
        if a:
            partial.append(pltpu.VMEM(tuple(sizes[:a]) + block, bf16))
    squares = [pltpu.VMEM((size, 8, 128), f32) for _, _, size in groups]
    copies = sum(size - 1 for size in sizes) + sum(size - 1 for _, _, size in groups)
    whole = pl.BlockSpec(memory_space=pltpu.VMEM)
    return pl.pallas_call(
        functools.partial(scatter_kernel, axes, groups),
        out_shape=(jax.ShapeDtypeStruct(block, f32), jax.ShapeDtypeStruct((8, 128), f32)),
        in_specs=[whole],
        out_specs=(whole, whole),
        scratch_shapes=arrived
        + partial
        + squares
        + [pltpu.SemaphoreType.DMA((copies,)), pltpu.SemaphoreType.DMA((copies,))],
        compiler_params=pltpu.CompilerParams(
            collective_id=1, has_side_effects=True, vmem_limit_bytes=32 * 1024 * 1024
        ),
    )(grads)


def adam(weight, first, second, grad, factor, rate, decay):
    clipped = grad * factor
    first_new = BETA_ONE * first + (1.0 - BETA_ONE) * clipped
    second_new = BETA_TWO * second + (1.0 - BETA_TWO) * clipped * clipped
    direction = (
        first_new
        / (1.0 - BETA_ONE**STEP)
        / (jnp.sqrt(second_new / (1.0 - BETA_TWO**STEP)) + ADAM_EPS)
    )
    return weight - rate * (direction + decay * weight), first_new, second_new


def update_kernel(red, sq, *refs):
    params, outs = refs[:15], refs[15:]
    rd, ro = params[0].shape[0], params[1].shape[0]
    norm = jnp.sqrt(jnp.sum(sq[...], keepdims=True))
    outs[0][...] = norm
    factor = jnp.minimum(1.0, CLIP_NORM / norm)
    rows = (0, 3 * rd, rd, 2 * rd, 3 * rd + ro)
    rates = (0.1, 0.5, 0.1, 0.1, 0.5)
    decays = (DECAY, DECAY, DECAY, DECAY, 0.0)
    for w in range(5):
        height, width = params[w].shape
        grad = red[rows[w] : rows[w] + height, :width]
        new, first_new, second_new = adam(
            params[w][...], params[5 + w][...], params[10 + w][...], grad, factor, rates[w], decays[w]
        )
        outs[1 + 3 * w][...] = new
        outs[2 + 3 * w][...] = first_new
        outs[3 + 3 * w][...] = second_new
        outs[16 + w][...] = grad
        outs[21 + w][...] = new.astype(bf16)


def update(red, sq, params):
    whole = pl.BlockSpec(memory_space=pltpu.VMEM)
    like = lambda p, dtype: jax.ShapeDtypeStruct(p.shape, dtype)
    shapes = [jax.ShapeDtypeStruct((1, 1), f32)]
    shapes += [like(p, f32) for p in params[:5] for _ in range(3)]
    shapes += [like(p, f32) for p in params[:5]]
    shapes += [like(p, bf16) for p in params[:5]]
    return pl.pallas_call(
        update_kernel,
        out_shape=shapes,
        in_specs=[whole] * 17,
        out_specs=[whole] * len(shapes),
        compiler_params=pltpu.CompilerParams(vmem_limit_bytes=32 * 1024 * 1024),
    )(red, sq, *params)


def per_device(n_dp, n_head, tokens, cotangent, lengths, *params):
    masters = params[:5]
    rd, ro = masters[0].shape[0], masters[1].shape[0]
    rows = -(-(3 * rd + 2 * ro) // 16) * 16
    axes = factors(n_dp, n_head)
    groups = [("dp", 1, n_dp), ("head", 1, n_head)]
    weights = gather(axes, rows, masters).reshape(n_head, n_dp, rows, 128)
    mixed, input_grad, grads = layer(lengths, weights, tokens, cotangent, rd, ro)
    grads = grads.reshape(tuple(size for _, _, size in axes) + (rows, 128))
    red, sq = scatter(axes, groups, grads)
    outs = update(red, sq, params)
    return (mixed, input_grad, outs[0].reshape(()), *outs[1:])


def solution(mesh):
    both, split, lens = P(("dp", "head"), None), P("dp", "head"), P("dp", None)
    weight = (split, both, split, split, both)
    return jax.shard_map(
        functools.partial(per_device, mesh.shape["dp"], mesh.shape["head"]),
        mesh=mesh,
        in_specs=(both, both, lens) + weight * 3,
        out_specs=(both, both, P())
        + tuple(spec for spec in weight for _ in range(3))
        + weight
        + weight,
        check_vma=False,
    )
```

```python
import functools
import itertools
import math

import jax
import jax.numpy as jnp
from jax import lax
from jax.experimental import pallas as pl
from jax.experimental.pallas import tpu as pltpu
from jax.sharding import PartitionSpec as P

MAX_LEN = 1024
STEP = 5
NORM_EPS = 1e-05
CLIP_NORM = 0.25
BETA_ONE = 0.5
BETA_TWO = 0.5
ADAM_EPS = 1e-08
DECAY = 0.1
HEADS = 4
HD = 32
D = 128
FF = 512
B = 256
CAP = 50
BIG = 2.0**100
LIMIT = 88.0
MASKED = -1e30
LN2 = math.log(2.0)
QSCALE = HD**-0.5 / LN2
f32 = jnp.float32
bf16 = jnp.bfloat16
MESH = pl.DeviceIdType.MESH


def mm(a, b):
    return lax.dot_general(a, b, (((1,), (0,)), ((), ())), preferred_element_type=f32)


def mm_nt(a, b):
    return lax.dot_general(a, b, (((1,), (1,)), ((), ())), preferred_element_type=f32)


def stats(value):
    mean = jnp.mean(value, axis=0, keepdims=True)
    centred = value - mean
    spread = jnp.mean(centred * centred, axis=0, keepdims=True)
    rate = lax.rsqrt(spread + NORM_EPS)
    return centred * rate, rate


def norm_back(grad, normed, rate, gain):
    scaled = grad * gain
    inner = jnp.mean(scaled, axis=0, keepdims=True)
    along = jnp.mean(scaled * normed, axis=0, keepdims=True)
    return rate * (scaled - inner - normed * along)


def split3(value):
    one = value.astype(bf16).astype(f32)
    two = (value - one).astype(bf16).astype(f32)
    return one, two, value - one - two


def lane_fold(value):
    out = value[:, :128]
    for j in range(1, value.shape[1] // 128):
        out = out + value[:, j * 128 : (j + 1) * 128]
    return out


def layer_kernel(
    rd,
    ro,
    lengths,
    w_ref,
    tokens,
    cot,
    mixed,
    igrad,
    grads,
    uq,
    uk,
    us,
    bounds,
    wqkv_t,
    wqkv,
    wout,
    wout_t,
    wup,
    wup_t,
    wdown,
    wdown_t,
    gains,
    stage,
    qf,
    kf,
    vf,
    kt,
    vt,
    dof,
    probs,
    ds,
    acc,
    dk_acc,
    dv_acc,
    resid_grad,
    first,
    causal,
    qn,
    kn,
    g_qkv,
    g_out,
    g_up,
    g_down,
    g_norm,
    g_stage,
):
    n_head, n_dp = w_ref.shape[:2]
    tiles = tokens.shape[0] // B
    row = lax.rem(lax.axis_index("head"), n_head)

    for h in range(n_head):
        qkv_h = jnp.concatenate([w_ref[h, d].astype(f32) for d in range(n_dp)], axis=0)
        stage[...] = qkv_h
        rp = w_ref.shape[2]
        pick = lambda lo, n: jnp.concatenate(
            [stage[d * rp + lo : d * rp + lo + n] for d in range(n_dp)], axis=0
        )
        q = pick(0, rd)
        wqkv_t[h] = q.T[: 3 * HD].astype(bf16)
        wqkv[:, h * 128 : (h + 1) * 128] = q.astype(bf16)
        u = pick(rd, rd)
        wup[:, h * 128 : (h + 1) * 128] = u.astype(bf16)
        wup_t[h * 128 : (h + 1) * 128] = u.T.astype(bf16)
        u = pick(2 * rd, rd)
        wdown[:, h * 128 : (h + 1) * 128] = u.astype(bf16)
        wdown_t[h * 128 : (h + 1) * 128] = u.T.astype(bf16)
        for d in range(n_dp):
            at = (d * n_head + h) * ro
            g_out[at : at + ro] = stage[d * rp + 3 * rd : d * rp + 3 * rd + ro]
            gains[at : at + ro] = stage[d * rp + 3 * rd + ro : d * rp + 3 * rd + 2 * ro]
    wo = g_out[...]
    wout[...] = wo.astype(bf16)
    wout_t[...] = wo.T.astype(bf16)
    gain1, shift1 = gains[:, 0:1], gains[:, 1:2]
    gain2, shift2 = gains[:, 2:3], gains[:, 3:4]

    starts, ends = [], []
    at = jnp.int32(0)
    for s in range(lengths.shape[1]):
        starts.append(at)
        at = at + lengths[row, s]
        ends.append(at)
    place = lax.broadcasted_iota(jnp.int32, (8, B), 0)
    start_v = jnp.zeros((8, B), jnp.int32)
    end_v = jnp.zeros((8, B), jnp.int32)
    for s in range(8):
        start_v = jnp.where(place == s, starts[s], start_v)
        end_v = jnp.where(place == s, ends[s], end_v)
    uq[0] = 0
    uk[0] = 0
    us[0] = 0

    def list_q(i, n):
        low = jnp.int32(0)
        for s in range(1, 8):
            low = jnp.where(starts[s] <= i * B, starts[s], low)

        def list_k(j, n):
            uq[n] = i
            uk[n] = j
            us[n] = jnp.minimum(n, CAP + 1)
            return n + 1

        return lax.fori_loop(lax.div(low, B), i + 1, list_k, n)

    units = lax.fori_loop(0, tiles, list_q, jnp.int32(1))
    uq[units] = 0
    uk[units] = 0
    us[units] = 0

    key_i = lax.broadcasted_iota(jnp.int32, (B, B), 0)
    query_i = lax.broadcasted_iota(jnp.int32, (B, B), 1)
    allowed = key_i <= query_i
    causal[0] = jnp.full((B, B), jnp.inf, bf16)
    causal[1] = jnp.where(allowed, jnp.inf, 0.0).astype(bf16)
    probs[0] = jnp.zeros_like(probs[0])
    ds[...] = jnp.zeros_like(ds)
    qn[...] = jnp.zeros_like(qn)
    kn[...] = jnp.zeros_like(kn)
    for ref in (acc, dk_acc, dv_acc, g_qkv, g_out, g_up, g_down, g_norm):
        ref[...] = jnp.zeros_like(ref)

    def project(i, carry):
        x = tokens[pl.ds(pl.multiple_of(i * B, B), B), :].astype(f32).T
        n1, _ = stats(x)
        f = (n1 * gain1 + shift1).astype(bf16)
        first[i] = f
        where_t = i * B + lax.broadcasted_iota(jnp.int32, (8, B), 1)
        inside = ((where_t >= start_v) & (where_t < end_v)).astype(f32)
        penalty = (1.0 - inside) * -BIG
        zeros8 = jnp.zeros((8, B), f32)
        ones8 = jnp.ones((8, B), f32)
        zeros16 = jnp.zeros((16, B), f32)
        for h in range(HEADS):
            packed = mm(wqkv_t[h], f).astype(bf16)
            pf = packed.astype(f32)
            q = (pf[:HD] * QSCALE).astype(bf16).astype(f32)
            k = pf[HD : 2 * HD]
            v = pf[2 * HD :]
            qn[h] = jnp.maximum(qn[h], jnp.sum(q * q, axis=0, keepdims=True))
            kn[h] = jnp.maximum(kn[h], jnp.sum(k * k, axis=0, keepdims=True))
            qf[h, i] = jnp.concatenate([q, penalty, zeros8, zeros16], axis=0).astype(bf16)
            kf[h, i] = packed[HD : 2 * HD]
            vf[h, i] = jnp.concatenate([v, ones8, zeros8], axis=0).astype(bf16)
            kt[h, i] = jnp.concatenate([k, inside, ones8, zeros16], axis=0).T.astype(bf16)
            vt[h, i] = jnp.concatenate([v, ones8, zeros8, zeros16], axis=0).T.astype(bf16)
        return carry

    lax.fori_loop(0, tiles, project, 0)

    bound = jnp.float32(0.0)
    for h in range(HEADS):
        bound = jnp.maximum(bound, jnp.max(qn[h]) * jnp.max(kn[h]))

    def scores(h, i, j):
        return mm(kt[h, j], qf[h, i])

    @pl.when(jnp.logical_not(bound <= LIMIT * LIMIT))
    def _():
        bounds[...] = jnp.full_like(bounds, MASKED)

        def top(t, carry):
            i, j = uq[t], uk[t]
            masked = jnp.where(allowed | (i != j), 0.0, MASKED)
            for h in range(HEADS):
                s = scores(h, i, j) + masked
                bounds[h, i] = jnp.maximum(bounds[h, i], jnp.max(s, axis=0, keepdims=True))
            return carry

        lax.fori_loop(1, units, top, 0)

        def shift(i, carry):
            for h in range(HEADS):
                one, two, three = split3(-bounds[h, i])
                r = lax.broadcasted_iota(jnp.int32, (16, B), 0)
                old = qf[h, i, HD : HD + 16].astype(f32)
                new = jnp.where(r == 8, one, jnp.where(r == 9, two, jnp.where(r == 10, three, old)))
                qf[h, i, HD : HD + 16] = new.astype(bf16)
            return carry

        lax.fori_loop(0, tiles, shift, 0)

    def weigh(t, slot):
        i, j = uq[t], uk[t]
        cut = causal[jnp.where(i == j, 1, 0)]
        for h in range(HEADS):
            probs[slot, h] = jnp.minimum(jnp.exp2(scores(h, i, j)).astype(bf16), cut)

    def forward(t, carry):
        i, j, slot = uq[t - 1], uk[t - 1], jnp.minimum(t - 1, CAP + 1)
        for h in range(HEADS):
            acc[h, i] += mm(vf[h, j, : HD + 8], probs[slot, h])
        weigh(t, jnp.minimum(t, CAP + 1))
        return carry

    lax.fori_loop(1, units + 1, forward, 0)

    def feed(i, carry):
        at = pl.ds(pl.multiple_of(i * B, B), B)
        outs, inv = [], []
        for h in range(HEADS):
            r = 1.0 / acc[h, i, HD : HD + 1]
            inv.append(r)
            outs.append(acc[h, i, :HD] * r)
        heads = jnp.concatenate(outs, axis=0).astype(bf16)
        x = tokens[at, :].astype(f32).T
        resid = x + mm(wout_t[...], heads)
        n2, rate2 = stats(resid)
        second = (n2 * gain2 + shift2).astype(bf16)
        c32 = cot[at, :].astype(f32).T
        c16 = c32.astype(bf16)
        pre = mm(wup_t[...], second)
        back = mm(wdown_t[...], c16)
        cdf = 0.5 * (1.0 + lax.erf(pre * (0.5**0.5)))
        pdf = jnp.exp(-0.5 * pre * pre) * (1.0 / math.sqrt(2.0 * math.pi))
        hidden = (pre * cdf).astype(bf16)
        pre_grad = (back * (cdf + pre * pdf)).astype(bf16)
        mixed[at, :] = (resid + mm(wdown[...], hidden)).T.astype(bf16)
        g_down[...] += mm_nt(c16, hidden)
        g_up[...] += mm_nt(second, pre_grad)
        second_in = mm(wup[...], pre_grad)
        g_norm[2] += lane_fold(second_in * n2)
        g_norm[3] += lane_fold(second_in)
        rg = c32 + norm_back(second_in, n2, rate2, gain2)
        resid_grad[i] = rg
        low = rg.astype(bf16)
        g_out[...] += mm_nt(heads, low)
        hg = mm(wout[...], low).astype(bf16).astype(f32)
        zeros16 = jnp.zeros((16, B), f32)
        r8 = lax.broadcasted_iota(jnp.int32, (16, B), 0)
        for h in range(HEADS):
            do = (hg[h * HD : (h + 1) * HD] * inv[h]).astype(bf16).astype(f32)
            delta = jnp.sum(do * outs[h], axis=0, keepdims=True)
            one, two, three = split3(-delta)
            extra = jnp.where(r8 == 0, one, jnp.where(r8 == 1, two, jnp.where(r8 == 2, three, 0.0)))
            dof[h, i] = jnp.concatenate([do, extra, zeros16], axis=0).astype(bf16)
        return carry

    lax.fori_loop(0, tiles, feed, 0)
    acc[...] = jnp.zeros_like(acc)

    def backward(t, carry):
        pl.when(us[t] > CAP)(lambda: weigh(t, us[t]))
        i, j = uq[t - 1], uk[t - 1]
        old = lax.rem(t - 1, 2)
        for h in range(HEADS):
            sg = ds[old, h]
            acc[h, i, :HD] += mm(kf[h, j], sg)
            dk_acc[h, j] += mm_nt(qf[h, i, :HD], sg)
        i, j, slot = uq[t], uk[t], us[t]
        new = lax.rem(t, 2)
        for h in range(HEADS):
            p = probs[slot, h]
            pg = mm(vt[h, j], dof[h, i])
            ds[new, h] = (p.astype(f32) * pg).astype(bf16)
            dv_acc[h, j] += mm_nt(dof[h, i, :HD], p)
        return carry

    lax.fori_loop(1, units + 1, backward, 0)

    def finish(i, carry):
        at = pl.ds(pl.multiple_of(i * B, B), B)
        rows = []
        for h in range(HEADS):
            rows += [acc[h, i, :HD] * HD**-0.5, dk_acc[h, i] * LN2, dv_acc[h, i], jnp.zeros((HD, B), f32)]
        packed_grad = jnp.concatenate(rows, axis=0).astype(bf16)
        g_qkv[...] += mm_nt(first[i], packed_grad)
        first_in = mm(wqkv[...], packed_grad)
        x = tokens[at, :].astype(f32).T
        n1, rate1 = stats(x)
        g_norm[0] += lane_fold(first_in * n1)
        g_norm[1] += lane_fold(first_in)
        out = resid_grad[i] + norm_back(first_in, n1, rate1, gain1)
        igrad[at, :] = out.T.astype(bf16)
        return carry

    lax.fori_loop(0, tiles, finish, 0)

    lane = lax.broadcasted_iota(jnp.int32, (D, 128), 1)
    norm = jnp.zeros((D, 128), f32)
    for c in range(4):
        norm = jnp.where(lane == c, jnp.sum(g_norm[c], axis=1, keepdims=True), norm)
    gains[...] = norm
    g_stage[...] = jnp.zeros_like(g_stage)
    for h in range(n_head):
        cols = slice(h * 128, (h + 1) * 128)
        for d in range(n_dp):
            rows = slice(d * rd, (d + 1) * rd)
            at = (d * n_head + h) * ro
            g_stage[0:rd] = g_qkv[rows, cols]
            g_stage[rd : 2 * rd] = g_up[rows, cols]
            g_stage[2 * rd : 3 * rd] = g_down[rows, cols]
            g_stage[3 * rd : 3 * rd + ro] = g_out[at : at + ro]
            g_stage[3 * rd + ro : 3 * rd + 2 * ro] = gains[at : at + ro]
            grads[h, d] = g_stage[...].astype(bf16)


def layer(lengths, weights, tokens, cot, rd, ro):
    n_head, n_dp, rp = weights.shape[:3]
    tiles = tokens.shape[0] // B
    listed = tiles * (MAX_LEN // B + 1) + 2
    vmem = lambda shape, dtype: pltpu.VMEM(shape, dtype)
    scratch = [
        pltpu.SMEM((listed,), jnp.int32),
        pltpu.SMEM((listed,), jnp.int32),
        pltpu.SMEM((listed,), jnp.int32),
        vmem((HEADS, tiles, 1, B), f32),
        vmem((HEADS, 3 * HD, D), bf16),
        vmem((D, HEADS * 128), bf16),
        vmem((D, D), bf16),
        vmem((D, D), bf16),
        vmem((D, FF), bf16),
        vmem((FF, D), bf16),
        vmem((D, FF), bf16),
        vmem((FF, D), bf16),
        vmem((D, 128), f32),
        vmem((n_dp * rp, 128), f32),
        vmem((HEADS, tiles, 64, B), bf16),
        vmem((HEADS, tiles, HD, B), bf16),
        vmem((HEADS, tiles, 48, B), bf16),
        vmem((HEADS, tiles, B, 64), bf16),
        vmem((HEADS, tiles, B, 64), bf16),
        vmem((HEADS, tiles, 64, B), bf16),
        vmem((CAP + 2, HEADS, B, B), bf16),
        vmem((2, HEADS, B, B), bf16),
        vmem((HEADS, tiles, HD + 8, B), f32),
        vmem((HEADS, tiles, HD, B), f32),
        vmem((HEADS, tiles, HD, B), f32),
        vmem((tiles, D, B), f32),
        vmem((tiles, D, B), bf16),
        vmem((2, B, B), bf16),
        vmem((HEADS, 1, B), f32),
        vmem((HEADS, 1, B), f32),
        vmem((D, HEADS * 128), f32),
        vmem((D, D), f32),
        vmem((D, FF), f32),
        vmem((D, FF), f32),
        vmem((4, D, 128), f32),
        vmem((rp, 128), f32),
    ]
    whole = pl.BlockSpec(memory_space=pltpu.VMEM)
    return pl.pallas_call(
        functools.partial(layer_kernel, rd, ro),
        out_shape=(
            jax.ShapeDtypeStruct(tokens.shape, bf16),
            jax.ShapeDtypeStruct(tokens.shape, bf16),
            jax.ShapeDtypeStruct((n_head, n_dp, rp, 128), bf16),
        ),
        in_specs=[pl.BlockSpec(memory_space=pltpu.SMEM), whole, whole, whole],
        out_specs=(whole, whole, whole),
        scratch_shapes=scratch,
        compiler_params=pltpu.CompilerParams(vmem_limit_bytes=62 * 1024 * 1024),
    )(lengths, weights, tokens, cot)


def factors(n_dp, n_head):
    if (n_dp, n_head) == (8, 4):
        axes = (("head", 2, 2), ("head", 1, 2), ("dp", 2, 4), ("dp", 1, 2))
        return axes, ((2,), (0, 3), (1,)), ((1,), (0, 3), (2,)), ((1,), (0, 2, 3))
    axes, left = [("head", 1, n_head)], n_dp
    while left > 1:
        size = 4 if left % 4 == 0 else left
        left //= size
        axes.append(("dp", left, size))
    each = tuple((a,) for a in range(len(axes)))
    return tuple(axes), each[::-1], each, each


def digit(axis, stride, size):
    return lax.rem(lax.div(lax.axis_index(axis), stride), size)


def others(axes, group):
    found = []
    for offsets in itertools.product(*(range(axes[a][2]) for a in group)):
        if not any(offsets):
            continue
        place, theirs, source = {}, {}, {}
        for a, offset in zip(group, offsets):
            axis, stride, size = axes[a]
            mine = digit(*axes[a])
            theirs[a] = lax.rem(mine + offset, size)
            source[a] = lax.rem(mine + size - offset, size)
            place[axis] = place.get(axis, lax.axis_index(axis)) + (theirs[a] - mine) * stride
        found.append((place, theirs, source))
    return found


def greet(peers):
    barrier = pltpu.get_barrier_semaphore()
    for device in peers:
        pl.semaphore_signal(barrier, inc=1, device_id=device, device_id_type=MESH)
    return lambda: pl.semaphore_wait(barrier, len(peers))


def remote(src, dst, sems, n, device):
    return pltpu.make_async_remote_copy(
        src_ref=src,
        dst_ref=dst,
        send_sem=sems[0].at[n],
        recv_sem=sems[1].at[n],
        device_id=device,
        device_id_type=MESH,
    )


def peers_of(axes, groups):
    return [place for group in groups for place, _, _ in others(axes, group)]


def gather_kernel(axes, groups, *refs):
    masters, w_ref = refs[:5], refs[5]
    held, (stage, block, local, send, recv) = refs[6:11], refs[11:]
    arrived = greet(peers_of(axes, groups))
    loads = [pltpu.make_async_copy(m, h, local.at[n]) for n, (m, h) in enumerate(zip(masters, held))]
    for load in loads:
        load.start()
    stage[...] = jnp.zeros_like(stage)
    for load in loads:
        load.wait()
    qkv, out, up, down, norm = held
    rd, ro = qkv.shape[0], out.shape[0]
    at = 0
    for part, height in ((qkv, rd), (up, rd), (down, rd), (out, ro), (norm, ro)):
        stage[at : at + height, : part.shape[1]] = part[...]
        at += height
    block[...] = stage[...].astype(bf16)
    have = [digit(*axis) for axis in axes]
    keep = pltpu.make_async_copy(block, w_ref.at[tuple(have)], local.at[0])
    keep.start()
    arrived()
    sent, n = [], 0
    for group in groups:
        coming = []
        for place, _, source in others(axes, group):
            mine = w_ref.at[tuple(have)]
            copy = remote(block if n < len(others(axes, groups[0])) else mine, mine, (send, recv), n, place)
            copy.start()
            sent.append(copy)
            there = list(have)
            for a in group:
                there[a] = source[a]
            there = w_ref.at[tuple(there)]
            coming.append(remote(there, there, (send, recv), n, place))
            n += 1
        if group is groups[0]:
            keep.wait()
        for copy in coming:
            copy.wait_recv()
        for a in group:
            have[a] = slice(None)
    for copy in sent:
        copy.wait_send()


ANY = pl.BlockSpec(memory_space=pl.ANY)
WHOLE = pl.BlockSpec(memory_space=pltpu.VMEM)


def copies_of(axes, groups):
    return sum(math.prod(axes[a][2] for a in group) - 1 for group in groups)


def gather(axes, groups, rows, masters, cid=0, out=ANY):
    copies = copies_of(axes, groups)
    shape = tuple(size for _, _, size in axes) + (rows, 128)
    return pl.pallas_call(
        functools.partial(gather_kernel, axes, groups),
        out_shape=jax.ShapeDtypeStruct(shape, bf16),
        in_specs=[ANY] * 5,
        out_specs=out,
        scratch_shapes=[pltpu.VMEM(m.shape, f32) for m in masters]
        + [
            pltpu.VMEM((rows, 128), f32),
            pltpu.VMEM((rows, 128), bf16),
            pltpu.SemaphoreType.DMA((5,)),
            pltpu.SemaphoreType.DMA((copies,)),
            pltpu.SemaphoreType.DMA((copies,)),
        ],
        compiler_params=pltpu.CompilerParams(
            collective_id=cid, has_side_effects=True, vmem_limit_bytes=32 * 1024 * 1024
        ),
    )(*masters)


def scatter_kernel(axes, groups, sums, g_ref, red_ref, sq_ref, *scratch):
    own, scratch = scratch[0], scratch[1:]
    arrived, scratch = scratch[: len(groups)], scratch[len(groups) :]
    partial, scratch = scratch[: len(groups) - 1], scratch[len(groups) - 1 :]
    squares, (local, send, recv) = scratch[:-3], scratch[-3:]
    peers = peers_of(axes, groups) + [p for s in sums if s not in groups for p in peers_of(axes, [s])]
    ready = greet(peers)
    left = list(range(len(axes)))
    pick = lambda digits: tuple(digits.get(a, slice(None)) for a in left)
    mine = lambda group: {a: digit(*axes[a]) for a in group}
    load = pltpu.make_async_copy(g_ref.at[pick(mine(groups[0]))], own, local.at[0])
    load.start()
    ready()
    sent, n = [], 0
    current = g_ref
    for s, group in enumerate(groups):
        coming = []
        for o, (place, theirs, _) in enumerate(others(axes, group)):
            copy = remote(current.at[pick(theirs)], arrived[s].at[o], (send, recv), n, place)
            copy.start()
            sent.append(copy)
            coming.append(copy)
            n += 1
        if s == 0:
            load.wait()
            total = own[...].astype(f32)
        else:
            total = current[pick(mine(group))].astype(f32)
        for o, copy in enumerate(coming):
            copy.wait_recv()
            total = total + arrived[s][o].astype(f32)
        left = [a for a in left if a not in group]
        if left:
            partial[s][...] = total.astype(bf16)
            current = partial[s]
    red_ref[...] = total
    square = total * total
    fold = square[0:8]
    for r in range(8, square.shape[0], 8):
        fold = fold + square[r : r + 8]
    fold = jnp.sum(fold, axis=0, keepdims=True)
    for group, ref in zip(sums, squares):
        digits = mine(group)
        ref[tuple(digits[a] for a in group)] = fold
        at = lambda digits: ref.at[tuple(digits[a] for a in group)]
        coming = []
        for place, _, source in others(axes, group):
            copy = remote(at(digits), at(digits), (send, recv), n, place)
            copy.start()
            sent.append(copy)
            coming.append(remote(at(source), at(source), (send, recv), n, place))
            n += 1
        for copy in coming:
            copy.wait_recv()
        fold = 0.0
        for index in itertools.product(*(range(axes[a][2]) for a in group)):
            fold = fold + ref[index]
    sq_ref[...] = fold
    for copy in sent:
        copy.wait_send()


def scatter(axes, groups, sums, grads, cid=1):
    size = lambda a: axes[a][2]
    block = grads.shape[-2:]
    left = list(range(len(axes)))
    arrived, partial = [], []
    for group in groups:
        left = [a for a in left if a not in group]
        shape = tuple(size(a) for a in left) + block
        arrived.append(pltpu.VMEM((math.prod(size(a) for a in group) - 1,) + shape, bf16))
        partial.append(pltpu.VMEM(shape, bf16))
    squares = [pltpu.VMEM(tuple(size(a) for a in group) + (1, 128), f32) for group in sums]
    copies = copies_of(axes, groups) + copies_of(axes, sums)
    return pl.pallas_call(
        functools.partial(scatter_kernel, axes, groups, sums),
        out_shape=(jax.ShapeDtypeStruct(block, f32), jax.ShapeDtypeStruct((1, 128), f32)),
        in_specs=[ANY],
        out_specs=(WHOLE, WHOLE),
        scratch_shapes=[partial[0]]
        + arrived
        + partial[:-1]
        + squares
        + [
            pltpu.SemaphoreType.DMA((1,)),
            pltpu.SemaphoreType.DMA((copies,)),
            pltpu.SemaphoreType.DMA((copies,)),
        ],
        compiler_params=pltpu.CompilerParams(
            collective_id=cid, has_side_effects=True, vmem_limit_bytes=32 * 1024 * 1024
        ),
    )(grads)


def adam(weight, first, second, grad, factor, rate, decay):
    clipped = grad * factor
    first_new = BETA_ONE * first + (1.0 - BETA_ONE) * clipped
    second_new = BETA_TWO * second + (1.0 - BETA_TWO) * clipped * clipped
    direction = (
        first_new
        / (1.0 - BETA_ONE**STEP)
        / (jnp.sqrt(second_new / (1.0 - BETA_TWO**STEP)) + ADAM_EPS)
    )
    return weight - rate * (direction + decay * weight), first_new, second_new


def update_kernel(red, sq, *refs):
    params, outs = refs[:15], refs[15:]
    rd, ro = params[0].shape[0], params[1].shape[0]
    norm = jnp.sqrt(jnp.sum(sq[...], keepdims=True))
    outs[0][...] = norm
    factor = jnp.minimum(1.0, CLIP_NORM / norm)
    rows = (0, 3 * rd, rd, 2 * rd, 3 * rd + ro)
    rates = (0.1, 0.5, 0.1, 0.1, 0.5)
    decays = (DECAY, DECAY, DECAY, DECAY, 0.0)
    for w in range(5):
        height, width = params[w].shape
        grad = red[rows[w] : rows[w] + height, :width]
        new, first_new, second_new = adam(
            params[w][...], params[5 + w][...], params[10 + w][...], grad, factor, rates[w], decays[w]
        )
        outs[1 + 3 * w][...] = new
        outs[2 + 3 * w][...] = first_new
        outs[3 + 3 * w][...] = second_new
        outs[16 + w][...] = grad
        outs[21 + w][...] = new.astype(bf16)


def update(red, sq, params):
    whole = pl.BlockSpec(memory_space=pltpu.VMEM)
    like = lambda p, dtype: jax.ShapeDtypeStruct(p.shape, dtype)
    shapes = [jax.ShapeDtypeStruct((1, 1), f32)]
    shapes += [like(p, f32) for p in params[:5] for _ in range(3)]
    shapes += [like(p, f32) for p in params[:5]]
    shapes += [like(p, bf16) for p in params[:5]]
    return pl.pallas_call(
        update_kernel,
        out_shape=shapes,
        in_specs=[whole] * 17,
        out_specs=[whole] * len(shapes),
        compiler_params=pltpu.CompilerParams(vmem_limit_bytes=32 * 1024 * 1024),
    )(red, sq, *params)


def per_device(n_dp, n_head, tokens, cotangent, lengths, *params):
    masters = params[:5]
    rd, ro = masters[0].shape[0], masters[1].shape[0]
    rows = -(-(3 * rd + 2 * ro) // 16) * 16
    axes, inward, outward, sums = factors(n_dp, n_head)
    weights = gather(axes, inward, rows, masters).reshape(n_head, n_dp, rows, 128)
    mixed, input_grad, grads = layer(lengths, weights, tokens, cotangent, rd, ro)
    grads = grads.reshape(tuple(size for _, _, size in axes) + (rows, 128))
    red, sq = scatter(axes, outward, sums, grads)
    outs = update(red, sq, params)
    return (mixed, input_grad, outs[0].reshape(()), *outs[1:])


def solution(mesh):
    both, split, lens = P(("dp", "head"), None), P("dp", "head"), P("dp", None)
    weight = (split, both, split, split, both)
    return jax.shard_map(
        functools.partial(per_device, mesh.shape["dp"], mesh.shape["head"]),
        mesh=mesh,
        in_specs=(both, both, lens) + weight * 3,
        out_specs=(both, both, P())
        + tuple(spec for spec in weight for _ in range(3))
        + weight
        + weight,
        check_vma=False,
    )
```

```python
import functools
import itertools
import math

import jax
import jax.numpy as jnp
from jax import lax
from jax.experimental import pallas as pl
from jax.experimental.pallas import tpu as pltpu
from jax.sharding import PartitionSpec as P

MAX_LEN = 1024
STEP = 5
NORM_EPS = 1e-05
CLIP_NORM = 0.25
BETA_ONE = 0.5
BETA_TWO = 0.5
ADAM_EPS = 1e-08
DECAY = 0.1
HEADS = 4
HD = 32
D = 128
FF = 512
B = 256
CAP = 50
WIDE = 2 * B
BIG = 2.0**100
LIMIT = 88.0
MASKED = -1e30
SCALE = HD**-0.5 / math.log(2.0)
f32 = jnp.float32
bf16 = jnp.bfloat16
MESH = pl.DeviceIdType.MESH
ANY = pl.BlockSpec(memory_space=pl.ANY)
WHOLE = pl.BlockSpec(memory_space=pltpu.VMEM)


def mm(a, b):
    return lax.dot_general(a, b, (((1,), (0,)), ((), ())), preferred_element_type=f32)


def mm_nt(a, b):
    return lax.dot_general(a, b, (((1,), (1,)), ((), ())), preferred_element_type=f32)


def stats(value):
    mean = jnp.mean(value, axis=0, keepdims=True)
    centred = value - mean
    spread = jnp.mean(centred * centred, axis=0, keepdims=True)
    rate = lax.rsqrt(spread + NORM_EPS)
    return centred * rate, rate


def norm_back(grad, normed, rate, gain):
    scaled = grad * gain
    inner = jnp.mean(scaled, axis=0, keepdims=True)
    along = jnp.mean(scaled * normed, axis=0, keepdims=True)
    return rate * (scaled - inner - normed * along)


def split3(value):
    one = value.astype(bf16).astype(f32)
    two = (value - one).astype(bf16).astype(f32)
    return one, two, value - one - two


def lane_fold(value):
    out = value[:, :128]
    for j in range(1, value.shape[1] // 128):
        out = out + value[:, j * 128 : (j + 1) * 128]
    return out


def together(steps, tiles):
    def pair(p, carry):
        running = [steps(p, half) for half in range(2)]
        while running:
            running = [r for r in running if next(r, "done") != "done"]
        return carry

    lax.fori_loop(0, tiles // 2, pair, 0)


def layer_kernel(
    rd,
    ro,
    lengths,
    w_hbm,
    tokens_hbm,
    cot_hbm,
    mixed_hbm,
    igrad_hbm,
    grads_hbm,
    uq,
    uk,
    us,
    w_ref,
    tokens,
    cot,
    result,
    grads,
    loads,
    stores,
    bounds,
    wqkv_t,
    wqkv,
    wout,
    wout_t,
    wup,
    wup_t,
    wdown,
    wdown_t,
    gains,
    stage,
    qf,
    kf,
    vf,
    kt,
    vt,
    dof,
    probs,
    ds,
    acc,
    dk_acc,
    dv_acc,
    resid_grad,
    first,
    cot_s,
    heads_s,
    second_s,
    low_s,
    hidden_s,
    pre_s,
    causal,
    qn,
    kn,
    g_qkv,
    g_out,
    g_up,
    g_down,
    g_norm,
    g_stage,
):
    n_head, n_dp, rp = w_ref.shape[:3]
    tiles = tokens.shape[0] // B
    row = lax.rem(lax.axis_index("head"), n_head)
    load = [
        pltpu.make_async_copy(src, dst, loads.at[n])
        for n, (src, dst) in enumerate(((w_hbm, w_ref), (tokens_hbm, tokens), (cot_hbm, cot)))
    ]
    for copy in load:
        copy.start()

    starts, ends = [], []
    at = jnp.int32(0)
    for s in range(lengths.shape[1]):
        starts.append(at)
        at = at + lengths[row, s]
        ends.append(at)
    place = lax.broadcasted_iota(jnp.int32, (8, B), 0)
    start_v = jnp.zeros((8, B), jnp.int32)
    end_v = jnp.zeros((8, B), jnp.int32)
    for s in range(8):
        start_v = jnp.where(place == s, starts[s], start_v)
        end_v = jnp.where(place == s, ends[s], end_v)

    def kept(t):
        return jnp.where(t - 1 <= CAP, t - 1, CAP + 1 + lax.rem(t, 2))

    def blank(t, carry):
        uq[t] = 0
        uk[t] = 0
        us[t] = 0
        return carry

    def list_q(i, n):
        low = jnp.int32(0)
        for s in range(1, 8):
            low = jnp.where(starts[s] <= i * B, starts[s], low)

        def list_k(j, n):
            uq[n] = i
            uk[n] = j
            us[n] = kept(n)
            return n + 1

        return lax.fori_loop(lax.div(low, B), i + 1, list_k, n)

    lax.fori_loop(0, 2, blank, 0)
    units = lax.fori_loop(0, tiles, list_q, jnp.int32(2))
    lax.fori_loop(units, units + 4, blank, 0)
    pairs = lax.div(units + 1, 2) + 1

    key_i = lax.broadcasted_iota(jnp.int32, (B, B), 0)
    query_i = lax.broadcasted_iota(jnp.int32, (B, B), 1)
    allowed = key_i <= query_i
    causal[0] = jnp.full((B, B), jnp.inf, bf16)
    causal[1] = jnp.where(allowed, jnp.inf, 0.0).astype(bf16)
    probs[0] = jnp.zeros_like(probs[0])
    for ref in (ds, qn, kn, g_qkv, g_out, g_up, g_down, g_norm, cot_s, heads_s, second_s, low_s, hidden_s, pre_s):
        ref[...] = jnp.zeros_like(ref)

    load[0].wait()
    for h in range(n_head):
        stage[...] = jnp.concatenate([w_ref[h, d].astype(f32) for d in range(n_dp)], axis=0)
        pick = lambda lo, n: jnp.concatenate(
            [stage[d * rp + lo : d * rp + lo + n] for d in range(n_dp)], axis=0
        )
        q = pick(0, rd)
        wqkv_t[h] = q.T[: 3 * HD].astype(bf16)
        wqkv[:, h * 3 * HD : (h + 1) * 3 * HD] = q[:, : 3 * HD].astype(bf16)
        u = pick(rd, rd)
        wup[:, h * 128 : (h + 1) * 128] = u.astype(bf16)
        wup_t[h * 128 : (h + 1) * 128] = u.T.astype(bf16)
        u = pick(2 * rd, rd)
        wdown[:, h * 128 : (h + 1) * 128] = u.astype(bf16)
        wdown_t[h * 128 : (h + 1) * 128] = u.T.astype(bf16)
        for d in range(n_dp):
            at = (d * n_head + h) * ro
            g_out[at : at + ro] = stage[d * rp + 3 * rd : d * rp + 3 * rd + ro]
            gains[at : at + ro] = stage[d * rp + 3 * rd + ro : d * rp + 3 * rd + 2 * ro]
    wo = g_out[...]
    wout[...] = wo.astype(bf16)
    wout_t[...] = wo.T.astype(bf16)
    g_out[...] = jnp.zeros_like(g_out)
    gain1, shift1 = gains[:, 0:1], gains[:, 1:2]
    gain2, shift2 = gains[:, 2:3], gains[:, 3:4]

    def project(p, half):
        i = 2 * p + half
        x = tokens[pl.ds(pl.multiple_of(i * B, B), B), :].astype(f32).T
        yield
        n1, _ = stats(x)
        f = (n1 * gain1 + shift1).astype(bf16)
        first[p, :, half * B : (half + 1) * B] = f
        yield
        where_t = i * B + lax.broadcasted_iota(jnp.int32, (8, B), 1)
        inside = ((where_t >= start_v) & (where_t < end_v)).astype(f32)
        penalty = (1.0 - inside) * -BIG
        zeros8 = jnp.zeros((8, B), f32)
        ones8 = jnp.ones((8, B), f32)
        zeros16 = jnp.zeros((16, B), f32)
        for h in range(HEADS):
            packed = mm(wqkv_t[h], f).astype(bf16)
            yield
            pf = packed.astype(f32)
            q = pf[:HD]
            k = pf[HD : 2 * HD]
            v = pf[2 * HD :]
            qn[h] = jnp.maximum(qn[h], jnp.sum(q * q, axis=0, keepdims=True))
            kn[h] = jnp.maximum(kn[h], jnp.sum(k * k, axis=0, keepdims=True))
            qf[h, i] = jnp.concatenate([q, penalty, zeros8, zeros16], axis=0).astype(bf16)
            kf[h, i] = packed[HD : 2 * HD]
            vf[h, i] = jnp.concatenate([v, ones8, zeros8], axis=0).astype(bf16)
            kt[h, i] = jnp.concatenate([k, inside, ones8, zeros16], axis=0).T.astype(bf16)
            vt[h, i] = jnp.concatenate([v, ones8, zeros8, zeros16], axis=0).T.astype(bf16)
            acc[h, i] = jnp.zeros_like(acc[h, i])
            dk_acc[h, i] = jnp.zeros_like(dk_acc[h, i])
            dv_acc[h, i] = jnp.zeros_like(dv_acc[h, i])
            yield

    load[1].wait()
    together(project, tiles)

    bound = jnp.float32(0.0)
    for h in range(HEADS):
        bound = jnp.maximum(bound, jnp.max(qn[h]) * jnp.max(kn[h]))

    def scores(h, i, j):
        return mm(kt[h, j], qf[h, i])

    @pl.when(jnp.logical_not(bound * SCALE**2 <= LIMIT * LIMIT))
    def _():
        bounds[...] = jnp.full_like(bounds, MASKED)

        def top(t, carry):
            i, j = uq[t], uk[t]
            masked = jnp.where(allowed | (i != j), 0.0, MASKED)
            for h in range(HEADS):
                s = scores(h, i, j) + masked
                bounds[h, i] = jnp.maximum(bounds[h, i], jnp.max(s, axis=0, keepdims=True))
            return carry

        lax.fori_loop(2, units, top, 0)

        def shift(i, carry):
            for h in range(HEADS):
                one, two, three = split3(-bounds[h, i])
                r = lax.broadcasted_iota(jnp.int32, (16, B), 0)
                old = qf[h, i, HD : HD + 16].astype(f32)
                new = jnp.where(r == 8, one, jnp.where(r == 9, two, jnp.where(r == 10, three, old)))
                qf[h, i, HD : HD + 16] = new.astype(bf16)
            return carry

        lax.fori_loop(0, tiles, shift, 0)

    def weigh(t, slot):
        i, j = uq[t], uk[t]
        cut = causal[jnp.where(i == j, 1, 0)]
        for h in range(HEADS):
            probs[slot, h] = jnp.minimum(jnp.exp2(scores(h, i, j) * SCALE).astype(bf16), cut)

    def forward(p, carry):
        for t in (2 * p - 2, 2 * p - 1):
            i, j, slot = uq[t], uk[t], us[t]
            for h in range(HEADS):
                acc[h, i] += mm(vf[h, j, : HD + 8], probs[slot, h])
        for t in (2 * p, 2 * p + 1):
            weigh(t, kept(t))
        return carry

    lax.fori_loop(1, pairs, forward, 0)

    def feed_grads():
        g_down[...] += mm_nt(cot_s[...], hidden_s[...])
        g_up[...] += mm_nt(second_s[...], pre_s[...])
        g_out[...] += mm_nt(heads_s[...], low_s[...])

    def write_tile(p, half, hbm):
        i = 2 * p + half
        at = pl.ds(pl.multiple_of(i * B, B), B)
        return pltpu.make_async_copy(result.at[at], hbm.at[at], stores.at[i])

    def feed(p, half):
        i = 2 * p + half
        at = pl.ds(pl.multiple_of(i * B, B), B)
        lanes = slice(half * B, (half + 1) * B)
        if half == 0:
            feed_grads()
        outs, inv = [], []
        for h in range(HEADS):
            r = 1.0 / acc[h, i, HD : HD + 1]
            inv.append(r)
            outs.append(acc[h, i, :HD] * r)
            acc[h, i] = jnp.zeros_like(acc[h, i])
        heads = jnp.concatenate(outs, axis=0).astype(bf16)
        x = tokens[at, :].astype(f32).T
        c32 = cot[at, :].astype(f32).T
        c16 = c32.astype(bf16)
        yield
        resid = x + mm(wout_t[...], heads)
        yield
        n2, rate2 = stats(resid)
        second = (n2 * gain2 + shift2).astype(bf16)
        yield
        heads_s[:, lanes] = heads
        cot_s[:, lanes] = c16
        second_s[:, lanes] = second
        for c in range(0, FF, 128):
            rows = slice(c, c + 128)
            pre = mm(wup_t[rows], second)
            back = mm(wdown_t[rows], c16)
            yield
            cdf = 0.5 * (1.0 + lax.erf(pre * (0.5**0.5)))
            pdf = jnp.exp(-0.5 * pre * pre) * (1.0 / math.sqrt(2.0 * math.pi))
            hidden_s[rows, lanes] = (pre * cdf).astype(bf16)
            pre_s[rows, lanes] = (back * (cdf + pre * pdf)).astype(bf16)
            yield
        second_in = mm(wup[...], pre_s[:, lanes])
        yield
        result[at, :] = (resid + mm(wdown[...], hidden_s[:, lanes])).T.astype(bf16)
        g_norm[2] += lane_fold(second_in * n2)
        g_norm[3] += lane_fold(second_in)
        rg = c32 + norm_back(second_in, n2, rate2, gain2)
        low = rg.astype(bf16)
        yield
        hg = mm(wout[...], low).astype(bf16).astype(f32)
        resid_grad[i] = rg
        low_s[:, lanes] = low
        yield
        zeros16 = jnp.zeros((16, B), f32)
        r8 = lax.broadcasted_iota(jnp.int32, (16, B), 0)
        for h in range(HEADS):
            do = (hg[h * HD : (h + 1) * HD] * inv[h]).astype(bf16).astype(f32)
            delta = jnp.sum(do * outs[h], axis=0, keepdims=True)
            one, two, three = split3(-delta)
            extra = jnp.where(r8 == 0, one, jnp.where(r8 == 1, two, jnp.where(r8 == 2, three, 0.0)))
            dof[h, i] = jnp.concatenate([do, extra, zeros16], axis=0).astype(bf16)
        write_tile(p, half, mixed_hbm).start()

    load[2].wait()
    together(feed, tiles)
    feed_grads()

    def backward(p, carry):
        for t in (2 * p, 2 * p + 1):
            pl.when(us[t] > CAP)(lambda: weigh(t, us[t]))
        for s, t in enumerate((2 * p - 2, 2 * p - 1)):
            i, j = uq[t], uk[t]
            for h in range(HEADS):
                sg = ds[s, h]
                acc[h, i, :HD] += mm(kf[h, j], sg)
                dk_acc[h, j] += mm_nt(qf[h, i, :HD], sg)
        for s, t in enumerate((2 * p, 2 * p + 1)):
            i, j, slot = uq[t], uk[t], us[t]
            for h in range(HEADS):
                w = probs[slot, h]
                pg = mm(vt[h, j], dof[h, i])
                ds[s, h] = (w.astype(f32) * pg).astype(bf16)
                dv_acc[h, j] += mm_nt(dof[h, i, :HD], w)
        return carry

    lax.fori_loop(1, pairs, backward, 0)

    def wait_tile(i, carry):
        at = pl.ds(pl.multiple_of(i * B, B), B)
        pltpu.make_async_copy(result.at[at], mixed_hbm.at[at], stores.at[i]).wait()
        return carry

    lax.fori_loop(0, tiles, wait_tile, 0)

    def finish(p, half):
        i = 2 * p + half
        at = pl.ds(pl.multiple_of(i * B, B), B)
        lanes = slice(half * B, (half + 1) * B)
        rows = []
        for h in range(HEADS):
            rows += [acc[h, i, :HD] * HD**-0.5, dk_acc[h, i] * HD**-0.5, dv_acc[h, i]]
        packed_grad = jnp.concatenate(rows, axis=0).astype(bf16)
        hidden_s[: 3 * D, lanes] = packed_grad
        yield
        first_in = mm(wqkv[...], packed_grad)
        if half == 1:
            g_qkv[...] += mm_nt(first[p], hidden_s[: 3 * D, :])
        x = tokens[at, :].astype(f32).T
        yield
        n1, rate1 = stats(x)
        yield
        g_norm[0] += lane_fold(first_in * n1)
        g_norm[1] += lane_fold(first_in)
        out = resid_grad[i] + norm_back(first_in, n1, rate1, gain1)
        yield
        result[at, :] = out.T.astype(bf16)
        write_tile(p, half, igrad_hbm).start()

    together(finish, tiles)

    lane = lax.broadcasted_iota(jnp.int32, (D, 128), 1)
    norm = jnp.zeros((D, 128), f32)
    for c in range(4):
        norm = jnp.where(lane == c, jnp.sum(g_norm[c], axis=1, keepdims=True), norm)
    gains[...] = norm
    g_stage[...] = jnp.zeros_like(g_stage)
    for h in range(n_head):
        cols = slice(h * 128, (h + 1) * 128)
        qkv = g_qkv[:, h * 3 * HD : (h + 1) * 3 * HD]
        for d in range(n_dp):
            rows = slice(d * rd, (d + 1) * rd)
            at = (d * n_head + h) * ro
            g_stage[0:rd, : 3 * HD] = qkv[rows]
            g_stage[rd : 2 * rd] = g_up[rows, cols]
            g_stage[2 * rd : 3 * rd] = g_down[rows, cols]
            g_stage[3 * rd : 3 * rd + ro] = g_out[at : at + ro]
            g_stage[3 * rd + ro : 3 * rd + 2 * ro] = gains[at : at + ro]
            grads[h, d] = g_stage[...].astype(bf16)
    out = pltpu.make_async_copy(grads, grads_hbm, loads.at[0])
    out.start()

    def wait_last(i, carry):
        at = pl.ds(pl.multiple_of(i * B, B), B)
        pltpu.make_async_copy(result.at[at], igrad_hbm.at[at], stores.at[i]).wait()
        return carry

    lax.fori_loop(0, tiles, wait_last, 0)
    out.wait()


def layer(lengths, weights, tokens, cot, rd, ro):
    n_head, n_dp, rp = weights.shape[:3]
    tiles = tokens.shape[0] // B
    listed = tiles * (MAX_LEN // B + 1) + 8
    vmem = lambda shape, dtype: pltpu.VMEM(shape, dtype)
    scratch = [
        pltpu.SMEM((listed,), jnp.int32),
        pltpu.SMEM((listed,), jnp.int32),
        pltpu.SMEM((listed,), jnp.int32),
        vmem(weights.shape, bf16),
        vmem(tokens.shape, bf16),
        vmem(tokens.shape, bf16),
        vmem(tokens.shape, bf16),
        vmem((n_head, n_dp, rp, 128), bf16),
        pltpu.SemaphoreType.DMA((3,)),
        pltpu.SemaphoreType.DMA((tiles,)),
        vmem((HEADS, tiles, 1, B), f32),
        vmem((HEADS, 3 * HD, D), bf16),
        vmem((D, 3 * D), bf16),
        vmem((D, D), bf16),
        vmem((D, D), bf16),
        vmem((D, FF), bf16),
        vmem((FF, D), bf16),
        vmem((D, FF), bf16),
        vmem((FF, D), bf16),
        vmem((D, 128), f32),
        vmem((n_dp * rp, 128), f32),
        vmem((HEADS, tiles, 64, B), bf16),
        vmem((HEADS, tiles, HD, B), bf16),
        vmem((HEADS, tiles, 48, B), bf16),
        vmem((HEADS, tiles, B, 64), bf16),
        vmem((HEADS, tiles, B, 64), bf16),
        vmem((HEADS, tiles, 64, B), bf16),
        vmem((CAP + 3, HEADS, B, B), bf16),
        vmem((2, HEADS, B, B), bf16),
        vmem((HEADS, tiles, HD + 8, B), f32),
        vmem((HEADS, tiles, HD, B), f32),
        vmem((HEADS, tiles, HD, B), f32),
        vmem((tiles, D, B), f32),
        vmem((tiles // 2, D, WIDE), bf16),
        vmem((D, WIDE), bf16),
        vmem((D, WIDE), bf16),
        vmem((D, WIDE), bf16),
        vmem((D, WIDE), bf16),
        vmem((FF, WIDE), bf16),
        vmem((FF, WIDE), bf16),
        vmem((2, B, B), bf16),
        vmem((HEADS, 1, B), f32),
        vmem((HEADS, 1, B), f32),
        vmem((D, 3 * D), f32),
        vmem((D, D), f32),
        vmem((D, FF), f32),
        vmem((D, FF), f32),
        vmem((4, D, 128), f32),
        vmem((rp, 128), f32),
    ]
    return pl.pallas_call(
        functools.partial(layer_kernel, rd, ro),
        out_shape=(
            jax.ShapeDtypeStruct(tokens.shape, bf16),
            jax.ShapeDtypeStruct(tokens.shape, bf16),
            jax.ShapeDtypeStruct((n_head, n_dp, rp, 128), bf16),
        ),
        in_specs=[pl.BlockSpec(memory_space=pltpu.SMEM), ANY, ANY, ANY],
        out_specs=(ANY, ANY, ANY),
        scratch_shapes=scratch,
        compiler_params=pltpu.CompilerParams(vmem_limit_bytes=63 * 1024 * 1024),
    )(lengths, weights, tokens, cot)


def factors(n_dp, n_head):
    if (n_dp, n_head) == (8, 4):
        axes = (("head", 2, 2), ("head", 1, 2), ("dp", 2, 4), ("dp", 1, 2))
        return axes, ((2,), (0, 3), (1,)), ((1,), (0, 3), (2,)), ((1,), (0, 2, 3))
    axes, left = [("head", 1, n_head)], n_dp
    while left > 1:
        size = 4 if left % 4 == 0 else left
        left //= size
        axes.append(("dp", left, size))
    each = tuple((a,) for a in range(len(axes)))
    return tuple(axes), each[::-1], each, each


def digit(axis, stride, size):
    return lax.rem(lax.div(lax.axis_index(axis), stride), size)


def others(axes, group):
    found = []
    for offsets in itertools.product(*(range(axes[a][2]) for a in group)):
        if not any(offsets):
            continue
        place, theirs, source = {}, {}, {}
        for a, offset in zip(group, offsets):
            axis, stride, size = axes[a]
            mine = digit(*axes[a])
            theirs[a] = lax.rem(mine + offset, size)
            source[a] = lax.rem(mine + size - offset, size)
            place[axis] = place.get(axis, lax.axis_index(axis)) + (theirs[a] - mine) * stride
        found.append((place, theirs, source))
    return found


def greet(peers):
    barrier = pltpu.get_barrier_semaphore()
    for device in peers:
        pl.semaphore_signal(barrier, inc=1, device_id=device, device_id_type=MESH)
    return lambda: pl.semaphore_wait(barrier, len(peers))


def remote(src, dst, sems, n, device):
    return pltpu.make_async_remote_copy(
        src_ref=src,
        dst_ref=dst,
        send_sem=sems[0].at[n],
        recv_sem=sems[1].at[n],
        device_id=device,
        device_id_type=MESH,
    )


def peers_of(axes, groups):
    return [place for group in groups for place, _, _ in others(axes, group)]


def gather_kernel(axes, groups, *refs):
    masters, w_ref = refs[:5], refs[5]
    held, (stage, block, local, send, recv) = refs[6:11], refs[11:]
    arrived = greet(peers_of(axes, groups))
    loads = [pltpu.make_async_copy(m, h, local.at[n]) for n, (m, h) in enumerate(zip(masters, held))]
    for load in loads:
        load.start()
    stage[...] = jnp.zeros_like(stage)
    for load in loads:
        load.wait()
    qkv, out, up, down, norm = held
    rd, ro = qkv.shape[0], out.shape[0]
    at = 0
    for part, height in ((qkv, rd), (up, rd), (down, rd), (out, ro), (norm, ro)):
        stage[at : at + height, : part.shape[1]] = part[...]
        at += height
    block[...] = stage[...].astype(bf16)
    have = [digit(*axis) for axis in axes]
    keep = pltpu.make_async_copy(block, w_ref.at[tuple(have)], local.at[0])
    keep.start()
    arrived()
    sent, n = [], 0
    for group in groups:
        coming = []
        for place, _, source in others(axes, group):
            mine = w_ref.at[tuple(have)]
            copy = remote(block if n < len(others(axes, groups[0])) else mine, mine, (send, recv), n, place)
            copy.start()
            sent.append(copy)
            there = list(have)
            for a in group:
                there[a] = source[a]
            there = w_ref.at[tuple(there)]
            coming.append(remote(there, there, (send, recv), n, place))
            n += 1
        if group is groups[0]:
            keep.wait()
        for copy in coming:
            copy.wait_recv()
        for a in group:
            have[a] = slice(None)
    for copy in sent:
        copy.wait_send()


def copies_of(axes, groups):
    return sum(math.prod(axes[a][2] for a in group) - 1 for group in groups)


def gather(axes, groups, rows, masters, cid=0, out=ANY):
    copies = copies_of(axes, groups)
    shape = tuple(size for _, _, size in axes) + (rows, 128)
    return pl.pallas_call(
        functools.partial(gather_kernel, axes, groups),
        out_shape=jax.ShapeDtypeStruct(shape, bf16),
        in_specs=[ANY] * 5,
        out_specs=out,
        scratch_shapes=[pltpu.VMEM(m.shape, f32) for m in masters]
        + [
            pltpu.VMEM((rows, 128), f32),
            pltpu.VMEM((rows, 128), bf16),
            pltpu.SemaphoreType.DMA((5,)),
            pltpu.SemaphoreType.DMA((copies,)),
            pltpu.SemaphoreType.DMA((copies,)),
        ],
        compiler_params=pltpu.CompilerParams(
            collective_id=cid, has_side_effects=True, vmem_limit_bytes=62 * 1024 * 1024
        ),
    )(*masters)


def scatter_kernel(axes, groups, sums, g_ref, red_ref, sq_ref, *scratch):
    own, scratch = scratch[0], scratch[1:]
    arrived, scratch = scratch[: len(groups)], scratch[len(groups) :]
    partial, scratch = scratch[: len(groups) - 1], scratch[len(groups) - 1 :]
    squares, (local, send, recv) = scratch[:-3], scratch[-3:]
    peers = peers_of(axes, groups) + [p for s in sums if s not in groups for p in peers_of(axes, [s])]
    ready = greet(peers)
    left = list(range(len(axes)))
    pick = lambda digits: tuple(digits.get(a, slice(None)) for a in left)
    mine = lambda group: {a: digit(*axes[a]) for a in group}
    load = pltpu.make_async_copy(g_ref.at[pick(mine(groups[0]))], own, local.at[0])
    load.start()
    ready()
    sent, n = [], 0
    current = g_ref
    for s, group in enumerate(groups):
        coming = []
        for o, (place, theirs, _) in enumerate(others(axes, group)):
            copy = remote(current.at[pick(theirs)], arrived[s].at[o], (send, recv), n, place)
            copy.start()
            sent.append(copy)
            coming.append(copy)
            n += 1
        if s == 0:
            load.wait()
            total = own[...].astype(f32)
        else:
            total = current[pick(mine(group))].astype(f32)
        for o, copy in enumerate(coming):
            copy.wait_recv()
            total = total + arrived[s][o].astype(f32)
        left = [a for a in left if a not in group]
        if left:
            partial[s][...] = total.astype(bf16)
            current = partial[s]
    red_ref[...] = total
    square = total * total
    fold = square[0:8]
    for r in range(8, square.shape[0], 8):
        fold = fold + square[r : r + 8]
    fold = jnp.sum(fold, axis=0, keepdims=True)
    for group, ref in zip(sums, squares):
        digits = mine(group)
        ref[tuple(digits[a] for a in group)] = fold
        at = lambda digits: ref.at[tuple(digits[a] for a in group)]
        coming = []
        for place, _, source in others(axes, group):
            copy = remote(at(digits), at(digits), (send, recv), n, place)
            copy.start()
            sent.append(copy)
            coming.append(remote(at(source), at(source), (send, recv), n, place))
            n += 1
        for copy in coming:
            copy.wait_recv()
        fold = 0.0
        for index in itertools.product(*(range(axes[a][2]) for a in group)):
            fold = fold + ref[index]
    sq_ref[...] = fold
    for copy in sent:
        copy.wait_send()


def scatter(axes, groups, sums, grads, cid=1):
    size = lambda a: axes[a][2]
    block = grads.shape[-2:]
    left = list(range(len(axes)))
    arrived, partial = [], []
    for group in groups:
        left = [a for a in left if a not in group]
        shape = tuple(size(a) for a in left) + block
        arrived.append(pltpu.VMEM((math.prod(size(a) for a in group) - 1,) + shape, bf16))
        partial.append(pltpu.VMEM(shape, bf16))
    squares = [pltpu.VMEM(tuple(size(a) for a in group) + (1, 128), f32) for group in sums]
    copies = copies_of(axes, groups) + copies_of(axes, sums)
    return pl.pallas_call(
        functools.partial(scatter_kernel, axes, groups, sums),
        out_shape=(jax.ShapeDtypeStruct(block, f32), jax.ShapeDtypeStruct((1, 128), f32)),
        in_specs=[ANY],
        out_specs=(WHOLE, WHOLE),
        scratch_shapes=[partial[0]]
        + arrived
        + partial[:-1]
        + squares
        + [
            pltpu.SemaphoreType.DMA((1,)),
            pltpu.SemaphoreType.DMA((copies,)),
            pltpu.SemaphoreType.DMA((copies,)),
        ],
        compiler_params=pltpu.CompilerParams(
            collective_id=cid, has_side_effects=True, vmem_limit_bytes=65228 * 1024
        ),
    )(grads)


def adam(weight, first, second, grad, factor, rate, decay):
    clipped = grad * factor
    first_new = BETA_ONE * first + (1.0 - BETA_ONE) * clipped
    second_new = BETA_TWO * second + (1.0 - BETA_TWO) * clipped * clipped
    direction = (
        first_new
        / (1.0 - BETA_ONE**STEP)
        / (jnp.sqrt(second_new / (1.0 - BETA_TWO**STEP)) + ADAM_EPS)
    )
    return weight - rate * (direction + decay * weight), first_new, second_new


def update_kernel(red, sq, *refs):
    params, outs = refs[:15], refs[15:]
    rd, ro = params[0].shape[0], params[1].shape[0]
    norm = jnp.sqrt(jnp.sum(sq[...], keepdims=True))
    outs[0][...] = norm
    factor = jnp.minimum(1.0, CLIP_NORM / norm)
    rows = (0, 3 * rd, rd, 2 * rd, 3 * rd + ro)
    rates = (0.1, 0.5, 0.1, 0.1, 0.5)
    decays = (DECAY, DECAY, DECAY, DECAY, 0.0)
    for w in range(5):
        height, width = params[w].shape
        grad = red[rows[w] : rows[w] + height, :width]
        new, first_new, second_new = adam(
            params[w][...], params[5 + w][...], params[10 + w][...], grad, factor, rates[w], decays[w]
        )
        outs[1 + 3 * w][...] = new
        outs[2 + 3 * w][...] = first_new
        outs[3 + 3 * w][...] = second_new
        outs[16 + w][...] = grad
        outs[21 + w][...] = new.astype(bf16)


def update(red, sq, params):
    like = lambda p, dtype: jax.ShapeDtypeStruct(p.shape, dtype)
    shapes = [jax.ShapeDtypeStruct((1, 1), f32)]
    shapes += [like(p, f32) for p in params[:5] for _ in range(3)]
    shapes += [like(p, f32) for p in params[:5]]
    shapes += [like(p, bf16) for p in params[:5]]
    return pl.pallas_call(
        update_kernel,
        out_shape=shapes,
        in_specs=[WHOLE] * 17,
        out_specs=[WHOLE] * len(shapes),
        compiler_params=pltpu.CompilerParams(vmem_limit_bytes=32 * 1024 * 1024),
    )(red, sq, *params)


def per_device(n_dp, n_head, tokens, cotangent, lengths, *params):
    masters = params[:5]
    rd, ro = masters[0].shape[0], masters[1].shape[0]
    rows = -(-(3 * rd + 2 * ro) // 16) * 16
    axes, inward, outward, sums = factors(n_dp, n_head)
    weights = gather(axes, inward, rows, masters).reshape(n_head, n_dp, rows, 128)
    mixed, input_grad, grads = layer(lengths, weights, tokens, cotangent, rd, ro)
    grads = grads.reshape(tuple(size for _, _, size in axes) + (rows, 128))
    red, sq = scatter(axes, outward, sums, grads)
    outs = update(red, sq, params)
    return (mixed, input_grad, outs[0].reshape(()), *outs[1:])


def solution(mesh):
    both, split, lens = P(("dp", "head"), None), P("dp", "head"), P("dp", None)
    weight = (split, both, split, split, both)
    return jax.shard_map(
        functools.partial(per_device, mesh.shape["dp"], mesh.shape["head"]),
        mesh=mesh,
        in_specs=(both, both, lens) + weight * 3,
        out_specs=(both, both, P())
        + tuple(spec for spec in weight for _ in range(3))
        + weight
        + weight,
        check_vma=False,
    )
```

```python
import functools
import itertools
import math

import jax
import jax.numpy as jnp
from jax import lax
from jax.experimental import pallas as pl
from jax.experimental.pallas import tpu as pltpu
from jax.sharding import PartitionSpec as P

MAX_LEN = 1024
STEP = 5
NORM_EPS = 1e-05
CLIP_NORM = 0.25
BETA_ONE = 0.5
BETA_TWO = 0.5
ADAM_EPS = 1e-08
DECAY = 0.1
HEADS = 4
HD = 32
D = 128
FF = 512
B = 256
CAP = 46
CHUNK = 128
GROUP = 2
SIDE = 4
WIDE = SIDE * B
BIG = 2.0**100
LIMIT = 88.0
MASKED = -1e30
SCALE = HD**-0.5 / math.log(2.0)
f32 = jnp.float32
bf16 = jnp.bfloat16
MESH = pl.DeviceIdType.MESH
HBM = pl.BlockSpec(memory_space=pltpu.HBM)
WHOLE = pl.BlockSpec(memory_space=pltpu.VMEM)


def mm(a, b):
    return lax.dot_general(a, b, (((1,), (0,)), ((), ())), preferred_element_type=f32)


def mm_nt(a, b):
    return lax.dot_general(a, b, (((1,), (1,)), ((), ())), preferred_element_type=f32)


def stats(value):
    mean = jnp.mean(value, axis=0, keepdims=True)
    centred = value - mean
    spread = jnp.mean(centred * centred, axis=0, keepdims=True)
    rate = lax.rsqrt(spread + NORM_EPS)
    return centred * rate, rate


def norm_back(grad, normed, rate, gain):
    scaled = grad * gain
    inner = jnp.mean(scaled, axis=0, keepdims=True)
    along = jnp.mean(scaled * normed, axis=0, keepdims=True)
    return rate * (scaled - inner - normed * along)


def split3(value):
    one = value.astype(bf16).astype(f32)
    two = (value - one).astype(bf16).astype(f32)
    return one, two, value - one - two


def lane_fold(value):
    out = value[:, :128]
    for j in range(1, value.shape[1] // 128):
        out = out + value[:, j * 128 : (j + 1) * 128]
    return out


def together(steps, tiles):
    def pair(p, carry):
        running = [steps(p, half) for half in range(SIDE)]
        while running:
            running = [r for r in running if next(r, "done") != "done"]
        return carry

    lax.fori_loop(0, tiles // SIDE, pair, 0)


def layer_kernel(
    rd,
    ro,
    lengths,
    w_hbm,
    tokens_hbm,
    cot_hbm,
    mixed_hbm,
    igrad_hbm,
    grads_hbm,
    uq,
    uk,
    us,
    w_ref,
    tokens,
    cot,
    result,
    grads,
    loads,
    stores,
    bounds,
    wqkv_t,
    wqkv,
    wout,
    wout_t,
    wup,
    wup_t,
    wdown,
    wdown_t,
    gains,
    stage,
    qf,
    kf,
    vf,
    kt,
    vt,
    dof,
    probs,
    turn_a,
    turn_b,
    acc,
    dk_acc,
    dv_acc,
    resid_grad,
    first,
    cot_s,
    heads_s,
    second_s,
    low_s,
    hidden_s,
    pre_s,
    causal,
    qn,
    kn,
    g_qkv,
    g_out,
    g_up,
    g_down,
    g_norm,
    g_stage,
):
    n_head, n_dp, rp = w_ref.shape[:3]
    tiles = tokens.shape[0] // B
    row = lax.rem(lax.axis_index("head"), n_head)
    load = [
        pltpu.make_async_copy(src, dst, loads.at[n])
        for n, (src, dst) in enumerate(((w_hbm, w_ref), (tokens_hbm, tokens), (cot_hbm, cot)))
    ]
    for copy in load:
        copy.start()

    starts, ends = [], []
    at = jnp.int32(0)
    for s in range(lengths.shape[1]):
        starts.append(at)
        at = at + lengths[row, s]
        ends.append(at)
    place = lax.broadcasted_iota(jnp.int32, (8, B), 0)
    start_v = jnp.zeros((8, B), jnp.int32)
    end_v = jnp.zeros((8, B), jnp.int32)
    for s in range(8):
        start_v = jnp.where(place == s, starts[s], start_v)
        end_v = jnp.where(place == s, ends[s], end_v)

    def kept(t):
        return jnp.where(t - GROUP < CAP, t - GROUP + 1, CAP + 1 + lax.rem(t, GROUP))

    def blank(t, carry):
        uq[t] = 0
        uk[t] = 0
        us[t] = 0
        return carry

    def list_q(i, n):
        low = jnp.int32(0)
        for s in range(1, 8):
            low = jnp.where(starts[s] <= i * B, starts[s], low)

        def list_k(j, n):
            uq[n] = i
            uk[n] = j
            us[n] = kept(n)
            return n + 1

        return lax.fori_loop(lax.div(low, B), i + 1, list_k, n)

    lax.fori_loop(0, GROUP, blank, 0)
    units = lax.fori_loop(0, tiles, list_q, jnp.int32(GROUP))
    lax.fori_loop(units, units + 2 * GROUP, blank, 0)
    steps = lax.div(units, GROUP) + 1

    key_i = lax.broadcasted_iota(jnp.int32, (B, B), 0)
    query_i = lax.broadcasted_iota(jnp.int32, (B, B), 1)
    allowed = key_i <= query_i
    causal[0] = jnp.full((B, B), jnp.inf, bf16)
    causal[1] = jnp.where(allowed, jnp.inf, 0.0).astype(bf16)
    causal[2] = jnp.zeros((B, B), bf16)
    probs[0] = jnp.zeros_like(probs[0])
    for ref in (qn, kn, g_qkv, g_out, g_up, g_down, g_norm, cot_s, heads_s, second_s, low_s, hidden_s, pre_s):
        ref[...] = jnp.zeros_like(ref)

    load[0].wait()
    for h in range(n_head):
        stage[...] = jnp.concatenate([w_ref[h, d].astype(f32) for d in range(n_dp)], axis=0)
        pick = lambda lo, n: jnp.concatenate(
            [stage[d * rp + lo : d * rp + lo + n] for d in range(n_dp)], axis=0
        )
        q = pick(0, rd)
        wqkv_t[h] = q.T[: 3 * HD].astype(bf16)
        wqkv[:, h * 3 * HD : (h + 1) * 3 * HD] = q[:, : 3 * HD].astype(bf16)
        u = pick(rd, rd)
        wup[:, h * 128 : (h + 1) * 128] = u.astype(bf16)
        wup_t[h * 128 : (h + 1) * 128] = u.T.astype(bf16)
        u = pick(2 * rd, rd)
        wdown[:, h * 128 : (h + 1) * 128] = u.astype(bf16)
        wdown_t[h * 128 : (h + 1) * 128] = u.T.astype(bf16)
        for d in range(n_dp):
            at = (d * n_head + h) * ro
            g_out[at : at + ro] = stage[d * rp + 3 * rd : d * rp + 3 * rd + ro]
            gains[at : at + ro] = stage[d * rp + 3 * rd + ro : d * rp + 3 * rd + 2 * ro]
    wo = g_out[...]
    wout[...] = wo.astype(bf16)
    wout_t[...] = wo.T.astype(bf16)
    g_out[...] = jnp.zeros_like(g_out)
    gain1, shift1 = gains[:, 0:1], gains[:, 1:2]
    gain2, shift2 = gains[:, 2:3], gains[:, 3:4]

    def project(p, half):
        i = SIDE * p + half
        x = tokens[pl.ds(pl.multiple_of(i * B, B), B), :].astype(f32).T
        yield
        n1, _ = stats(x)
        f = (n1 * gain1 + shift1).astype(bf16)
        first[p, :, half * B : (half + 1) * B] = f
        yield
        where_t = i * B + lax.broadcasted_iota(jnp.int32, (8, B), 1)
        inside = ((where_t >= start_v) & (where_t < end_v)).astype(f32)
        zeros8 = jnp.zeros((8, B), f32)
        ones8 = jnp.ones((8, B), f32)
        key_side = jnp.concatenate([inside, ones8], axis=0).astype(bf16)
        query_side = jnp.concatenate([(1.0 - inside) * -BIG, zeros8], axis=0).astype(bf16)
        value_side = jnp.concatenate([ones8, zeros8], axis=0).astype(bf16)
        for h in range(HEADS):
            packed = mm(wqkv_t[h], f).astype(bf16)
            yield
            q, k, v = (packed[n * HD : (n + 1) * HD] for n in range(3))
            squares = packed.astype(f32)
            squares = squares * squares
            qn[h] = jnp.maximum(qn[h], jnp.sum(squares[:HD], axis=0, keepdims=True))
            kn[h] = jnp.maximum(kn[h], jnp.sum(squares[HD : 2 * HD], axis=0, keepdims=True))
            qf[h, i, :HD] = q
            qf[h, i, HD:] = query_side
            kf[h, i] = k
            vf[h, i, :HD] = v
            vf[h, i, HD:] = value_side
            kt[h, i] = jnp.concatenate([k, key_side], axis=0).T
            vt[h, i] = jnp.concatenate([v, value_side], axis=0).T
            acc[h, i] = jnp.zeros_like(acc[h, i])
            dk_acc[h, i] = jnp.zeros_like(dk_acc[h, i])
            dv_acc[h, i] = jnp.zeros_like(dv_acc[h, i])
            yield

    load[1].wait()
    together(project, tiles)

    bound = jnp.float32(0.0)
    for h in range(HEADS):
        bound = jnp.maximum(bound, jnp.max(qn[h]) * jnp.max(kn[h]))

    def scores(h, i, j):
        return mm(kt[h, j], qf[h, i])

    @pl.when(jnp.logical_not(bound * SCALE**2 <= LIMIT * LIMIT))
    def _():
        bounds[...] = jnp.full_like(bounds, MASKED)

        def top(t, carry):
            i, j = uq[t], uk[t]
            masked = jnp.where(allowed | (i != j), 0.0, MASKED)
            for h in range(HEADS):
                s = scores(h, i, j) + masked
                bounds[h, i] = jnp.maximum(bounds[h, i], jnp.max(s, axis=0, keepdims=True))
            return carry

        lax.fori_loop(GROUP, units, top, 0)

        def shift(i, carry):
            for h in range(HEADS):
                one, two, three = split3(-bounds[h, i])
                r = lax.broadcasted_iota(jnp.int32, (16, B), 0)
                old = qf[h, i, HD : HD + 16].astype(f32)
                new = jnp.where(r == 8, one, jnp.where(r == 9, two, jnp.where(r == 10, three, old)))
                qf[h, i, HD : HD + 16] = new.astype(bf16)
            return carry

        lax.fori_loop(0, tiles, shift, 0)

    def weigh(t, slot, *kept_too):
        i, j = uq[t], uk[t]
        cut = causal[jnp.where(t >= units, 2, jnp.where(i == j, 1, 0))]
        for h in range(HEADS):
            p = jnp.minimum(jnp.exp2(scores(h, i, j) * SCALE).astype(bf16), cut)
            for ref in (probs.at[slot], *kept_too):
                ref[h] = p

    def forward(p, carry):
        for u in range(GROUP):
            t = GROUP * p + u
            weigh(t, kept(t), turns[u % 2])
            i, j = uq[t - 1], uk[t - 1]
            for h in range(HEADS):
                acc[h, i] += mm(vf[h, j, : HD + 8], turns[1 - u % 2][h])
        return carry

    turns = (turn_a, turn_b)
    for ref in turns:
        ref[...] = jnp.zeros_like(ref)
    lax.fori_loop(1, steps, forward, 0)

    def feed_grads():
        g_down[...] += mm_nt(hidden_s[...], cot_s[...])
        g_up[...] += mm_nt(pre_s[...], second_s[...])
        g_out[...] += mm_nt(heads_s[...], low_s[...])

    def write_tile(p, half, hbm):
        i = SIDE * p + half
        at = pl.ds(pl.multiple_of(i * B, B), B)
        return pltpu.make_async_copy(result.at[at], hbm.at[at], stores.at[i])

    def feed(p, half):
        i = SIDE * p + half
        at = pl.ds(pl.multiple_of(i * B, B), B)
        lanes = slice(half * B, (half + 1) * B)
        if half == 0:
            feed_grads()
        outs, inv = [], []
        for h in range(HEADS):
            r = 1.0 / acc[h, i, HD : HD + 1]
            inv.append(r)
            outs.append(acc[h, i, :HD] * r)
            acc[h, i] = jnp.zeros_like(acc[h, i])
        heads = jnp.concatenate(outs, axis=0).astype(bf16)
        x = tokens[at, :].astype(f32).T
        c32 = cot[at, :].astype(f32).T
        c16 = c32.astype(bf16)
        yield
        resid = x + mm(wout_t[...], heads)
        yield
        n2, rate2 = stats(resid)
        second = (n2 * gain2 + shift2).astype(bf16)
        yield
        heads_s[:, lanes] = heads
        cot_s[:, lanes] = c16
        second_s[:, lanes] = second
        for c in range(0, FF, CHUNK):
            rows = slice(c, c + CHUNK)
            pre = mm(wup_t[rows], second)
            back = mm(wdown_t[rows], c16)
            yield
            cdf = 0.5 * (1.0 + lax.erf(pre * (0.5**0.5)))
            pdf = jnp.exp(-0.5 * pre * pre) * (1.0 / math.sqrt(2.0 * math.pi))
            hidden_s[rows, lanes] = (pre * cdf).astype(bf16)
            pre_s[rows, lanes] = (back * (cdf + pre * pdf)).astype(bf16)
            yield
        second_in = mm(wup[...], pre_s[:, lanes])
        yield
        result[at, :] = (resid + mm(wdown[...], hidden_s[:, lanes])).T.astype(bf16)
        g_norm[2] += lane_fold(second_in * n2)
        g_norm[3] += lane_fold(second_in)
        rg = c32 + norm_back(second_in, n2, rate2, gain2)
        low = rg.astype(bf16)
        yield
        hg = mm(wout[...], low).astype(bf16).astype(f32)
        resid_grad[i] = rg
        low_s[:, lanes] = low
        yield
        r8 = lax.broadcasted_iota(jnp.int32, (16, B), 0)
        for h in range(HEADS):
            do16 = (hg[h * HD : (h + 1) * HD] * inv[h]).astype(bf16)
            do = do16.astype(f32)
            delta = jnp.sum(do * outs[h], axis=0, keepdims=True)
            one, two, three = split3(-delta)
            extra = jnp.where(r8 == 0, one, jnp.where(r8 == 1, two, jnp.where(r8 == 2, three, 0.0)))
            dof[h, i, :HD] = do16
            dof[h, i, HD:] = extra.astype(bf16)
        write_tile(p, half, mixed_hbm).start()

    load[2].wait()
    together(feed, tiles)
    feed_grads()

    def backward(p, carry):
        for u in range(GROUP):
            t = GROUP * p + u
            pl.when(us[t] > CAP)(lambda: weigh(t, us[t]))
        for u in range(GROUP):
            t = GROUP * p + u
            i, j, slot = uq[t], uk[t], us[t]
            for h in range(HEADS):
                w = probs[slot, h]
                pg = mm(vt[h, j], dof[h, i])
                turns[u % 2][h] = (w.astype(f32) * pg).astype(bf16)
                dv_acc[h, j] += mm_nt(dof[h, i, :HD], w)
            i, j = uq[t - 1], uk[t - 1]
            for h in range(HEADS):
                sg = turns[1 - u % 2][h]
                acc[h, i, :HD] += mm(kf[h, j], sg)
                dk_acc[h, j] += mm_nt(qf[h, i, :HD], sg)
        return carry

    for ref in turns:
        ref[...] = jnp.zeros_like(ref)
    lax.fori_loop(1, steps, backward, 0)

    def wait_tile(i, carry):
        at = pl.ds(pl.multiple_of(i * B, B), B)
        pltpu.make_async_copy(result.at[at], mixed_hbm.at[at], stores.at[i]).wait()
        return carry

    lax.fori_loop(0, tiles, wait_tile, 0)

    def finish(p, half):
        i = SIDE * p + half
        at = pl.ds(pl.multiple_of(i * B, B), B)
        lanes = slice(half * B, (half + 1) * B)
        rows = []
        for h in range(HEADS):
            rows += [acc[h, i, :HD] * HD**-0.5, dk_acc[h, i] * HD**-0.5, dv_acc[h, i]]
        packed_grad = jnp.concatenate(rows, axis=0).astype(bf16)
        hidden_s[: 3 * D, lanes] = packed_grad
        yield
        first_in = mm(wqkv[...], packed_grad)
        if half == SIDE - 1:
            g_qkv[...] += mm_nt(hidden_s[: 3 * D, :], first[p])
        x = tokens[at, :].astype(f32).T
        yield
        n1, rate1 = stats(x)
        yield
        g_norm[0] += lane_fold(first_in * n1)
        g_norm[1] += lane_fold(first_in)
        out = resid_grad[i] + norm_back(first_in, n1, rate1, gain1)
        yield
        result[at, :] = out.T.astype(bf16)
        write_tile(p, half, igrad_hbm).start()

    together(finish, tiles)

    lane = lax.broadcasted_iota(jnp.int32, (D, 128), 1)
    norm = jnp.zeros((D, 128), f32)
    for c in range(4):
        norm = jnp.where(lane == c, jnp.sum(g_norm[c], axis=1, keepdims=True), norm)
    gains[...] = norm
    g_stage[...] = jnp.zeros_like(g_stage)
    for h in range(n_head):
        cols = slice(h * 128, (h + 1) * 128)
        qkv = g_qkv[h * 3 * HD : (h + 1) * 3 * HD].T
        up, down = g_up[cols].T, g_down[cols].T
        for d in range(n_dp):
            rows = slice(d * rd, (d + 1) * rd)
            at = (d * n_head + h) * ro
            g_stage[0:rd, : 3 * HD] = qkv[rows]
            g_stage[rd : 2 * rd] = up[rows]
            g_stage[2 * rd : 3 * rd] = down[rows]
            g_stage[3 * rd : 3 * rd + ro] = g_out[at : at + ro]
            g_stage[3 * rd + ro : 3 * rd + 2 * ro] = gains[at : at + ro]
            grads[h, d] = g_stage[...].astype(bf16)
    out = pltpu.make_async_copy(grads, grads_hbm, loads.at[0])
    out.start()

    def wait_last(i, carry):
        at = pl.ds(pl.multiple_of(i * B, B), B)
        pltpu.make_async_copy(result.at[at], igrad_hbm.at[at], stores.at[i]).wait()
        return carry

    lax.fori_loop(0, tiles, wait_last, 0)
    out.wait()


def layer(lengths, weights, tokens, cot, rd, ro):
    n_head, n_dp, rp = weights.shape[:3]
    tiles = tokens.shape[0] // B
    listed = tiles * (MAX_LEN // B + 1) + 3 * GROUP + 2
    vmem = lambda shape, dtype: pltpu.VMEM(shape, dtype)
    scratch = [
        pltpu.SMEM((listed,), jnp.int32),
        pltpu.SMEM((listed,), jnp.int32),
        pltpu.SMEM((listed,), jnp.int32),
        vmem(weights.shape, bf16),
        vmem(tokens.shape, bf16),
        vmem(tokens.shape, bf16),
        vmem(tokens.shape, bf16),
        vmem((n_head, n_dp, rp, 128), bf16),
        pltpu.SemaphoreType.DMA((3,)),
        pltpu.SemaphoreType.DMA((tiles,)),
        vmem((HEADS, tiles, 1, B), f32),
        vmem((HEADS, 3 * HD, D), bf16),
        vmem((D, 3 * D), bf16),
        vmem((D, D), bf16),
        vmem((D, D), bf16),
        vmem((D, FF), bf16),
        vmem((FF, D), bf16),
        vmem((D, FF), bf16),
        vmem((FF, D), bf16),
        vmem((D, 128), f32),
        vmem((n_dp * rp, 128), f32),
        vmem((HEADS, tiles, 48, B), bf16),
        vmem((HEADS, tiles, HD, B), bf16),
        vmem((HEADS, tiles, 48, B), bf16),
        vmem((HEADS, tiles, B, 48), bf16),
        vmem((HEADS, tiles, B, 48), bf16),
        vmem((HEADS, tiles, 48, B), bf16),
        vmem((CAP + 1 + GROUP, HEADS, B, B), bf16),
        vmem((HEADS, B, B), bf16),
        vmem((HEADS, B, B), bf16),
        vmem((HEADS, tiles, HD + 8, B), f32),
        vmem((HEADS, tiles, HD, B), f32),
        vmem((HEADS, tiles, HD, B), f32),
        vmem((tiles, D, B), f32),
        vmem((tiles // SIDE, D, WIDE), bf16),
        vmem((D, WIDE), bf16),
        vmem((D, WIDE), bf16),
        vmem((D, WIDE), bf16),
        vmem((D, WIDE), bf16),
        vmem((FF, WIDE), bf16),
        vmem((FF, WIDE), bf16),
        vmem((3, B, B), bf16),
        vmem((HEADS, 1, B), f32),
        vmem((HEADS, 1, B), f32),
        vmem((3 * D, D), f32),
        vmem((D, D), f32),
        vmem((FF, D), f32),
        vmem((FF, D), f32),
        vmem((4, D, 128), f32),
        vmem((rp, 128), f32),
    ]
    return pl.pallas_call(
        functools.partial(layer_kernel, rd, ro),
        out_shape=(
            jax.ShapeDtypeStruct(tokens.shape, bf16),
            jax.ShapeDtypeStruct(tokens.shape, bf16),
            jax.ShapeDtypeStruct((n_head, n_dp, rp, 128), bf16),
        ),
        in_specs=[pl.BlockSpec(memory_space=pltpu.SMEM), HBM, HBM, HBM],
        out_specs=(HBM, HBM, HBM),
        scratch_shapes=scratch,
        compiler_params=pltpu.CompilerParams(vmem_limit_bytes=63 * 1024 * 1024),
    )(lengths, weights, tokens, cot)


def factors(n_dp, n_head):
    if (n_dp, n_head) == (8, 4):
        return (("head", 2, 2), ("head", 1, 2), ("dp", 2, 4), ("dp", 1, 2)), (2, (0, 3), 1)
    own = 2 if n_dp % 2 == 0 else 1
    far = 4 if n_dp // own % 4 == 0 else 1
    near = n_dp // own // far
    return (("head", 1, n_head), ("dp", own * far, near), ("dp", own, far), ("dp", 1, own)), (2, (0, 1), 3)


def digit(axis, stride, size):
    return lax.rem(lax.div(lax.axis_index(axis), stride), size)


def others(axes, group):
    found = []
    for offsets in itertools.product(*(range(axes[a][2]) for a in group)):
        if not any(offsets):
            continue
        place, theirs, source = {}, {}, {}
        for a, offset in zip(group, offsets):
            axis, stride, size = axes[a]
            mine = digit(*axes[a])
            theirs[a] = lax.rem(mine + offset, size)
            source[a] = lax.rem(mine + size - offset, size)
            place[axis] = place.get(axis, lax.axis_index(axis)) + (theirs[a] - mine) * stride
        found.append((place, theirs, source))
    return found


def greet(peers):
    barrier = pltpu.get_barrier_semaphore()
    for device, _, _ in peers:
        pl.semaphore_signal(barrier, inc=1, device_id=device, device_id_type=MESH)
    return lambda: pl.semaphore_wait(barrier, len(peers))


class Links:
    def __init__(self, send, recv):
        self.send, self.recv, self.count, self.started = send, recv, 0, []

    def copy(self, n, src, dst, place):
        return pltpu.make_async_remote_copy(
            src_ref=src,
            dst_ref=dst,
            send_sem=self.send.at[n],
            recv_sem=self.recv.at[n],
            device_id=place,
            device_id_type=MESH,
        )

    def start(self, src, dst, place, lands):
        n = self.count
        self.count += 1
        out = self.copy(n, src, dst, place)
        out.start()
        self.started.append(out)
        return self.copy(n, lands, lands, place).wait_recv

    def drain(self):
        for out in self.started:
            out.wait_send()


def gather_kernel(axes, roles, *refs):
    masters, w_ref = refs[:5], refs[5]
    held, (stage, block, local, send, recv) = refs[6:11], refs[11:]
    far, near, own = roles
    line, plane, chip = others(axes, (far,)), others(axes, near), others(axes, (own,))
    arrived = greet(line + plane + chip)
    loads = [pltpu.make_async_copy(m, h, local.at[n]) for n, (m, h) in enumerate(zip(masters, held))]
    for load in loads:
        load.start()
    stage[...] = jnp.zeros_like(stage)
    for load in loads:
        load.wait()
    qkv, out, up, down, norm = held
    rd, ro = qkv.shape[0], out.shape[0]
    at = 0
    for part, height in ((qkv, rd), (up, rd), (down, rd), (out, ro), (norm, ro)):
        stage[at : at + height, : part.shape[1]] = part[...]
        at += height
    block[...] = stage[...].astype(bf16)
    mine = {a: digit(*axes[a]) for a in range(4)}
    at = lambda digits: w_ref.at[tuple({**mine, **digits}[a] for a in range(4))]
    keep = pltpu.make_async_copy(block, at({}), local.at[0])
    keep.start()
    arrived()
    links = Links(send, recv)
    first = [links.start(block, at({}), place, at(source)) for place, _, source in line]

    for wait in first:
        wait()
    keep.wait()
    done = {far: slice(None)}
    for group, peers in ((near, plane), ((own,), chip)):
        block = at(done)
        waits = [links.start(block, block, place, at({**done, **source})) for place, _, source in peers]
        for wait in waits:
            wait()
        done.update({a: slice(None) for a in group})
    links.drain()


def gather(axes, roles, rows, masters, cid=0):
    sizes = [size for _, _, size in axes]
    far, near, own = roles
    copies = sizes[far] + math.prod(sizes[a] for a in near) + sizes[own]
    return pl.pallas_call(
        functools.partial(gather_kernel, axes, roles),
        out_shape=jax.ShapeDtypeStruct(tuple(sizes) + (rows, 128), bf16),
        in_specs=[HBM] * 5,
        out_specs=HBM,
        scratch_shapes=[pltpu.VMEM(m.shape, f32) for m in masters]
        + [
            pltpu.VMEM((rows, 128), f32),
            pltpu.VMEM((rows, 128), bf16),
            pltpu.SemaphoreType.DMA((5,)),
            pltpu.SemaphoreType.DMA((copies,)),
            pltpu.SemaphoreType.DMA((copies,)),
        ],
        compiler_params=pltpu.CompilerParams(
            collective_id=cid, has_side_effects=True, vmem_limit_bytes=62 * 1024 * 1024
        ),
    )(*masters)


def scatter_kernel(axes, roles, g_ref, red_ref, sq_ref, *scratch):
    held, from_chip, partial, from_plane, passed, from_line, sq_chip, sq_all, local, send, recv = scratch
    far, near, own = roles
    line, plane, chip = others(axes, (far,)), others(axes, near), others(axes, (own,))
    every = others(axes, tuple(sorted((far,) + near)))
    ready = greet(chip + every)
    mine = {a: digit(*axes[a]) for a in range(4)}
    pick = lambda digits: g_ref.at[tuple(digits.get(a, slice(None)) for a in range(4))]
    pieces = [theirs for _, theirs, _ in line] + [{far: mine[far]}]
    loads = []
    for k, piece in enumerate(pieces):
        loads.append(pltpu.make_async_copy(pick({**piece, own: mine[own]}), held.at[k], local.at[k]))
        loads[-1].start()
    ready()
    links = Links(send, recv)
    first = [
        [
            links.start(pick({**piece, **theirs}), from_chip.at[k, n], place, from_chip.at[k, n])
            for n, (place, theirs, _) in enumerate(chip)
        ]
        for k, piece in enumerate(pieces)
    ]
    second = []
    inner = lambda digits: tuple(digits[a] for a in near)
    for k in range(len(pieces)):
        loads[k].wait()
        total = held[k].astype(f32)
        for n, wait in enumerate(first[k]):
            wait()
            total = total + from_chip[k, n].astype(f32)
        partial[k] = total.astype(bf16)
        second.append(
            [
                links.start(partial.at[(k,) + inner(theirs)], from_plane.at[k, n], place, from_plane.at[k, n])
                for n, (place, theirs, _) in enumerate(plane)
            ]
        )
    third = []
    for k in range(len(pieces)):
        total = partial[(k,) + inner(mine)].astype(f32)
        for n, wait in enumerate(second[k]):
            wait()
            total = total + from_plane[k, n].astype(f32)
        if k < len(line):
            passed[k] = total.astype(bf16)
            third.append(links.start(passed.at[k], from_line.at[k], line[k][0], from_line.at[k]))
    for n, wait in enumerate(third):
        wait()
        total = total + from_line[n].astype(f32)
    red_ref[...] = total
    square = total * total
    fold = square[0:8]
    for r in range(8, square.shape[0], 8):
        fold = fold + square[r : r + 8]
    fold = jnp.sum(fold, axis=0, keepdims=True)
    for group, peers, ref in (((own,), chip, sq_chip), (tuple(sorted((far,) + near)), every, sq_all)):
        at = lambda digits: ref.at[tuple(digits[a] for a in group)]
        ref[tuple(mine[a] for a in group)] = fold
        waits = [links.start(at(mine), at(mine), place, at(source)) for place, _, source in peers]
        for wait in waits:
            wait()
        fold = 0.0
        for index in itertools.product(*(range(axes[a][2]) for a in group)):
            fold = fold + ref[index]
    sq_ref[...] = fold
    links.drain()


def scatter(axes, roles, grads, cid=1):
    sizes = [size for _, _, size in axes]
    far, near, own = roles
    block = grads.shape[-2:]
    spread = tuple(sizes[a] for a in range(4) if a in near) + block
    nf, np_, no = sizes[far], math.prod(sizes[a] for a in near), sizes[own]
    least = lambda n: max(n, 1)
    copies = nf * (no - 1) + nf * (np_ - 1) + (nf - 1) + (no - 1) + (nf * np_ - 1)
    together = tuple(sizes[a] for a in sorted((far,) + near))
    return pl.pallas_call(
        functools.partial(scatter_kernel, axes, roles),
        out_shape=(jax.ShapeDtypeStruct(block, f32), jax.ShapeDtypeStruct((1, 128), f32)),
        in_specs=[HBM],
        out_specs=(WHOLE, WHOLE),
        scratch_shapes=[
            pltpu.VMEM((nf,) + spread, bf16),
            pltpu.VMEM((nf, least(no - 1)) + spread, bf16),
            pltpu.VMEM((nf,) + spread, bf16),
            pltpu.VMEM((nf, least(np_ - 1)) + block, bf16),
            pltpu.VMEM((least(nf - 1),) + block, bf16),
            pltpu.VMEM((least(nf - 1),) + block, bf16),
            pltpu.VMEM((no, 1, 128), f32),
            pltpu.VMEM(together + (1, 128), f32),
            pltpu.SemaphoreType.DMA((nf,)),
            pltpu.SemaphoreType.DMA((copies,)),
            pltpu.SemaphoreType.DMA((copies,)),
        ],
        compiler_params=pltpu.CompilerParams(
            collective_id=cid, has_side_effects=True, vmem_limit_bytes=62 * 1024 * 1024
        ),
    )(grads)


def adam(weight, first, second, grad, factor, rate, decay):
    clipped = grad * factor
    first_new = BETA_ONE * first + (1.0 - BETA_ONE) * clipped
    second_new = BETA_TWO * second + (1.0 - BETA_TWO) * clipped * clipped
    direction = (
        first_new
        / (1.0 - BETA_ONE**STEP)
        / (jnp.sqrt(second_new / (1.0 - BETA_TWO**STEP)) + ADAM_EPS)
    )
    return weight - rate * (direction + decay * weight), first_new, second_new


def update_kernel(*refs):
    held = refs[-18:-1]
    copies = [pltpu.make_async_copy(src, dst, refs[-1].at[n]) for n, (src, dst) in enumerate(zip(refs, held))]
    for copy in copies:
        copy.start()
    for copy in copies:
        copy.wait()
    (red, sq, *params), outs = held, refs[17:-18]
    rd, ro = params[0].shape[0], params[1].shape[0]
    norm = jnp.sqrt(jnp.sum(sq[...], keepdims=True))
    outs[0][...] = norm
    factor = jnp.minimum(1.0, CLIP_NORM / norm)
    rows = (0, 3 * rd, rd, 2 * rd, 3 * rd + ro)
    rates = (0.1, 0.5, 0.1, 0.1, 0.5)
    decays = (DECAY, DECAY, DECAY, DECAY, 0.0)
    for w in range(5):
        height, width = params[w].shape
        grad = red[rows[w] : rows[w] + height, :width]
        new, first_new, second_new = adam(
            params[w][...], params[5 + w][...], params[10 + w][...], grad, factor, rates[w], decays[w]
        )
        outs[1 + 3 * w][...] = new
        outs[2 + 3 * w][...] = first_new
        outs[3 + 3 * w][...] = second_new
        outs[16 + w][...] = grad
        outs[21 + w][...] = new.astype(bf16)


def update(red, sq, params):
    like = lambda p, dtype: jax.ShapeDtypeStruct(p.shape, dtype)
    shapes = [jax.ShapeDtypeStruct((1, 1), f32)]
    shapes += [like(p, f32) for p in params[:5] for _ in range(3)]
    shapes += [like(p, f32) for p in params[:5]]
    shapes += [like(p, bf16) for p in params[:5]]
    return pl.pallas_call(
        update_kernel,
        out_shape=shapes,
        in_specs=[HBM] * 17,
        out_specs=[WHOLE] * len(shapes),
        scratch_shapes=[pltpu.VMEM(a.shape, f32) for a in (red, sq, *params)] + [pltpu.SemaphoreType.DMA((17,))],
        compiler_params=pltpu.CompilerParams(vmem_limit_bytes=62 * 1024 * 1024),
    )(red, sq, *params)


def per_device(n_dp, n_head, tokens, cotangent, lengths, *params):
    masters = params[:5]
    rd, ro = masters[0].shape[0], masters[1].shape[0]
    rows = -(-(3 * rd + 2 * ro) // 16) * 16
    axes, roles = factors(n_dp, n_head)
    weights = gather(axes, roles, rows, masters).reshape(n_head, n_dp, rows, 128)
    mixed, input_grad, grads = layer(lengths, weights, tokens, cotangent, rd, ro)
    grads = grads.reshape(tuple(size for _, _, size in axes) + (rows, 128))
    red, sq = scatter(axes, roles, grads)
    outs = update(red, sq, params)
    return (mixed, input_grad, outs[0].reshape(()), *outs[1:])


def solution(mesh):
    both, split, lens = P(("dp", "head"), None), P("dp", "head"), P("dp", None)
    weight = (split, both, split, split, both)
    return jax.shard_map(
        functools.partial(per_device, mesh.shape["dp"], mesh.shape["head"]),
        mesh=mesh,
        in_specs=(both, both, lens) + weight * 3,
        out_specs=(both, both, P())
        + tuple(spec for spec in weight for _ in range(3))
        + weight
        + weight,
        check_vma=False,
    )
```

```python
import functools
import itertools
import math

import jax
import jax.numpy as jnp
from jax import lax
from jax.experimental import pallas as pl
from jax.experimental.pallas import tpu as pltpu
from jax.sharding import PartitionSpec as P

MAX_LEN = 1024
STEP = 5
NORM_EPS = 1e-05
CLIP_NORM = 0.25
BETA_ONE = 0.5
BETA_TWO = 0.5
ADAM_EPS = 1e-08
DECAY = 0.1
HEADS = 4
HD = 32
D = 128
FF = 512
B = 256
CAP = 46
CHUNK = 128
FGROUP = 8
GROUP = 8
SIDE = 4
WIDE = SIDE * B
BIG = 2.0**100
PDF_SHIFT = math.log2(4.0 / math.sqrt(2.0 * math.pi))
LIMIT = 88.0
MASKED = -1e30
SCALE = HD**-0.5 / math.log(2.0)
f32 = jnp.float32
bf16 = jnp.bfloat16
MESH = pl.DeviceIdType.MESH
HBM = pl.BlockSpec(memory_space=pltpu.HBM)
WHOLE = pl.BlockSpec(memory_space=pltpu.VMEM)


def mm(a, b):
    return lax.dot_general(a, b, (((1,), (0,)), ((), ())), preferred_element_type=f32)


def mm_nt(a, b):
    return lax.dot_general(a, b, (((1,), (1,)), ((), ())), preferred_element_type=f32)


def stats(value):
    mean = jnp.mean(value, axis=0, keepdims=True)
    centred = value - mean
    spread = jnp.mean(centred * centred, axis=0, keepdims=True)
    rate = lax.rsqrt(spread + NORM_EPS)
    return centred * rate, rate


def norm_back(grad, normed, rate, gain):
    scaled = grad * gain
    inner = jnp.mean(scaled, axis=0, keepdims=True)
    along = jnp.mean(scaled * normed, axis=0, keepdims=True)
    return rate * (scaled - inner - normed * along)


def split3(value):
    one = value.astype(bf16).astype(f32)
    two = (value - one).astype(bf16).astype(f32)
    return one, two, value - one - two


def lane_fold(value):
    out = value[:, :128]
    for j in range(1, value.shape[1] // 128):
        out = out + value[:, j * 128 : (j + 1) * 128]
    return out


def together(steps, tiles):
    def pair(p, carry):
        running = [steps(p, half) for half in range(SIDE)]
        while running:
            running = [r for r in running if next(r, "done") != "done"]
        return carry

    lax.fori_loop(0, tiles // SIDE, pair, 0)


def layer_kernel(
    rd,
    ro,
    lengths_hbm,
    w_hbm,
    tokens_hbm,
    cot_hbm,
    mixed_hbm,
    igrad_hbm,
    grads_hbm,
    uq,
    uk,
    us,
    lengths,
    w_ref,
    tokens,
    cot,
    loads,
    stores,
    bounds,
    wqkv_t,
    wqkv,
    wout,
    wout_t,
    wup,
    wup_t,
    wdown,
    wdown_t,
    gains,
    stage,
    qf,
    kf,
    vf,
    kt,
    vt,
    dof,
    probs,
    turn_a,
    turn_b,
    acc,
    dk_acc,
    dv_acc,
    resid_grad,
    first,
    cot_s,
    heads_s,
    second_s,
    low_s,
    hidden_s,
    pre_s,
    causal,
    qn,
    kn,
    g_qkv,
    g_out,
    g_up,
    g_down,
    g_norm,
    g_stage,
):
    n_head, n_dp, rp = w_ref.shape[:3]
    tiles = tokens.shape[0] // B
    row = lax.rem(lax.axis_index("head"), n_head)
    load = [
        pltpu.make_async_copy(src, dst, loads.at[n])
        for n, (src, dst) in enumerate(((w_hbm, w_ref), (tokens_hbm, tokens), (cot_hbm, cot), (lengths_hbm, lengths)))
    ]
    for copy in load[::-1]:
        copy.start()
    load[3].wait()

    starts, ends = [], []
    at = jnp.int32(0)
    for s in range(lengths.shape[1]):
        starts.append(at)
        at = at + lengths[row, s]
        ends.append(at)
    place = lax.broadcasted_iota(jnp.int32, (8, B), 0)
    start_v = jnp.zeros((8, B), jnp.int32)
    end_v = jnp.zeros((8, B), jnp.int32)
    for s in range(8):
        start_v = jnp.where(place == s, starts[s], start_v)
        end_v = jnp.where(place == s, ends[s], end_v)

    def kept(t):
        return jnp.where(t - GROUP < CAP, t - GROUP + 1, CAP + 1 + lax.rem(t, GROUP))

    def blank(t, carry):
        uq[t] = 0
        uk[t] = 0
        us[t] = 0
        return carry

    def list_q(i, n):
        low = jnp.int32(0)
        for s in range(1, 8):
            low = jnp.where(starts[s] <= i * B, starts[s], low)

        def list_k(j, n):
            uq[n] = i
            uk[n] = j
            us[n] = kept(n)
            return n + 1

        return lax.fori_loop(lax.div(low, B), i + 1, list_k, n)

    lax.fori_loop(0, GROUP, blank, 0)
    units = lax.fori_loop(0, tiles, list_q, jnp.int32(GROUP))
    lax.fori_loop(units, units + 2 * GROUP + 4, blank, 0)
    steps = lax.div(units + GROUP - 1, GROUP)

    key_i = lax.broadcasted_iota(jnp.int32, (B, B), 0)
    query_i = lax.broadcasted_iota(jnp.int32, (B, B), 1)
    allowed = key_i <= query_i
    causal[0] = jnp.full((B, B), jnp.inf, bf16)
    causal[1] = jnp.where(allowed, jnp.inf, 0.0).astype(bf16)
    causal[2] = jnp.zeros((B, B), bf16)
    probs[0] = jnp.zeros_like(probs[0])
    for ref in (qn, kn, g_qkv, g_out, g_up, g_down, g_norm, cot_s, heads_s, second_s, low_s, hidden_s, pre_s):
        ref[...] = jnp.zeros_like(ref)

    load[0].wait()
    for h in range(n_head):
        stage[...] = jnp.concatenate([w_ref[h, d].astype(f32) for d in range(n_dp)], axis=0)
        pick = lambda lo, n: jnp.concatenate(
            [stage[d * rp + lo : d * rp + lo + n] for d in range(n_dp)], axis=0
        )
        q = pick(0, rd)
        wqkv_t[h] = q.T[: 3 * HD].astype(bf16)
        wqkv[:, h * 3 * HD : (h + 1) * 3 * HD] = q[:, : 3 * HD].astype(bf16)
        u = pick(rd, rd)
        wup[:, h * 128 : (h + 1) * 128] = u.astype(bf16)
        wup_t[h * 128 : (h + 1) * 128] = (0.5 * u.T).astype(bf16)
        u = pick(2 * rd, rd)
        wdown[:, h * 128 : (h + 1) * 128] = u.astype(bf16)
        wdown_t[h * 128 : (h + 1) * 128] = (0.5 * u.T).astype(bf16)
        for d in range(n_dp):
            at = (d * n_head + h) * ro
            g_out[at : at + ro] = stage[d * rp + 3 * rd : d * rp + 3 * rd + ro]
            gains[at : at + ro] = stage[d * rp + 3 * rd + ro : d * rp + 3 * rd + 2 * ro]
    wo = g_out[...]
    wout[...] = wo.astype(bf16)
    wout_t[...] = wo.T.astype(bf16)
    g_out[...] = jnp.zeros_like(g_out)
    gain1, shift1 = gains[:, 0:1], gains[:, 1:2]
    gain2, shift2 = gains[:, 2:3], gains[:, 3:4]

    def project(p, half):
        i = SIDE * p + half
        x = tokens[pl.ds(pl.multiple_of(i * B, B), B), :].astype(f32).T
        yield
        n1, _ = stats(x)
        f = (n1 * gain1 + shift1).astype(bf16)
        first[p, :, half * B : (half + 1) * B] = f
        yield
        where_t = i * B + lax.broadcasted_iota(jnp.int32, (8, B), 1)
        inside = ((where_t >= start_v) & (where_t < end_v)).astype(f32)
        zeros8 = jnp.zeros((8, B), f32)
        ones8 = jnp.ones((8, B), f32)
        key_side = jnp.concatenate([inside, ones8], axis=0).astype(bf16)
        query_side = jnp.concatenate([(1.0 - inside) * -BIG, zeros8], axis=0).astype(bf16)
        value_side = jnp.concatenate([ones8, zeros8], axis=0).astype(bf16)
        for h in range(HEADS):
            packed = mm(wqkv_t[h], f).astype(bf16)
            yield
            q, k, v = (packed[n * HD : (n + 1) * HD] for n in range(3))
            squares = packed.astype(f32)
            squares = squares * squares
            qn[h] = jnp.maximum(qn[h], jnp.sum(squares[:HD], axis=0, keepdims=True))
            kn[h] = jnp.maximum(kn[h], jnp.sum(squares[HD : 2 * HD], axis=0, keepdims=True))
            qf[h, i, :HD] = q
            qf[h, i, HD:] = query_side
            kf[h, i] = k
            vf[h, i, :HD] = v
            vf[h, i, HD:] = value_side
            kt[h, i] = jnp.concatenate([k, key_side], axis=0).T
            vt[h, i] = jnp.concatenate([v, value_side], axis=0).T
            acc[h, i] = jnp.zeros_like(acc[h, i])
            dk_acc[h, i] = jnp.zeros_like(dk_acc[h, i])
            dv_acc[h, i] = jnp.zeros_like(dv_acc[h, i])
            yield

    load[1].wait()
    together(project, tiles)

    bound = jnp.float32(0.0)
    for h in range(HEADS):
        bound = jnp.maximum(bound, jnp.max(qn[h]) * jnp.max(kn[h]))

    def scores(h, i, j):
        return mm(kt[h, j], qf[h, i])

    @pl.when(jnp.logical_not(bound * SCALE**2 <= LIMIT * LIMIT))
    def _():
        bounds[...] = jnp.full_like(bounds, MASKED)

        def top(t, carry):
            i, j = uq[t], uk[t]
            masked = jnp.where(allowed | (i != j), 0.0, MASKED)
            for h in range(HEADS):
                s = scores(h, i, j) + masked
                bounds[h, i] = jnp.maximum(bounds[h, i], jnp.max(s, axis=0, keepdims=True))
            return carry

        lax.fori_loop(GROUP, units, top, 0)

        def shift(i, carry):
            for h in range(HEADS):
                one, two, three = split3(-bounds[h, i])
                r = lax.broadcasted_iota(jnp.int32, (16, B), 0)
                old = qf[h, i, HD : HD + 16].astype(f32)
                new = jnp.where(r == 8, one, jnp.where(r == 9, two, jnp.where(r == 10, three, old)))
                qf[h, i, HD : HD + 16] = new.astype(bf16)
            return carry

        lax.fori_loop(0, tiles, shift, 0)

    def weigh(t, slot, *kept_too):
        i, j = uq[t], uk[t]
        cut = causal[jnp.where(t >= units, 2, jnp.where(i == j, 1, 0))]
        for h in range(HEADS):
            p = jnp.minimum(jnp.exp2(scores(h, i, j) * SCALE).astype(bf16), cut)
            for ref in (probs.at[slot], *kept_too):
                ref[h] = p

    def weighted(t, block):
        i, j = uq[t], uk[t]
        for h in range(HEADS):
            acc[h, i] += mm(vf[h, j, : HD + 8], block[h])

    def forward(p, carry):
        for u in range(FGROUP):
            t = FGROUP * p + u + (GROUP - FGROUP)
            weigh(t, kept(t), turns[u % 2])
            weighted(t - 1, turns[1 - u % 2])
        return carry

    turns = (turn_a, turn_b)
    turn_b[...] = jnp.zeros_like(turn_b)
    fsteps = lax.div(units - GROUP + FGROUP - 1, FGROUP)
    lax.fori_loop(1, fsteps + 1, forward, 0)
    weighted(FGROUP * fsteps + GROUP - 1, turn_b)

    def feed_grads():
        g_down[...] += mm_nt(hidden_s[...], cot_s[...])
        g_up[...] += mm_nt(pre_s[...], second_s[...])
        g_out[...] += mm_nt(heads_s[...], low_s[...])

    def write_tile(i, result, hbm):
        at = pl.ds(pl.multiple_of(i * B, B), B)
        return pltpu.make_async_copy(result.at[at], hbm.at[at], stores.at[i])

    def wait_tiles(result, hbm):
        def wait_tile(i, carry):
            write_tile(i, result, hbm).wait()
            return carry

        lax.fori_loop(0, tiles, wait_tile, 0)

    def feed(p, half):
        i = SIDE * p + half
        at = pl.ds(pl.multiple_of(i * B, B), B)
        lanes = slice(half * B, (half + 1) * B)
        if half == 0:
            feed_grads()
        outs, inv = [], []
        for h in range(HEADS):
            r = 1.0 / acc[h, i, HD : HD + 1]
            inv.append(r)
            outs.append(acc[h, i, :HD] * r)
            acc[h, i] = jnp.zeros_like(acc[h, i])
        heads = jnp.concatenate(outs, axis=0).astype(bf16)
        x = tokens[at, :].astype(f32).T
        c32 = cot[at, :].astype(f32).T
        c16 = c32.astype(bf16)
        yield
        resid = x + mm(wout_t[...], heads)
        yield
        n2, rate2 = stats(resid)
        second = (n2 * gain2 + shift2).astype(bf16)
        yield
        heads_s[:, lanes] = heads
        cot_s[:, lanes] = c16
        second_s[:, lanes] = second
        for c in range(0, FF, CHUNK):
            rows = slice(c, c + CHUNK)
            half_pre = mm(wup_t[rows], second)
            half_back = mm(wdown_t[rows], c16)
            yield
            twice_cdf = 1.0 + lax.erf(half_pre * 2.0**0.5)
            slope = half_pre * jnp.exp2(half_pre * half_pre * (-2.0 / math.log(2.0)) + PDF_SHIFT)
            hidden_s[rows, lanes] = (half_pre * twice_cdf).astype(bf16)
            pre_s[rows, lanes] = (half_back * (twice_cdf + slope)).astype(bf16)
            yield
        second_in = mm(wup[...], pre_s[:, lanes])
        yield
        cot[at, :] = (resid + mm(wdown[...], hidden_s[:, lanes])).T.astype(bf16)
        g_norm[2] += lane_fold(second_in * n2)
        g_norm[3] += lane_fold(second_in)
        rg = c32 + norm_back(second_in, n2, rate2, gain2)
        low = rg.astype(bf16)
        yield
        hg = mm(wout[...], low).astype(bf16).astype(f32)
        resid_grad[i] = rg
        low_s[:, lanes] = low
        yield
        r8 = lax.broadcasted_iota(jnp.int32, (16, B), 0)
        for h in range(HEADS):
            do16 = (hg[h * HD : (h + 1) * HD] * inv[h]).astype(bf16)
            do = do16.astype(f32)
            delta = jnp.sum(do * outs[h], axis=0, keepdims=True)
            one, two, three = split3(-delta)
            extra = jnp.where(r8 == 0, one, jnp.where(r8 == 1, two, jnp.where(r8 == 2, three, 0.0)))
            dof[h, i, :HD] = do16
            dof[h, i, HD:] = extra.astype(bf16)
        write_tile(i, cot, mixed_hbm).start()

    load[2].wait()
    together(feed, tiles)
    feed_grads()

    def pulled(t, block):
        i, j = uq[t], uk[t]
        for h in range(HEADS):
            acc[h, i, :HD] += mm(kf[h, j], block[h])
            dk_acc[h, j] += mm_nt(qf[h, i, :HD], block[h])

    def backward(p, carry):
        def again(t, carry):
            weigh(t, kept(t))
            return carry

        def all_again():
            lax.fori_loop(jnp.maximum(GROUP * p, CAP + GROUP), jnp.minimum(GROUP * (p + 1), units), again, 0)

        pl.when(GROUP * (p + 1) > CAP + GROUP)(all_again)
        for u in range(GROUP):
            t = GROUP * p + u
            i, j, slot = uq[t], uk[t], us[t]
            for h in range(HEADS):
                w = probs[slot, h]
                pg = mm(vt[h, j], dof[h, i])
                turns[u % 2][h] = (w.astype(f32) * pg).astype(bf16)
                dv_acc[h, j] += mm_nt(dof[h, i, :HD], w)
            pulled(t - 1, turns[1 - u % 2])
        return carry

    turn_b[...] = jnp.zeros_like(turn_b)
    lax.fori_loop(1, steps, backward, 0)
    pulled(GROUP * steps - 1, turn_b)

    wait_tiles(cot, mixed_hbm)

    def finish(p, half):
        i = SIDE * p + half
        at = pl.ds(pl.multiple_of(i * B, B), B)
        lanes = slice(half * B, (half + 1) * B)
        rows = []
        for h in range(HEADS):
            rows += [acc[h, i, :HD] * HD**-0.5, dk_acc[h, i] * HD**-0.5, dv_acc[h, i]]
        packed_grad = jnp.concatenate(rows, axis=0).astype(bf16)
        hidden_s[: 3 * D, lanes] = packed_grad
        yield
        first_in = mm(wqkv[...], packed_grad)
        if half == SIDE - 1:
            g_qkv[...] += mm_nt(hidden_s[: 3 * D, :], first[p])
        x = tokens[at, :].astype(f32).T
        yield
        n1, rate1 = stats(x)
        yield
        g_norm[0] += lane_fold(first_in * n1)
        g_norm[1] += lane_fold(first_in)
        out = resid_grad[i] + norm_back(first_in, n1, rate1, gain1)
        yield
        tokens[at, :] = out.T.astype(bf16)
        write_tile(i, tokens, igrad_hbm).start()

    together(finish, tiles)

    lane = lax.broadcasted_iota(jnp.int32, (D, 128), 1)
    norm = jnp.zeros((D, 128), f32)
    for c in range(4):
        norm = jnp.where(lane == c, jnp.sum(g_norm[c], axis=1, keepdims=True), norm)
    gains[...] = norm
    g_stage[...] = jnp.zeros_like(g_stage)
    for h in range(n_head):
        cols = slice(h * 128, (h + 1) * 128)
        qkv = g_qkv[h * 3 * HD : (h + 1) * 3 * HD].T
        up, down = g_up[cols].T, g_down[cols].T
        for d in range(n_dp):
            rows = slice(d * rd, (d + 1) * rd)
            at = (d * n_head + h) * ro
            g_stage[0:rd, : 3 * HD] = qkv[rows]
            g_stage[rd : 2 * rd] = up[rows]
            g_stage[2 * rd : 3 * rd] = down[rows]
            g_stage[3 * rd : 3 * rd + ro] = g_out[at : at + ro]
            g_stage[3 * rd + ro : 3 * rd + 2 * ro] = gains[at : at + ro]
            w_ref[h, d] = g_stage[...].astype(bf16)
    out = pltpu.make_async_copy(w_ref, grads_hbm, loads.at[0])
    out.start()
    wait_tiles(tokens, igrad_hbm)
    out.wait()


def layer(lengths, weights, tokens, cot, rd, ro):
    n_head, n_dp, rp = weights.shape[:3]
    tiles = tokens.shape[0] // B
    listed = tiles * (MAX_LEN // B + 1) + 3 * GROUP + 8
    vmem = lambda shape, dtype: pltpu.VMEM(shape, dtype)
    scratch = [
        pltpu.SMEM((listed,), jnp.int32),
        pltpu.SMEM((listed,), jnp.int32),
        pltpu.SMEM((listed,), jnp.int32),
        pltpu.SMEM(lengths.shape, jnp.int32),
        vmem(weights.shape, bf16),
        vmem(tokens.shape, bf16),
        vmem(tokens.shape, bf16),
        pltpu.SemaphoreType.DMA((4,)),
        pltpu.SemaphoreType.DMA((tiles,)),
        vmem((HEADS, tiles, 1, B), f32),
        vmem((HEADS, 3 * HD, D), bf16),
        vmem((D, 3 * D), bf16),
        vmem((D, D), bf16),
        vmem((D, D), bf16),
        vmem((D, FF), bf16),
        vmem((FF, D), bf16),
        vmem((D, FF), bf16),
        vmem((FF, D), bf16),
        vmem((D, 128), f32),
        vmem((n_dp * rp, 128), f32),
        vmem((HEADS, tiles, 48, B), bf16),
        vmem((HEADS, tiles, HD, B), bf16),
        vmem((HEADS, tiles, 48, B), bf16),
        vmem((HEADS, tiles, B, 48), bf16),
        vmem((HEADS, tiles, B, 48), bf16),
        vmem((HEADS, tiles, 48, B), bf16),
        vmem((CAP + 1 + GROUP, HEADS, B, B), bf16),
        vmem((HEADS, B, B), bf16),
        vmem((HEADS, B, B), bf16),
        vmem((HEADS, tiles, HD + 8, B), f32),
        vmem((HEADS, tiles, HD, B), f32),
        vmem((HEADS, tiles, HD, B), f32),
        vmem((tiles, D, B), f32),
        vmem((tiles // SIDE, D, WIDE), bf16),
        vmem((D, WIDE), bf16),
        vmem((D, WIDE), bf16),
        vmem((D, WIDE), bf16),
        vmem((D, WIDE), bf16),
        vmem((FF, WIDE), bf16),
        vmem((FF, WIDE), bf16),
        vmem((3, B, B), bf16),
        vmem((HEADS, 1, B), f32),
        vmem((HEADS, 1, B), f32),
        vmem((3 * D, D), f32),
        vmem((D, D), f32),
        vmem((FF, D), f32),
        vmem((FF, D), f32),
        vmem((4, D, 128), f32),
        vmem((rp, 128), f32),
    ]
    return pl.pallas_call(
        functools.partial(layer_kernel, rd, ro),
        out_shape=(
            jax.ShapeDtypeStruct(tokens.shape, bf16),
            jax.ShapeDtypeStruct(tokens.shape, bf16),
            jax.ShapeDtypeStruct((n_head, n_dp, rp, 128), bf16),
        ),
        in_specs=[HBM] * 4,
        out_specs=(HBM, HBM, HBM),
        scratch_shapes=scratch,
        compiler_params=pltpu.CompilerParams(vmem_limit_bytes=63 * 1024 * 1024),
    )(lengths, weights, tokens, cot)


def factors(n_dp, n_head):
    if (n_dp, n_head) == (8, 4):
        return (("head", 2, 2), ("head", 1, 2), ("dp", 2, 4), ("dp", 1, 2)), (2, (0, 3), 1)
    own = 2 if n_dp % 2 == 0 else 1
    far = 4 if n_dp // own % 4 == 0 else 1
    near = n_dp // own // far
    return (("head", 1, n_head), ("dp", own * far, near), ("dp", own, far), ("dp", 1, own)), (2, (0, 1), 3)


def digit(axis, stride, size):
    return lax.rem(lax.div(lax.axis_index(axis), stride), size)


def others(axes, group):
    found = []
    for offsets in itertools.product(*(range(axes[a][2]) for a in group)):
        if not any(offsets):
            continue
        place, theirs, source = {}, {}, {}
        for a, offset in zip(group, offsets):
            axis, stride, size = axes[a]
            mine = digit(*axes[a])
            theirs[a] = lax.rem(mine + offset, size)
            source[a] = lax.rem(mine + size - offset, size)
            place[axis] = place.get(axis, lax.axis_index(axis)) + (theirs[a] - mine) * stride
        found.append((place, theirs, source))
    return found


def greet(peers):
    barrier = pltpu.get_barrier_semaphore()
    for device, _, _ in peers:
        pl.semaphore_signal(barrier, inc=1, device_id=device, device_id_type=MESH)
    return lambda: pl.semaphore_wait(barrier, len(peers))


class Links:
    def __init__(self, send, recv):
        self.send, self.recv, self.count, self.started = send, recv, 0, []

    def copy(self, n, src, dst, place):
        return pltpu.make_async_remote_copy(
            src_ref=src,
            dst_ref=dst,
            send_sem=self.send.at[n],
            recv_sem=self.recv.at[n],
            device_id=place,
            device_id_type=MESH,
        )

    def start(self, src, dst, place, lands):
        n = self.count
        self.count += 1
        out = self.copy(n, src, dst, place)
        out.start()
        self.started.append(out)
        return self.copy(n, lands, lands, place).wait_recv

    def drain(self):
        for out in self.started:
            out.wait_send()


def gather_kernel(axes, roles, *refs):
    masters, w_ref = refs[:5], refs[5]
    held, (stage, block, local, send, recv) = refs[6:11], refs[11:]
    far, near, own = roles
    line, plane, chip = others(axes, (far,)), others(axes, near), others(axes, (own,))
    arrived = greet(line + plane + chip)
    loads = [pltpu.make_async_copy(m, h, local.at[n]) for n, (m, h) in enumerate(zip(masters, held))]
    for load in loads:
        load.start()
    stage[...] = jnp.zeros_like(stage)
    for load in loads:
        load.wait()
    qkv, out, up, down, norm = held
    rd, ro = qkv.shape[0], out.shape[0]
    at = 0
    for part, height in ((qkv, rd), (up, rd), (down, rd), (out, ro), (norm, ro)):
        stage[at : at + height, : part.shape[1]] = part[...]
        at += height
    block[...] = stage[...].astype(bf16)
    mine = {a: digit(*axes[a]) for a in range(4)}
    at = lambda digits: w_ref.at[tuple({**mine, **digits}[a] for a in range(4))]
    keep = pltpu.make_async_copy(block, at({}), local.at[0])
    keep.start()
    arrived()
    links = Links(send, recv)
    first = [links.start(block, at({}), place, at(source)) for place, _, source in line]

    for wait in first:
        wait()
    keep.wait()
    done = {far: slice(None)}
    for group, peers in ((near, plane), ((own,), chip)):
        block = at(done)
        waits = [links.start(block, block, place, at({**done, **source})) for place, _, source in peers]
        for wait in waits:
            wait()
        done.update({a: slice(None) for a in group})
    links.drain()


def gather(axes, roles, rows, masters, cid=0):
    sizes = [size for _, _, size in axes]
    far, near, own = roles
    copies = sizes[far] + math.prod(sizes[a] for a in near) + sizes[own]
    return pl.pallas_call(
        functools.partial(gather_kernel, axes, roles),
        out_shape=jax.ShapeDtypeStruct(tuple(sizes) + (rows, 128), bf16),
        in_specs=[HBM] * 5,
        out_specs=HBM,
        scratch_shapes=[pltpu.VMEM(m.shape, f32) for m in masters]
        + [
            pltpu.VMEM((rows, 128), f32),
            pltpu.VMEM((rows, 128), bf16),
            pltpu.SemaphoreType.DMA((5,)),
            pltpu.SemaphoreType.DMA((copies,)),
            pltpu.SemaphoreType.DMA((copies,)),
        ],
        compiler_params=pltpu.CompilerParams(
            collective_id=cid, has_side_effects=True, vmem_limit_bytes=62 * 1024 * 1024
        ),
    )(*masters)


def scatter_kernel(axes, roles, g_ref, red_ref, sq_ref, *scratch):
    held, from_chip, partial, from_plane, passed, from_line, sq_chip, sq_all, local, send, recv = scratch
    far, near, own = roles
    line, plane, chip = others(axes, (far,)), others(axes, near), others(axes, (own,))
    every = others(axes, tuple(sorted((far,) + near)))
    ready = greet(chip + every)
    mine = {a: digit(*axes[a]) for a in range(4)}
    pick = lambda digits: g_ref.at[tuple(digits.get(a, slice(None)) for a in range(4))]
    pieces = [theirs for _, theirs, _ in line] + [{far: mine[far]}]
    loads = []
    for k, piece in enumerate(pieces):
        loads.append(pltpu.make_async_copy(pick({**piece, own: mine[own]}), held.at[k], local.at[k]))
        loads[-1].start()
    ready()
    links = Links(send, recv)
    first = [
        [
            links.start(pick({**piece, **theirs}), from_chip.at[k, n], place, from_chip.at[k, n])
            for n, (place, theirs, _) in enumerate(chip)
        ]
        for k, piece in enumerate(pieces)
    ]
    second = []
    inner = lambda digits: tuple(digits[a] for a in near)
    for k in range(len(pieces)):
        loads[k].wait()
        total = held[k].astype(f32)
        for n, wait in enumerate(first[k]):
            wait()
            total = total + from_chip[k, n].astype(f32)
        partial[k] = total.astype(bf16)
        second.append(
            [
                links.start(partial.at[(k,) + inner(theirs)], from_plane.at[k, n], place, from_plane.at[k, n])
                for n, (place, theirs, _) in enumerate(plane)
            ]
        )
    third = []
    for k in range(len(pieces)):
        total = partial[(k,) + inner(mine)].astype(f32)
        for n, wait in enumerate(second[k]):
            wait()
            total = total + from_plane[k, n].astype(f32)
        if k < len(line):
            passed[k] = total.astype(bf16)
            third.append(links.start(passed.at[k], from_line.at[k], line[k][0], from_line.at[k]))
    for n, wait in enumerate(third):
        wait()
        total = total + from_line[n].astype(f32)
    red_ref[...] = total
    square = total * total
    fold = square[0:8]
    for r in range(8, square.shape[0], 8):
        fold = fold + square[r : r + 8]
    fold = jnp.sum(fold, axis=0, keepdims=True)
    for group, peers, ref in (((own,), chip, sq_chip), (tuple(sorted((far,) + near)), every, sq_all)):
        at = lambda digits: ref.at[tuple(digits[a] for a in group)]
        ref[tuple(mine[a] for a in group)] = fold
        waits = [links.start(at(mine), at(mine), place, at(source)) for place, _, source in peers]
        for wait in waits:
            wait()
        fold = 0.0
        for index in itertools.product(*(range(axes[a][2]) for a in group)):
            fold = fold + ref[index]
    sq_ref[...] = fold
    links.drain()


def scatter(axes, roles, grads, cid=1):
    sizes = [size for _, _, size in axes]
    far, near, own = roles
    block = grads.shape[-2:]
    spread = tuple(sizes[a] for a in range(4) if a in near) + block
    nf, np_, no = sizes[far], math.prod(sizes[a] for a in near), sizes[own]
    least = lambda n: max(n, 1)
    copies = nf * (no - 1) + nf * (np_ - 1) + (nf - 1) + (no - 1) + (nf * np_ - 1)
    together = tuple(sizes[a] for a in sorted((far,) + near))
    return pl.pallas_call(
        functools.partial(scatter_kernel, axes, roles),
        out_shape=(jax.ShapeDtypeStruct(block, f32), jax.ShapeDtypeStruct((1, 128), f32)),
        in_specs=[HBM],
        out_specs=(WHOLE, WHOLE),
        scratch_shapes=[
            pltpu.VMEM((nf,) + spread, bf16),
            pltpu.VMEM((nf, least(no - 1)) + spread, bf16),
            pltpu.VMEM((nf,) + spread, bf16),
            pltpu.VMEM((nf, least(np_ - 1)) + block, bf16),
            pltpu.VMEM((least(nf - 1),) + block, bf16),
            pltpu.VMEM((least(nf - 1),) + block, bf16),
            pltpu.VMEM((no, 1, 128), f32),
            pltpu.VMEM(together + (1, 128), f32),
            pltpu.SemaphoreType.DMA((nf,)),
            pltpu.SemaphoreType.DMA((copies,)),
            pltpu.SemaphoreType.DMA((copies,)),
        ],
        compiler_params=pltpu.CompilerParams(
            collective_id=cid, has_side_effects=True, vmem_limit_bytes=62 * 1024 * 1024
        ),
    )(grads)


def adam(weight, first, second, grad, factor, rate, decay):
    clipped = grad * factor
    first_new = BETA_ONE * first + (1.0 - BETA_ONE) * clipped
    second_new = BETA_TWO * second + (1.0 - BETA_TWO) * clipped * clipped
    direction = (
        first_new
        / (1.0 - BETA_ONE**STEP)
        / (jnp.sqrt(second_new / (1.0 - BETA_TWO**STEP)) + ADAM_EPS)
    )
    return weight - rate * (direction + decay * weight), first_new, second_new


def update_kernel(*refs):
    held = refs[-18:-1]
    copies = [pltpu.make_async_copy(src, dst, refs[-1].at[n]) for n, (src, dst) in enumerate(zip(refs, held))]
    for copy in copies:
        copy.start()
    for copy in copies:
        copy.wait()
    (red, sq, *params), outs = held, refs[17:-18]
    rd, ro = params[0].shape[0], params[1].shape[0]
    norm = jnp.sqrt(jnp.sum(sq[...], keepdims=True))
    outs[0][...] = norm
    factor = jnp.minimum(1.0, CLIP_NORM / norm)
    rows = (0, 3 * rd, rd, 2 * rd, 3 * rd + ro)
    rates = (0.1, 0.5, 0.1, 0.1, 0.5)
    decays = (DECAY, DECAY, DECAY, DECAY, 0.0)
    for w in range(5):
        height, width = params[w].shape
        grad = red[rows[w] : rows[w] + height, :width]
        new, first_new, second_new = adam(
            params[w][...], params[5 + w][...], params[10 + w][...], grad, factor, rates[w], decays[w]
        )
        outs[1 + 3 * w][...] = new
        outs[2 + 3 * w][...] = first_new
        outs[3 + 3 * w][...] = second_new
        outs[16 + w][...] = grad
        outs[21 + w][...] = new.astype(bf16)


def update(red, sq, params):
    like = lambda p, dtype: jax.ShapeDtypeStruct(p.shape, dtype)
    shapes = [jax.ShapeDtypeStruct((1, 1), f32)]
    shapes += [like(p, f32) for p in params[:5] for _ in range(3)]
    shapes += [like(p, f32) for p in params[:5]]
    shapes += [like(p, bf16) for p in params[:5]]
    return pl.pallas_call(
        update_kernel,
        out_shape=shapes,
        in_specs=[HBM] * 17,
        out_specs=[WHOLE] * len(shapes),
        scratch_shapes=[pltpu.VMEM(a.shape, f32) for a in (red, sq, *params)] + [pltpu.SemaphoreType.DMA((17,))],
        compiler_params=pltpu.CompilerParams(vmem_limit_bytes=62 * 1024 * 1024),
    )(red, sq, *params)


def per_device(n_dp, n_head, tokens, cotangent, lengths, *params):
    masters = params[:5]
    rd, ro = masters[0].shape[0], masters[1].shape[0]
    rows = -(-(3 * rd + 2 * ro) // 16) * 16
    axes, roles = factors(n_dp, n_head)
    weights = gather(axes, roles, rows, masters).reshape(n_head, n_dp, rows, 128)
    mixed, input_grad, grads = layer(lengths, weights, tokens, cotangent, rd, ro)
    grads = grads.reshape(tuple(size for _, _, size in axes) + (rows, 128))
    red, sq = scatter(axes, roles, grads)
    outs = update(red, sq, params)
    return (mixed, input_grad, outs[0].reshape(()), *outs[1:])


def solution(mesh):
    both, split, lens = P(("dp", "head"), None), P("dp", "head"), P("dp", None)
    weight = (split, both, split, split, both)
    return jax.shard_map(
        functools.partial(per_device, mesh.shape["dp"], mesh.shape["head"]),
        mesh=mesh,
        in_specs=(both, both, lens) + weight * 3,
        out_specs=(both, both, P())
        + tuple(spec for spec in weight for _ in range(3))
        + weight
        + weight,
        check_vma=False,
    )
```

```python
import functools
import itertools
import math

import jax
import jax.numpy as jnp
from jax import lax
from jax.experimental import pallas as pl
from jax.experimental.pallas import tpu as pltpu
from jax.sharding import PartitionSpec as P

MAX_LEN = 1024
STEP = 5
NORM_EPS = 1e-05
CLIP_NORM = 0.25
BETA_ONE = 0.5
BETA_TWO = 0.5
ADAM_EPS = 1e-08
DECAY = 0.1
HEADS = 4
HD = 32
D = 128
FF = 512
B = 256
CAP = 48
CHUNK = 128
GROUP = 8
SIDE = 4
WIDE = SIDE * B
BIG = 2.0**100
PDF_SHIFT = math.log2(4.0 / math.sqrt(2.0 * math.pi))
LIMIT = 88.0
MASKED = -1e30
SCALE = HD**-0.5 / math.log(2.0)
f32 = jnp.float32
bf16 = jnp.bfloat16
MESH = pl.DeviceIdType.MESH
HBM = pl.BlockSpec(memory_space=pltpu.HBM)
WHOLE = pl.BlockSpec(memory_space=pltpu.VMEM)


def mm(a, b):
    return lax.dot_general(a, b, (((1,), (0,)), ((), ())), preferred_element_type=f32)


def mm_nt(a, b):
    return lax.dot_general(a, b, (((1,), (1,)), ((), ())), preferred_element_type=f32)


def stats(value):
    mean = jnp.mean(value, axis=0, keepdims=True)
    centred = value - mean
    spread = jnp.mean(centred * centred, axis=0, keepdims=True)
    rate = lax.rsqrt(spread + NORM_EPS)
    return centred * rate, rate


def norm_back(grad, normed, rate, gain):
    scaled = grad * gain
    inner = jnp.mean(scaled, axis=0, keepdims=True)
    along = jnp.mean(scaled * normed, axis=0, keepdims=True)
    return rate * (scaled - inner - normed * along)


def split3(value):
    one = value.astype(bf16).astype(f32)
    two = (value - one).astype(bf16).astype(f32)
    return one, two, value - one - two


def lane_fold(value):
    out = value[:, :128]
    for j in range(1, value.shape[1] // 128):
        out = out + value[:, j * 128 : (j + 1) * 128]
    return out


def together(steps, tiles):
    def pair(p, carry):
        running = [steps(p, half) for half in range(SIDE)]
        while running:
            running = [r for r in running if next(r, "done") != "done"]
        return carry

    lax.fori_loop(0, tiles // SIDE, pair, 0)


def layer_kernel(
    rd,
    ro,
    lengths_hbm,
    w_hbm,
    tokens_hbm,
    cot_hbm,
    mixed_hbm,
    igrad_hbm,
    grads_hbm,
    uq,
    uk,
    lengths,
    w_ref,
    tokens,
    cot,
    loads,
    stores,
    bounds,
    wqkv_t,
    wqkv,
    wout,
    wout_t,
    wup,
    wup_t,
    wdown,
    wdown_t,
    gains,
    stage,
    qf,
    kf,
    vf,
    kt,
    vt,
    dof,
    probs,
    turn_a,
    turn_b,
    acc,
    dk_acc,
    dv_acc,
    resid_grad,
    first,
    cot_s,
    heads_s,
    second_s,
    low_s,
    hidden_s,
    pre_s,
    causal,
    qn,
    kn,
    g_qkv,
    g_out,
    g_up,
    g_down,
    g_norm,
    g_stage,
):
    n_head, n_dp, rp = w_ref.shape[:3]
    tiles = tokens.shape[0] // B
    row = lax.rem(lax.axis_index("head"), n_head)
    load = [
        pltpu.make_async_copy(src, dst, loads.at[n])
        for n, (src, dst) in enumerate(((lengths_hbm, lengths), (w_hbm, w_ref), (tokens_hbm, tokens), (cot_hbm, cot)))
    ]
    for copy in load:
        copy.start()
    load[0].wait()

    starts, ends = [], []
    at = jnp.int32(0)
    for s in range(lengths.shape[1]):
        starts.append(at)
        at = at + lengths[row, s]
        ends.append(at)
    place = lax.broadcasted_iota(jnp.int32, (8, B), 0)
    start_v = jnp.zeros((8, B), jnp.int32)
    end_v = jnp.zeros((8, B), jnp.int32)
    for s in range(8):
        start_v = jnp.where(place == s, starts[s], start_v)
        end_v = jnp.where(place == s, ends[s], end_v)

    def blank(t, carry):
        uq[t] = 0
        uk[t] = 0
        return carry

    def list_q(i, n):
        low = jnp.int32(0)
        for s in range(1, 8):
            low = jnp.where(starts[s] <= i * B, starts[s], low)

        def list_k(j, n):
            uq[n] = i
            uk[n] = j
            return n + 1

        return lax.fori_loop(lax.div(low, B), i + 1, list_k, n)

    blank(0, 0)
    units = lax.fori_loop(0, tiles, list_q, jnp.int32(1))
    lax.fori_loop(units, units + GROUP, blank, 0)
    steps = lax.div(jnp.minimum(units - 1, CAP) + GROUP - 1, GROUP)

    key_i = lax.broadcasted_iota(jnp.int32, (B, B), 0)
    query_i = lax.broadcasted_iota(jnp.int32, (B, B), 1)
    allowed = key_i <= query_i
    causal[0] = jnp.full((B, B), jnp.inf, bf16)
    causal[1] = jnp.where(allowed, jnp.inf, 0.0).astype(bf16)
    causal[2] = jnp.zeros((B, B), bf16)
    for ref in (qn, kn, g_qkv, g_out, g_up, g_down, g_norm, cot_s, heads_s, second_s, low_s, hidden_s, pre_s):
        ref[...] = jnp.zeros_like(ref)

    load[1].wait()
    for h in range(n_head):
        stage[...] = jnp.concatenate([w_ref[h, d].astype(f32) for d in range(n_dp)], axis=0)
        pick = lambda lo, n: jnp.concatenate(
            [stage[d * rp + lo : d * rp + lo + n] for d in range(n_dp)], axis=0
        )
        q = pick(0, rd)
        wqkv_t[h] = q.T[: 3 * HD].astype(bf16)
        wqkv[:, h * 3 * HD : (h + 1) * 3 * HD] = q[:, : 3 * HD].astype(bf16)
        u = pick(rd, rd)
        wup[:, h * 128 : (h + 1) * 128] = u.astype(bf16)
        wup_t[h * 128 : (h + 1) * 128] = (0.5 * u.T).astype(bf16)
        u = pick(2 * rd, rd)
        wdown[:, h * 128 : (h + 1) * 128] = u.astype(bf16)
        wdown_t[h * 128 : (h + 1) * 128] = (0.5 * u.T).astype(bf16)
        for d in range(n_dp):
            at = (d * n_head + h) * ro
            g_out[at : at + ro] = stage[d * rp + 3 * rd : d * rp + 3 * rd + ro]
            gains[at : at + ro] = stage[d * rp + 3 * rd + ro : d * rp + 3 * rd + 2 * ro]
    wo = g_out[...]
    wout[...] = wo.astype(bf16)
    wout_t[...] = wo.T.astype(bf16)
    g_out[...] = jnp.zeros_like(g_out)
    gain1, shift1 = gains[:, 0:1], gains[:, 1:2]
    gain2, shift2 = gains[:, 2:3], gains[:, 3:4]

    def project(p, half):
        i = SIDE * p + half
        x = tokens[pl.ds(pl.multiple_of(i * B, B), B), :].T.astype(f32)
        yield
        n1, _ = stats(x)
        f = (n1 * gain1 + shift1).astype(bf16)
        first[p, :, half * B : (half + 1) * B] = f
        yield
        where_t = i * B + lax.broadcasted_iota(jnp.int32, (8, B), 1)
        inside = ((where_t >= start_v) & (where_t < end_v)).astype(f32)
        zeros8 = jnp.zeros((8, B), f32)
        ones8 = jnp.ones((8, B), f32)
        key_side = jnp.concatenate([inside, ones8], axis=0).astype(bf16)
        query_side = jnp.concatenate([(1.0 - inside) * -BIG, zeros8], axis=0).astype(bf16)
        value_side = jnp.concatenate([ones8, zeros8], axis=0).astype(bf16)
        for h in range(HEADS):
            packed = mm(wqkv_t[h], f).astype(bf16)
            yield
            q, k, v = (packed[n * HD : (n + 1) * HD] for n in range(3))
            squares = packed.astype(f32)
            squares = squares * squares
            qn[h] = jnp.maximum(qn[h], jnp.sum(squares[:HD], axis=0, keepdims=True))
            kn[h] = jnp.maximum(kn[h], jnp.sum(squares[HD : 2 * HD], axis=0, keepdims=True))
            qf[h, i, :HD] = q
            qf[h, i, HD:] = query_side
            kf[h, i] = k
            vf[h, i, :HD] = v
            vf[h, i, HD:] = value_side
            kt[h, i] = jnp.concatenate([k, key_side], axis=0).T
            vt[h, i] = jnp.concatenate([v, value_side], axis=0).T
            acc[h, i] = jnp.zeros_like(acc[h, i])
            dk_acc[h, i] = jnp.zeros_like(dk_acc[h, i])
            dv_acc[h, i] = jnp.zeros_like(dv_acc[h, i])
            yield

    load[2].wait()
    together(project, tiles)

    bound = jnp.float32(0.0)
    for h in range(HEADS):
        bound = jnp.maximum(bound, jnp.max(qn[h]) * jnp.max(kn[h]))

    def scores(h, i, j):
        return mm(kt[h, j], qf[h, i])

    @pl.when(jnp.logical_not(bound * SCALE**2 <= LIMIT * LIMIT))
    def _():
        bounds[...] = jnp.full_like(bounds, MASKED)

        def top(t, carry):
            i, j = uq[t], uk[t]
            masked = jnp.where(allowed | (i != j), 0.0, MASKED)
            for h in range(HEADS):
                s = scores(h, i, j) + masked
                bounds[h, i] = jnp.maximum(bounds[h, i], jnp.max(s, axis=0, keepdims=True))
            return carry

        lax.fori_loop(1, units, top, 0)

        def shift(i, carry):
            for h in range(HEADS):
                one, two, three = split3(-bounds[h, i])
                r = lax.broadcasted_iota(jnp.int32, (16, B), 0)
                old = qf[h, i, HD : HD + 16].astype(f32)
                new = jnp.where(r == 8, one, jnp.where(r == 9, two, jnp.where(r == 10, three, old)))
                qf[h, i, HD : HD + 16] = new.astype(bf16)
            return carry

        lax.fori_loop(0, tiles, shift, 0)

    def weigh(t, slot, *kept_too):
        i, j = uq[t], uk[t]
        cut = causal[jnp.where(t >= units, 2, jnp.where(i == j, 1, 0))]
        for h in range(HEADS):
            p = jnp.minimum(jnp.exp2(scores(h, i, j) * SCALE).astype(bf16), cut)
            for ref in (probs.at[slot], *kept_too):
                ref[h] = p

    def weighted(t, block):
        i, j = uq[t], uk[t]
        for h in range(HEADS):
            acc[h, i] += mm(vf[h, j, : HD + 8], block[h])

    def forward(p, carry):
        for u in range(GROUP):
            t = GROUP * p + 1 + u
            weigh(t, t - 1, turns[u % 2])
            weighted(t - 1, turns[1 - u % 2])
        return carry

    def forward_rest(t, carry):
        weigh(t, CAP)
        weighted(t, probs.at[CAP])
        return carry

    turns = (turn_a, turn_b)
    turn_b[...] = jnp.zeros_like(turn_b)
    lax.fori_loop(0, steps, forward, 0)
    weighted(GROUP * steps, turn_b)
    lax.fori_loop(CAP + 1, units, forward_rest, 0)

    def feed_grads():
        g_down[...] += mm_nt(hidden_s[...], cot_s[...])
        g_up[...] += mm_nt(pre_s[...], second_s[...])
        g_out[...] += mm_nt(heads_s[...], low_s[...])

    def write_tile(i, result, hbm):
        at = pl.ds(pl.multiple_of(i * B, B), B)
        return pltpu.make_async_copy(result.at[at], hbm.at[at], stores.at[i])

    def wait_tiles(result, hbm):
        def wait_tile(i, carry):
            write_tile(i, result, hbm).wait()
            return carry

        lax.fori_loop(0, tiles, wait_tile, 0)

    def feed(p, half):
        i = SIDE * p + half
        at = pl.ds(pl.multiple_of(i * B, B), B)
        lanes = slice(half * B, (half + 1) * B)
        if half == 0:
            feed_grads()
        outs, inv = [], []
        for h in range(HEADS):
            r = 1.0 / acc[h, i, HD : HD + 1]
            inv.append(r)
            outs.append(acc[h, i, :HD] * r)
            acc[h, i] = jnp.zeros_like(acc[h, i])
        heads = jnp.concatenate(outs, axis=0).astype(bf16)
        x = tokens[at, :].T.astype(f32)
        c16 = cot[at, :].T
        c32 = c16.astype(f32)
        yield
        resid = x + mm(wout_t[...], heads)
        yield
        n2, rate2 = stats(resid)
        second = (n2 * gain2 + shift2).astype(bf16)
        yield
        heads_s[:, lanes] = heads
        cot_s[:, lanes] = c16
        second_s[:, lanes] = second
        for c in range(0, FF, CHUNK):
            rows = slice(c, c + CHUNK)
            half_pre = mm(wup_t[rows], second)
            half_back = mm(wdown_t[rows], c16)
            yield
            twice_cdf = 1.0 + lax.erf(half_pre * 2.0**0.5)
            slope = half_pre * jnp.exp2(half_pre * half_pre * (-2.0 / math.log(2.0)) + PDF_SHIFT)
            hidden_s[rows, lanes] = (half_pre * twice_cdf).astype(bf16)
            pre_s[rows, lanes] = (half_back * (twice_cdf + slope)).astype(bf16)
            yield
        second_in = mm(wup[...], pre_s[:, lanes])
        yield
        cot[at, :] = (resid + mm(wdown[...], hidden_s[:, lanes])).astype(bf16).T
        g_norm[2] += lane_fold(second_in * n2)
        g_norm[3] += lane_fold(second_in)
        rg = c32 + norm_back(second_in, n2, rate2, gain2)
        low = rg.astype(bf16)
        yield
        hg = mm(wout[...], low).astype(bf16).astype(f32)
        resid_grad[i] = rg
        low_s[:, lanes] = low
        yield
        r8 = lax.broadcasted_iota(jnp.int32, (16, B), 0)
        for h in range(HEADS):
            do16 = (hg[h * HD : (h + 1) * HD] * inv[h]).astype(bf16)
            do = do16.astype(f32)
            delta = jnp.sum(do * outs[h], axis=0, keepdims=True)
            one, two, three = split3(-delta)
            extra = jnp.where(r8 == 0, one, jnp.where(r8 == 1, two, jnp.where(r8 == 2, three, 0.0)))
            dof[h, i, :HD] = do16
            dof[h, i, HD:] = extra.astype(bf16)
        write_tile(i, cot, mixed_hbm).start()

    load[3].wait()
    together(feed, tiles)
    feed_grads()

    def pushed(t, slot, block):
        i, j = uq[t], uk[t]
        for h in range(HEADS):
            w = probs[slot, h]
            pg = mm(vt[h, j], dof[h, i])
            block[h] = (w.astype(f32) * pg).astype(bf16)
            dv_acc[h, j] += mm_nt(dof[h, i, :HD], w)

    def pulled(t, block):
        i, j = uq[t], uk[t]
        for h in range(HEADS):
            acc[h, i, :HD] += mm(kf[h, j], block[h])
            dk_acc[h, j] += mm_nt(qf[h, i, :HD], block[h])

    def backward(p, carry):
        for u in range(GROUP):
            t = GROUP * p + 1 + u
            pushed(t, t - 1, turns[u % 2])
            pulled(t - 1, turns[1 - u % 2])
        return carry

    def backward_rest(t, carry):
        weigh(t, CAP)
        pushed(t, CAP, turn_a)
        pulled(t, turn_a)
        return carry

    turn_b[...] = jnp.zeros_like(turn_b)
    lax.fori_loop(0, steps, backward, 0)
    pulled(GROUP * steps, turn_b)
    lax.fori_loop(CAP + 1, units, backward_rest, 0)

    wait_tiles(cot, mixed_hbm)

    def finish(p, half):
        i = SIDE * p + half
        at = pl.ds(pl.multiple_of(i * B, B), B)
        lanes = slice(half * B, (half + 1) * B)
        rows = []
        for h in range(HEADS):
            rows += [acc[h, i, :HD] * HD**-0.5, dk_acc[h, i] * HD**-0.5, dv_acc[h, i]]
        packed_grad = jnp.concatenate(rows, axis=0).astype(bf16)
        hidden_s[: 3 * D, lanes] = packed_grad
        yield
        first_in = mm(wqkv[...], packed_grad)
        if half == SIDE - 1:
            g_qkv[...] += mm_nt(hidden_s[: 3 * D, :], first[p])
        x = tokens[at, :].T.astype(f32)
        yield
        n1, rate1 = stats(x)
        yield
        g_norm[0] += lane_fold(first_in * n1)
        g_norm[1] += lane_fold(first_in)
        out = resid_grad[i] + norm_back(first_in, n1, rate1, gain1)
        yield
        tokens[at, :] = out.astype(bf16).T
        write_tile(i, tokens, igrad_hbm).start()

    together(finish, tiles)

    lane = lax.broadcasted_iota(jnp.int32, (D, 128), 1)
    norm = jnp.zeros((D, 128), f32)
    for c in range(4):
        norm = jnp.where(lane == c, jnp.sum(g_norm[c], axis=1, keepdims=True), norm)
    gains[...] = norm
    g_stage[...] = jnp.zeros_like(g_stage)
    for h in range(n_head):
        cols = slice(h * 128, (h + 1) * 128)
        qkv = g_qkv[h * 3 * HD : (h + 1) * 3 * HD].T
        up, down = g_up[cols].T, g_down[cols].T
        for d in range(n_dp):
            rows = slice(d * rd, (d + 1) * rd)
            at = (d * n_head + h) * ro
            g_stage[0:rd, : 3 * HD] = qkv[rows]
            g_stage[rd : 2 * rd] = up[rows]
            g_stage[2 * rd : 3 * rd] = down[rows]
            g_stage[3 * rd : 3 * rd + ro] = g_out[at : at + ro]
            g_stage[3 * rd + ro : 3 * rd + 2 * ro] = gains[at : at + ro]
            w_ref[h, d] = g_stage[...].astype(bf16)
    out = pltpu.make_async_copy(w_ref, grads_hbm, loads.at[0])
    out.start()
    wait_tiles(tokens, igrad_hbm)
    out.wait()


def layer(lengths, weights, tokens, cot, rd, ro):
    n_head, n_dp, rp = weights.shape[:3]
    tiles = tokens.shape[0] // B
    listed = tiles * (MAX_LEN // B + 1) + GROUP + 1
    vmem = lambda shape, dtype: pltpu.VMEM(shape, dtype)
    scratch = [
        pltpu.SMEM((listed,), jnp.int32),
        pltpu.SMEM((listed,), jnp.int32),
        pltpu.SMEM(lengths.shape, jnp.int32),
        vmem(weights.shape, bf16),
        vmem(tokens.shape, bf16),
        vmem(tokens.shape, bf16),
        pltpu.SemaphoreType.DMA((4,)),
        pltpu.SemaphoreType.DMA((tiles,)),
        vmem((HEADS, tiles, 1, B), f32),
        vmem((HEADS, 3 * HD, D), bf16),
        vmem((D, 3 * D), bf16),
        vmem((D, D), bf16),
        vmem((D, D), bf16),
        vmem((D, FF), bf16),
        vmem((FF, D), bf16),
        vmem((D, FF), bf16),
        vmem((FF, D), bf16),
        vmem((D, 128), f32),
        vmem((n_dp * rp, 128), f32),
        vmem((HEADS, tiles, 48, B), bf16),
        vmem((HEADS, tiles, HD, B), bf16),
        vmem((HEADS, tiles, 48, B), bf16),
        vmem((HEADS, tiles, B, 48), bf16),
        vmem((HEADS, tiles, B, 48), bf16),
        vmem((HEADS, tiles, 48, B), bf16),
        vmem((CAP + 1, HEADS, B, B), bf16),
        vmem((HEADS, B, B), bf16),
        vmem((HEADS, B, B), bf16),
        vmem((HEADS, tiles, HD + 8, B), f32),
        vmem((HEADS, tiles, HD, B), f32),
        vmem((HEADS, tiles, HD, B), f32),
        vmem((tiles, D, B), f32),
        vmem((tiles // SIDE, D, WIDE), bf16),
        vmem((D, WIDE), bf16),
        vmem((D, WIDE), bf16),
        vmem((D, WIDE), bf16),
        vmem((D, WIDE), bf16),
        vmem((FF, WIDE), bf16),
        vmem((FF, WIDE), bf16),
        vmem((3, B, B), bf16),
        vmem((HEADS, 1, B), f32),
        vmem((HEADS, 1, B), f32),
        vmem((3 * D, D), f32),
        vmem((D, D), f32),
        vmem((FF, D), f32),
        vmem((FF, D), f32),
        vmem((4, D, 128), f32),
        vmem((rp, 128), f32),
    ]
    return pl.pallas_call(
        functools.partial(layer_kernel, rd, ro),
        out_shape=(
            jax.ShapeDtypeStruct(tokens.shape, bf16),
            jax.ShapeDtypeStruct(tokens.shape, bf16),
            jax.ShapeDtypeStruct((n_head, n_dp, rp, 128), bf16),
        ),
        in_specs=[HBM] * 4,
        out_specs=(HBM, HBM, HBM),
        scratch_shapes=scratch,
        compiler_params=pltpu.CompilerParams(vmem_limit_bytes=63 * 1024 * 1024),
    )(lengths, weights, tokens, cot)


def factors(n_dp, n_head):
    if (n_dp, n_head) == (8, 4):
        return (("head", 2, 2), ("head", 1, 2), ("dp", 2, 4), ("dp", 1, 2)), (2, (0, 3), 1)
    own = 2 if n_dp % 2 == 0 else 1
    far = 4 if n_dp // own % 4 == 0 else 1
    near = n_dp // own // far
    return (("head", 1, n_head), ("dp", own * far, near), ("dp", own, far), ("dp", 1, own)), (2, (0, 1), 3)


def digit(axis, stride, size):
    return lax.rem(lax.div(lax.axis_index(axis), stride), size)


def others(axes, group):
    found = []
    for offsets in itertools.product(*(range(axes[a][2]) for a in group)):
        if not any(offsets):
            continue
        place, theirs, source = {}, {}, {}
        for a, offset in zip(group, offsets):
            axis, stride, size = axes[a]
            mine = digit(*axes[a])
            theirs[a] = lax.rem(mine + offset, size)
            source[a] = lax.rem(mine + size - offset, size)
            place[axis] = place.get(axis, lax.axis_index(axis)) + (theirs[a] - mine) * stride
        found.append((place, theirs, source))
    return found


def greet(peers):
    barrier = pltpu.get_barrier_semaphore()
    for device, _, _ in peers:
        pl.semaphore_signal(barrier, inc=1, device_id=device, device_id_type=MESH)
    return lambda: pl.semaphore_wait(barrier, len(peers))


class Links:
    def __init__(self, send, recv):
        self.send, self.recv, self.count, self.started = send, recv, 0, []

    def copy(self, n, src, dst, place):
        return pltpu.make_async_remote_copy(
            src_ref=src,
            dst_ref=dst,
            send_sem=self.send.at[n],
            recv_sem=self.recv.at[n],
            device_id=place,
            device_id_type=MESH,
        )

    def start(self, src, dst, place, lands):
        n = self.count
        self.count += 1
        out = self.copy(n, src, dst, place)
        out.start()
        self.started.append(out)
        return self.copy(n, lands, lands, place).wait_recv

    def drain(self):
        for out in self.started:
            out.wait_send()


def gather_kernel(axes, roles, *refs):
    masters, w_ref = refs[:5], refs[5]
    held, (stage, block, local, send, recv) = refs[6:11], refs[11:]
    far, near, own = roles
    line, plane, chip = others(axes, (far,)), others(axes, near), others(axes, (own,))
    arrived = greet(line + plane + chip)
    loads = [pltpu.make_async_copy(m, h, local.at[n]) for n, (m, h) in enumerate(zip(masters, held))]
    for load in loads:
        load.start()
    stage[...] = jnp.zeros_like(stage)
    for load in loads:
        load.wait()
    qkv, out, up, down, norm = held
    rd, ro = qkv.shape[0], out.shape[0]
    at = 0
    for part, height in ((qkv, rd), (up, rd), (down, rd), (out, ro), (norm, ro)):
        stage[at : at + height, : part.shape[1]] = part[...]
        at += height
    block[...] = stage[...].astype(bf16)
    mine = {a: digit(*axes[a]) for a in range(4)}
    at = lambda digits: w_ref.at[tuple({**mine, **digits}[a] for a in range(4))]
    keep = pltpu.make_async_copy(block, at({}), local.at[0])
    keep.start()
    arrived()
    links = Links(send, recv)
    first = [links.start(block, at({}), place, at(source)) for place, _, source in line]

    def onward(src, digits):
        dst = at(digits)
        waits = [
            (links.start(src, dst, place, at({**digits, **source})), {**digits, **source})
            for place, _, source in plane
        ]
        return waits, [links.start(src, dst, place, at({**digits, **source})) for place, _, source in chip]

    second, third = onward(block, {})
    for wait, (_, _, source) in zip(first, line):
        wait()
        waits, more = onward(at(source), source)
        second += waits
        third += more
    for wait, digits in second:
        wait()
        third += [
            links.start(at(digits), at(digits), place, at({**digits, **source})) for place, _, source in chip
        ]
    for wait in third:
        wait()
    links.drain()
    keep.wait()


def gather(axes, roles, rows, masters, cid=0):
    sizes = [size for _, _, size in axes]
    copies = math.prod(sizes)
    return pl.pallas_call(
        functools.partial(gather_kernel, axes, roles),
        out_shape=jax.ShapeDtypeStruct(tuple(sizes) + (rows, 128), bf16),
        in_specs=[HBM] * 5,
        out_specs=HBM,
        scratch_shapes=[pltpu.VMEM(m.shape, f32) for m in masters]
        + [
            pltpu.VMEM((rows, 128), f32),
            pltpu.VMEM((rows, 128), bf16),
            pltpu.SemaphoreType.DMA((5,)),
            pltpu.SemaphoreType.DMA((copies,)),
            pltpu.SemaphoreType.DMA((copies,)),
        ],
        compiler_params=pltpu.CompilerParams(
            collective_id=cid, has_side_effects=True, vmem_limit_bytes=62 * 1024 * 1024
        ),
    )(*masters)


def scatter_kernel(axes, roles, g_ref, red_ref, sq_ref, *scratch):
    held, from_chip, partial, from_plane, passed, from_line, sq_chip, sq_all, local, send, recv = scratch
    far, near, own = roles
    line, plane, chip = others(axes, (far,)), others(axes, near), others(axes, (own,))
    every = others(axes, tuple(sorted((far,) + near)))
    ready = greet(chip + every)
    mine = {a: digit(*axes[a]) for a in range(4)}
    pick = lambda digits: g_ref.at[tuple(digits.get(a, slice(None)) for a in range(4))]
    pieces = [theirs for _, theirs, _ in line] + [{far: mine[far]}]
    loads = []
    for k, piece in enumerate(pieces):
        loads.append(pltpu.make_async_copy(pick({**piece, own: mine[own]}), held.at[k], local.at[k]))
        loads[-1].start()
    ready()
    links = Links(send, recv)
    first = [
        [
            links.start(pick({**piece, **theirs}), from_chip.at[k, n], place, from_chip.at[k, n])
            for n, (place, theirs, _) in enumerate(chip)
        ]
        for k, piece in enumerate(pieces)
    ]
    second = []
    inner = lambda digits: tuple(digits[a] for a in near)
    for k in range(len(pieces)):
        loads[k].wait()
        total = held[k].astype(f32)
        for n, wait in enumerate(first[k]):
            wait()
            total = total + from_chip[k, n].astype(f32)
        partial[k] = total.astype(bf16)
        second.append(
            [
                links.start(partial.at[(k,) + inner(theirs)], from_plane.at[k, n], place, from_plane.at[k, n])
                for n, (place, theirs, _) in enumerate(plane)
            ]
        )
    third = []
    for k in range(len(pieces)):
        total = partial[(k,) + inner(mine)].astype(f32)
        for n, wait in enumerate(second[k]):
            wait()
            total = total + from_plane[k, n].astype(f32)
        if k < len(line):
            passed[k] = total.astype(bf16)
            third.append(links.start(passed.at[k], from_line.at[k], line[k][0], from_line.at[k]))
    for n, wait in enumerate(third):
        wait()
        total = total + from_line[n].astype(f32)
    red_ref[...] = total
    square = total * total
    fold = square[0:8]
    for r in range(8, square.shape[0], 8):
        fold = fold + square[r : r + 8]
    fold = jnp.sum(fold, axis=0, keepdims=True)
    for group, peers, ref in (((own,), chip, sq_chip), (tuple(sorted((far,) + near)), every, sq_all)):
        at = lambda digits: ref.at[tuple(digits[a] for a in group)]
        ref[tuple(mine[a] for a in group)] = fold
        waits = [links.start(at(mine), at(mine), place, at(source)) for place, _, source in peers]
        for wait in waits:
            wait()
        fold = 0.0
        for index in itertools.product(*(range(axes[a][2]) for a in group)):
            fold = fold + ref[index]
    sq_ref[...] = fold
    links.drain()


def scatter(axes, roles, grads, cid=1):
    sizes = [size for _, _, size in axes]
    far, near, own = roles
    block = grads.shape[-2:]
    spread = tuple(sizes[a] for a in range(4) if a in near) + block
    nf, np_, no = sizes[far], math.prod(sizes[a] for a in near), sizes[own]
    least = lambda n: max(n, 1)
    copies = nf * (no - 1) + nf * (np_ - 1) + (nf - 1) + (no - 1) + (nf * np_ - 1)
    together = tuple(sizes[a] for a in sorted((far,) + near))
    return pl.pallas_call(
        functools.partial(scatter_kernel, axes, roles),
        out_shape=(jax.ShapeDtypeStruct(block, f32), jax.ShapeDtypeStruct((1, 128), f32)),
        in_specs=[HBM],
        out_specs=(WHOLE, WHOLE),
        scratch_shapes=[
            pltpu.VMEM((nf,) + spread, bf16),
            pltpu.VMEM((nf, least(no - 1)) + spread, bf16),
            pltpu.VMEM((nf,) + spread, bf16),
            pltpu.VMEM((nf, least(np_ - 1)) + block, bf16),
            pltpu.VMEM((least(nf - 1),) + block, bf16),
            pltpu.VMEM((least(nf - 1),) + block, bf16),
            pltpu.VMEM((no, 1, 128), f32),
            pltpu.VMEM(together + (1, 128), f32),
            pltpu.SemaphoreType.DMA((nf,)),
            pltpu.SemaphoreType.DMA((copies,)),
            pltpu.SemaphoreType.DMA((copies,)),
        ],
        compiler_params=pltpu.CompilerParams(
            collective_id=cid, has_side_effects=True, vmem_limit_bytes=62 * 1024 * 1024
        ),
    )(grads)


def adam(weight, first, second, grad, factor, rate, decay):
    clipped = grad * factor
    first_new = BETA_ONE * first + (1.0 - BETA_ONE) * clipped
    second_new = BETA_TWO * second + (1.0 - BETA_TWO) * clipped * clipped
    direction = (
        first_new
        / (1.0 - BETA_ONE**STEP)
        / (jnp.sqrt(second_new / (1.0 - BETA_TWO**STEP)) + ADAM_EPS)
    )
    return weight - rate * (direction + decay * weight), first_new, second_new


def update_kernel(*refs):
    held = refs[-18:-1]
    copies = [pltpu.make_async_copy(src, dst, refs[-1].at[n]) for n, (src, dst) in enumerate(zip(refs, held))]
    for copy in copies:
        copy.start()
    for copy in copies:
        copy.wait()
    (red, sq, *params), outs = held, refs[17:-18]
    rd, ro = params[0].shape[0], params[1].shape[0]
    norm = jnp.sqrt(jnp.sum(sq[...], keepdims=True))
    outs[0][...] = norm
    factor = jnp.minimum(1.0, CLIP_NORM / norm)
    rows = (0, 3 * rd, rd, 2 * rd, 3 * rd + ro)
    rates = (0.1, 0.5, 0.1, 0.1, 0.5)
    decays = (DECAY, DECAY, DECAY, DECAY, 0.0)
    for w in range(5):
        height, width = params[w].shape
        grad = red[rows[w] : rows[w] + height, :width]
        new, first_new, second_new = adam(
            params[w][...], params[5 + w][...], params[10 + w][...], grad, factor, rates[w], decays[w]
        )
        outs[1 + 3 * w][...] = new
        outs[2 + 3 * w][...] = first_new
        outs[3 + 3 * w][...] = second_new
        outs[16 + w][...] = grad
        outs[21 + w][...] = new.astype(bf16)


def update(red, sq, params):
    like = lambda p, dtype: jax.ShapeDtypeStruct(p.shape, dtype)
    shapes = [jax.ShapeDtypeStruct((1, 1), f32)]
    shapes += [like(p, f32) for p in params[:5] for _ in range(3)]
    shapes += [like(p, f32) for p in params[:5]]
    shapes += [like(p, bf16) for p in params[:5]]
    return pl.pallas_call(
        update_kernel,
        out_shape=shapes,
        in_specs=[HBM] * 17,
        out_specs=[WHOLE] * len(shapes),
        scratch_shapes=[pltpu.VMEM(a.shape, f32) for a in (red, sq, *params)] + [pltpu.SemaphoreType.DMA((17,))],
        compiler_params=pltpu.CompilerParams(vmem_limit_bytes=62 * 1024 * 1024),
    )(red, sq, *params)


def per_device(n_dp, n_head, tokens, cotangent, lengths, *params):
    masters = params[:5]
    rd, ro = masters[0].shape[0], masters[1].shape[0]
    rows = -(-(3 * rd + 2 * ro) // 16) * 16
    axes, roles = factors(n_dp, n_head)
    weights = gather(axes, roles, rows, masters).reshape(n_head, n_dp, rows, 128)
    mixed, input_grad, grads = layer(lengths, weights, tokens, cotangent, rd, ro)
    grads = grads.reshape(tuple(size for _, _, size in axes) + (rows, 128))
    red, sq = scatter(axes, roles, grads)
    outs = update(red, sq, params)
    return (mixed, input_grad, outs[0].reshape(()), *outs[1:])


def solution(mesh):
    both, split, lens = P(("dp", "head"), None), P("dp", "head"), P("dp", None)
    weight = (split, both, split, split, both)
    return jax.shard_map(
        functools.partial(per_device, mesh.shape["dp"], mesh.shape["head"]),
        mesh=mesh,
        in_specs=(both, both, lens) + weight * 3,
        out_specs=(both, both, P())
        + tuple(spec for spec in weight for _ in range(3))
        + weight
        + weight,
        check_vma=False,
    )
```

```python
import functools
import itertools
import math

import jax
import jax.numpy as jnp
from jax import lax
from jax.experimental import pallas as pl
from jax.experimental.pallas import tpu as pltpu
from jax.sharding import PartitionSpec as P

MAX_LEN = 1024
STEP = 5
NORM_EPS = 1e-05
CLIP_NORM = 0.25
BETA_ONE = 0.5
BETA_TWO = 0.5
ADAM_EPS = 1e-08
DECAY = 0.1
HEADS = 4
HD = 32
D = 128
FF = 512
B = 256
CAP = 48
CHUNK = 128
GROUP = 8
TAIL = 6
SIDE = 4
WIDE = SIDE * B
BIG = 2.0**100
PDF_SHIFT = math.log2(4.0 / math.sqrt(2.0 * math.pi))
LIMIT = 88.0
MASKED = -1e30
SCALE = HD**-0.5 / math.log(2.0)
f32 = jnp.float32
bf16 = jnp.bfloat16
MESH = pl.DeviceIdType.MESH
HBM = pl.BlockSpec(memory_space=pltpu.HBM)
WHOLE = pl.BlockSpec(memory_space=pltpu.VMEM)


def mm(a, b):
    return lax.dot_general(a, b, (((1,), (0,)), ((), ())), preferred_element_type=f32)


def mm_nt(a, b):
    return lax.dot_general(a, b, (((1,), (1,)), ((), ())), preferred_element_type=f32)


def stats(value):
    mean = jnp.mean(value, axis=0, keepdims=True)
    centred = value - mean
    spread = jnp.mean(centred * centred, axis=0, keepdims=True)
    rate = lax.rsqrt(spread + NORM_EPS)
    return centred * rate, rate


def norm_back(grad, normed, rate, gain):
    scaled = grad * gain
    inner = jnp.mean(scaled, axis=0, keepdims=True)
    along = jnp.mean(scaled * normed, axis=0, keepdims=True)
    return rate * (scaled - inner - normed * along)


def split3(value):
    one = value.astype(bf16).astype(f32)
    two = (value - one).astype(bf16).astype(f32)
    return one, two, value - one - two


def lane_fold(value):
    out = value[:, :128]
    for j in range(1, value.shape[1] // 128):
        out = out + value[:, j * 128 : (j + 1) * 128]
    return out


def together(steps, tiles):
    def pair(p, carry):
        running = [steps(p, half) for half in range(SIDE)]
        while running:
            running = [r for r in running if next(r, "done") != "done"]
        return carry

    lax.fori_loop(0, tiles // SIDE, pair, 0)


def layer_kernel(
    rd,
    ro,
    lengths_hbm,
    w_hbm,
    tokens_hbm,
    cot_hbm,
    mixed_hbm,
    igrad_hbm,
    grads_hbm,
    uq,
    uk,
    lengths,
    w_ref,
    tokens,
    cot,
    loads,
    stores,
    bounds,
    wqkv_t,
    wqkv,
    wout,
    wout_t,
    wup,
    wup_t,
    wdown,
    wdown_t,
    gains,
    stage,
    qf,
    kf,
    vf,
    kt,
    vt,
    dof,
    probs,
    turn_a,
    turn_b,
    acc,
    dk_acc,
    dv_acc,
    resid_grad,
    first,
    cot_s,
    heads_s,
    second_s,
    low_s,
    hidden_s,
    pre_s,
    causal,
    qn,
    kn,
    g_qkv,
    g_out,
    g_up,
    g_down,
    g_norm,
    g_stage,
):
    n_head, n_dp, rp = w_ref.shape[:3]
    tiles = tokens.shape[0] // B
    row = lax.rem(lax.axis_index("head"), n_head)
    load = [
        pltpu.make_async_copy(src, dst, loads.at[n])
        for n, (src, dst) in enumerate(((lengths_hbm, lengths), (w_hbm, w_ref), (tokens_hbm, tokens), (cot_hbm, cot)))
    ]
    for copy in load:
        copy.start()
    load[0].wait()

    starts, ends = [], []
    at = jnp.int32(0)
    for s in range(lengths.shape[1]):
        starts.append(at)
        at = at + lengths[row, s]
        ends.append(at)
    place = lax.broadcasted_iota(jnp.int32, (8, B), 0)
    start_v = jnp.zeros((8, B), jnp.int32)
    end_v = jnp.zeros((8, B), jnp.int32)
    for s in range(8):
        start_v = jnp.where(place == s, starts[s], start_v)
        end_v = jnp.where(place == s, ends[s], end_v)

    def blank(t, carry):
        uq[t] = 0
        uk[t] = 0
        return carry

    def list_q(i, n):
        low = jnp.int32(0)
        for s in range(1, 8):
            low = jnp.where(starts[s] <= i * B, starts[s], low)

        def list_k(j, n):
            uq[n] = i
            uk[n] = j
            return n + 1

        return lax.fori_loop(lax.div(low, B), i + 1, list_k, n)

    blank(0, 0)
    units = lax.fori_loop(0, tiles, list_q, jnp.int32(1))
    lax.fori_loop(units, units + GROUP, blank, 0)
    listed = jnp.minimum(units - 1, CAP)
    steps = lax.div(listed + GROUP - 1 - TAIL, GROUP)
    tail = jnp.where(listed > GROUP * steps, 1, 0)
    last = GROUP * steps + TAIL * tail

    def in_steps(step):
        def whole(p, carry):
            for u in range(GROUP):
                step(GROUP * p + 1 + u, u % 2)
            return carry

        def short(p, carry):
            for u in range(TAIL):
                step(GROUP * steps + 1 + u, u % 2)
            return carry

        lax.fori_loop(0, steps, whole, 0)
        lax.fori_loop(0, tail, short, 0)


    key_i = lax.broadcasted_iota(jnp.int32, (B, B), 0)
    query_i = lax.broadcasted_iota(jnp.int32, (B, B), 1)
    allowed = key_i <= query_i
    causal[0] = jnp.full((B, B), jnp.inf, bf16)
    causal[1] = jnp.where(allowed, jnp.inf, 0.0).astype(bf16)
    causal[2] = jnp.zeros((B, B), bf16)
    for ref in (qn, kn, g_qkv, g_out, g_up, g_down, g_norm, cot_s, heads_s, second_s, low_s, hidden_s, pre_s):
        ref[...] = jnp.zeros_like(ref)

    load[1].wait()
    for h in range(n_head):
        stage[...] = jnp.concatenate([w_ref[h, d].astype(f32) for d in range(n_dp)], axis=0)
        pick = lambda lo, n: jnp.concatenate(
            [stage[d * rp + lo : d * rp + lo + n] for d in range(n_dp)], axis=0
        )
        q = pick(0, rd)
        wqkv_t[h] = q.T[: 3 * HD].astype(bf16)
        wqkv[:, h * 3 * HD : (h + 1) * 3 * HD] = q[:, : 3 * HD].astype(bf16)
        u = pick(rd, rd)
        wup[:, h * 128 : (h + 1) * 128] = u.astype(bf16)
        wup_t[h * 128 : (h + 1) * 128] = (0.5 * u.T).astype(bf16)
        u = pick(2 * rd, rd)
        wdown[:, h * 128 : (h + 1) * 128] = u.astype(bf16)
        wdown_t[h * 128 : (h + 1) * 128] = (0.5 * u.T).astype(bf16)
        for d in range(n_dp):
            at = (d * n_head + h) * ro
            g_out[at : at + ro] = stage[d * rp + 3 * rd : d * rp + 3 * rd + ro]
            gains[at : at + ro] = stage[d * rp + 3 * rd + ro : d * rp + 3 * rd + 2 * ro]
    wo = g_out[...]
    wout[...] = wo.astype(bf16)
    wout_t[...] = wo.T.astype(bf16)
    g_out[...] = jnp.zeros_like(g_out)
    gain1, shift1 = gains[:, 0:1], gains[:, 1:2]
    gain2, shift2 = gains[:, 2:3], gains[:, 3:4]

    def project(p, half):
        i = SIDE * p + half
        x = tokens[pl.ds(pl.multiple_of(i * B, B), B), :].T.astype(f32)
        yield
        n1, _ = stats(x)
        f = (n1 * gain1 + shift1).astype(bf16)
        first[p, :, half * B : (half + 1) * B] = f
        yield
        where_t = i * B + lax.broadcasted_iota(jnp.int32, (8, B), 1)
        inside = ((where_t >= start_v) & (where_t < end_v)).astype(f32)
        zeros8 = jnp.zeros((8, B), f32)
        ones8 = jnp.ones((8, B), f32)
        key_side = jnp.concatenate([inside, ones8], axis=0).astype(bf16)
        query_side = jnp.concatenate([(1.0 - inside) * -BIG, zeros8], axis=0).astype(bf16)
        value_side = jnp.concatenate([ones8, zeros8], axis=0).astype(bf16)
        for h in range(HEADS):
            packed = mm(wqkv_t[h], f).astype(bf16)
            yield
            q, k, v = (packed[n * HD : (n + 1) * HD] for n in range(3))
            squares = packed.astype(f32)
            squares = squares * squares
            qn[h] = jnp.maximum(qn[h], jnp.sum(squares[:HD], axis=0, keepdims=True))
            kn[h] = jnp.maximum(kn[h], jnp.sum(squares[HD : 2 * HD], axis=0, keepdims=True))
            qf[h, i, :HD] = q
            qf[h, i, HD:] = query_side
            kf[h, i] = k
            vf[h, i, :HD] = v
            vf[h, i, HD:] = value_side
            kt[h, i] = jnp.concatenate([k, key_side], axis=0).T
            vt[h, i] = jnp.concatenate([v, value_side], axis=0).T
            acc[h, i] = jnp.zeros_like(acc[h, i])
            dk_acc[h, i] = jnp.zeros_like(dk_acc[h, i])
            dv_acc[h, i] = jnp.zeros_like(dv_acc[h, i])
            yield

    load[2].wait()
    together(project, tiles)

    bound = jnp.float32(0.0)
    for h in range(HEADS):
        bound = jnp.maximum(bound, jnp.max(qn[h]) * jnp.max(kn[h]))

    def scores(h, i, j):
        return mm(kt[h, j], qf[h, i])

    @pl.when(jnp.logical_not(bound * SCALE**2 <= LIMIT * LIMIT))
    def _():
        bounds[...] = jnp.full_like(bounds, MASKED)

        def top(t, carry):
            i, j = uq[t], uk[t]
            masked = jnp.where(allowed | (i != j), 0.0, MASKED)
            for h in range(HEADS):
                s = scores(h, i, j) + masked
                bounds[h, i] = jnp.maximum(bounds[h, i], jnp.max(s, axis=0, keepdims=True))
            return carry

        lax.fori_loop(1, units, top, 0)

        def shift(i, carry):
            for h in range(HEADS):
                one, two, three = split3(-bounds[h, i])
                r = lax.broadcasted_iota(jnp.int32, (16, B), 0)
                old = qf[h, i, HD : HD + 16].astype(f32)
                new = jnp.where(r == 8, one, jnp.where(r == 9, two, jnp.where(r == 10, three, old)))
                qf[h, i, HD : HD + 16] = new.astype(bf16)
            return carry

        lax.fori_loop(0, tiles, shift, 0)

    def weigh(t, slot, *kept_too):
        i, j = uq[t], uk[t]
        cut = causal[jnp.where(t >= units, 2, jnp.where(i == j, 1, 0))]
        for h in range(HEADS):
            p = jnp.minimum(jnp.exp2(scores(h, i, j) * SCALE).astype(bf16), cut)
            for ref in (probs.at[slot], *kept_too):
                ref[h] = p

    def weighted(t, block):
        i, j = uq[t], uk[t]
        for h in range(HEADS):
            acc[h, i] += mm(vf[h, j, : HD + 8], block[h])

    def forward(t, turn):
        weigh(t, t - 1, turns[turn])
        weighted(t - 1, turns[1 - turn])

    def forward_rest(t, carry):
        weigh(t, CAP)
        weighted(t, probs.at[CAP])
        return carry

    turns = (turn_a, turn_b)
    turn_b[...] = jnp.zeros_like(turn_b)
    in_steps(forward)
    weighted(last, turn_b)
    lax.fori_loop(CAP + 1, units, forward_rest, 0)

    def feed_grads():
        g_down[...] += mm_nt(hidden_s[...], cot_s[...])
        g_up[...] += mm_nt(pre_s[...], second_s[...])
        g_out[...] += mm_nt(heads_s[...], low_s[...])

    def write_tile(i, result, hbm):
        at = pl.ds(pl.multiple_of(i * B, B), B)
        return pltpu.make_async_copy(result.at[at], hbm.at[at], stores.at[i])

    def wait_tiles(result, hbm):
        def wait_tile(i, carry):
            write_tile(i, result, hbm).wait()
            return carry

        lax.fori_loop(0, tiles, wait_tile, 0)

    def feed(p, half):
        i = SIDE * p + half
        at = pl.ds(pl.multiple_of(i * B, B), B)
        lanes = slice(half * B, (half + 1) * B)
        if half == 0:
            feed_grads()
        outs, inv = [], []
        for h in range(HEADS):
            r = 1.0 / acc[h, i, HD : HD + 1]
            inv.append(r)
            outs.append(acc[h, i, :HD] * r)
            acc[h, i] = jnp.zeros_like(acc[h, i])
        heads = jnp.concatenate(outs, axis=0).astype(bf16)
        x = tokens[at, :].T.astype(f32)
        c16 = cot[at, :].T
        c32 = c16.astype(f32)
        yield
        resid = x + mm(wout_t[...], heads)
        yield
        n2, rate2 = stats(resid)
        second = (n2 * gain2 + shift2).astype(bf16)
        yield
        heads_s[:, lanes] = heads
        cot_s[:, lanes] = c16
        second_s[:, lanes] = second
        for c in range(0, FF, CHUNK):
            rows = slice(c, c + CHUNK)
            half_pre = mm(wup_t[rows], second)
            half_back = mm(wdown_t[rows], c16)
            yield
            twice_cdf = 1.0 + lax.erf(half_pre * 2.0**0.5)
            slope = half_pre * jnp.exp2(half_pre * half_pre * (-2.0 / math.log(2.0)) + PDF_SHIFT)
            hidden_s[rows, lanes] = (half_pre * twice_cdf).astype(bf16)
            pre_s[rows, lanes] = (half_back * (twice_cdf + slope)).astype(bf16)
            yield
        second_in = mm(wup[...], pre_s[:, lanes])
        yield
        cot[at, :] = (resid + mm(wdown[...], hidden_s[:, lanes])).astype(bf16).T
        g_norm[2] += lane_fold(second_in * n2)
        g_norm[3] += lane_fold(second_in)
        rg = c32 + norm_back(second_in, n2, rate2, gain2)
        low = rg.astype(bf16)
        yield
        hg = mm(wout[...], low).astype(bf16).astype(f32)
        resid_grad[i] = rg
        low_s[:, lanes] = low
        yield
        r8 = lax.broadcasted_iota(jnp.int32, (16, B), 0)
        for h in range(HEADS):
            do16 = (hg[h * HD : (h + 1) * HD] * inv[h]).astype(bf16)
            do = do16.astype(f32)
            delta = jnp.sum(do * outs[h], axis=0, keepdims=True)
            one, two, three = split3(-delta)
            extra = jnp.where(r8 == 0, one, jnp.where(r8 == 1, two, jnp.where(r8 == 2, three, 0.0)))
            dof[h, i, :HD] = do16
            dof[h, i, HD:] = extra.astype(bf16)
        write_tile(i, cot, mixed_hbm).start()

    load[3].wait()
    together(feed, tiles)
    feed_grads()

    def pushed(t, slot, block):
        i, j = uq[t], uk[t]
        for h in range(HEADS):
            w = probs[slot, h]
            pg = mm(vt[h, j], dof[h, i])
            block[h] = (w.astype(f32) * pg).astype(bf16)
            dv_acc[h, j] += mm_nt(dof[h, i, :HD], w)

    def pulled(t, block):
        i, j = uq[t], uk[t]
        for h in range(HEADS):
            acc[h, i, :HD] += mm(kf[h, j], block[h])
            dk_acc[h, j] += mm_nt(qf[h, i, :HD], block[h])

    def backward(t, turn):
        pushed(t, t - 1, turns[turn])
        pulled(t - 1, turns[1 - turn])

    def backward_rest(t, carry):
        weigh(t, CAP)
        pushed(t, CAP, turn_a)
        pulled(t, turn_a)
        return carry

    turn_b[...] = jnp.zeros_like(turn_b)
    in_steps(backward)
    pulled(last, turn_b)
    lax.fori_loop(CAP + 1, units, backward_rest, 0)

    wait_tiles(cot, mixed_hbm)

    def finish(p, half):
        i = SIDE * p + half
        at = pl.ds(pl.multiple_of(i * B, B), B)
        lanes = slice(half * B, (half + 1) * B)
        rows = []
        for h in range(HEADS):
            rows += [acc[h, i, :HD] * HD**-0.5, dk_acc[h, i] * HD**-0.5, dv_acc[h, i]]
        packed_grad = jnp.concatenate(rows, axis=0).astype(bf16)
        hidden_s[: 3 * D, lanes] = packed_grad
        yield
        first_in = mm(wqkv[...], packed_grad)
        if half == SIDE - 1:
            g_qkv[...] += mm_nt(hidden_s[: 3 * D, :], first[p])
        x = tokens[at, :].T.astype(f32)
        yield
        n1, rate1 = stats(x)
        yield
        g_norm[0] += lane_fold(first_in * n1)
        g_norm[1] += lane_fold(first_in)
        out = resid_grad[i] + norm_back(first_in, n1, rate1, gain1)
        yield
        tokens[at, :] = out.astype(bf16).T
        write_tile(i, tokens, igrad_hbm).start()

    together(finish, tiles)

    lane = lax.broadcasted_iota(jnp.int32, (D, 128), 1)
    norm = jnp.zeros((D, 128), f32)
    for c in range(4):
        norm = jnp.where(lane == c, jnp.sum(g_norm[c], axis=1, keepdims=True), norm)
    gains[...] = norm
    g_stage[...] = jnp.zeros_like(g_stage)
    for h in range(n_head):
        cols = slice(h * 128, (h + 1) * 128)
        qkv = g_qkv[h * 3 * HD : (h + 1) * 3 * HD].T
        up, down = g_up[cols].T, g_down[cols].T
        for d in range(n_dp):
            rows = slice(d * rd, (d + 1) * rd)
            at = (d * n_head + h) * ro
            g_stage[0:rd, : 3 * HD] = qkv[rows]
            g_stage[rd : 2 * rd] = up[rows]
            g_stage[2 * rd : 3 * rd] = down[rows]
            g_stage[3 * rd : 3 * rd + ro] = g_out[at : at + ro]
            g_stage[3 * rd + ro : 3 * rd + 2 * ro] = gains[at : at + ro]
            w_ref[h, d] = g_stage[...].astype(bf16)
    out = pltpu.make_async_copy(w_ref, grads_hbm, loads.at[0])
    out.start()
    wait_tiles(tokens, igrad_hbm)
    out.wait()


def layer(lengths, weights, tokens, cot, rd, ro):
    n_head, n_dp, rp = weights.shape[:3]
    tiles = tokens.shape[0] // B
    listed = tiles * (MAX_LEN // B + 1) + GROUP + 1
    vmem = lambda shape, dtype: pltpu.VMEM(shape, dtype)
    scratch = [
        pltpu.SMEM((listed,), jnp.int32),
        pltpu.SMEM((listed,), jnp.int32),
        pltpu.SMEM(lengths.shape, jnp.int32),
        vmem(weights.shape, bf16),
        vmem(tokens.shape, bf16),
        vmem(tokens.shape, bf16),
        pltpu.SemaphoreType.DMA((4,)),
        pltpu.SemaphoreType.DMA((tiles,)),
        vmem((HEADS, tiles, 1, B), f32),
        vmem((HEADS, 3 * HD, D), bf16),
        vmem((D, 3 * D), bf16),
        vmem((D, D), bf16),
        vmem((D, D), bf16),
        vmem((D, FF), bf16),
        vmem((FF, D), bf16),
        vmem((D, FF), bf16),
        vmem((FF, D), bf16),
        vmem((D, 128), f32),
        vmem((n_dp * rp, 128), f32),
        vmem((HEADS, tiles, 48, B), bf16),
        vmem((HEADS, tiles, HD, B), bf16),
        vmem((HEADS, tiles, 48, B), bf16),
        vmem((HEADS, tiles, B, 48), bf16),
        vmem((HEADS, tiles, B, 48), bf16),
        vmem((HEADS, tiles, 48, B), bf16),
        vmem((CAP + 1, HEADS, B, B), bf16),
        vmem((HEADS, B, B), bf16),
        vmem((HEADS, B, B), bf16),
        vmem((HEADS, tiles, HD + 8, B), f32),
        vmem((HEADS, tiles, HD, B), f32),
        vmem((HEADS, tiles, HD, B), f32),
        vmem((tiles, D, B), f32),
        vmem((tiles // SIDE, D, WIDE), bf16),
        vmem((D, WIDE), bf16),
        vmem((D, WIDE), bf16),
        vmem((D, WIDE), bf16),
        vmem((D, WIDE), bf16),
        vmem((FF, WIDE), bf16),
        vmem((FF, WIDE), bf16),
        vmem((3, B, B), bf16),
        vmem((HEADS, 1, B), f32),
        vmem((HEADS, 1, B), f32),
        vmem((3 * D, D), f32),
        vmem((D, D), f32),
        vmem((FF, D), f32),
        vmem((FF, D), f32),
        vmem((4, D, 128), f32),
        vmem((rp, 128), f32),
    ]
    return pl.pallas_call(
        functools.partial(layer_kernel, rd, ro),
        out_shape=(
            jax.ShapeDtypeStruct(tokens.shape, bf16),
            jax.ShapeDtypeStruct(tokens.shape, bf16),
            jax.ShapeDtypeStruct((n_head, n_dp, rp, 128), bf16),
        ),
        in_specs=[HBM] * 4,
        out_specs=(HBM, HBM, HBM),
        scratch_shapes=scratch,
        compiler_params=pltpu.CompilerParams(vmem_limit_bytes=63 * 1024 * 1024),
    )(lengths, weights, tokens, cot)


def factors(n_dp, n_head):
    if (n_dp, n_head) == (8, 4):
        return (("head", 2, 2), ("head", 1, 2), ("dp", 2, 4), ("dp", 1, 2)), (2, (0, 3), 1)
    own = 2 if n_dp % 2 == 0 else 1
    far = 4 if n_dp // own % 4 == 0 else 1
    near = n_dp // own // far
    return (("head", 1, n_head), ("dp", own * far, near), ("dp", own, far), ("dp", 1, own)), (2, (0, 1), 3)


def digit(axis, stride, size):
    return lax.rem(lax.div(lax.axis_index(axis), stride), size)


def others(axes, group):
    found = []
    for offsets in itertools.product(*(range(axes[a][2]) for a in group)):
        if not any(offsets):
            continue
        place, theirs, source = {}, {}, {}
        for a, offset in zip(group, offsets):
            axis, stride, size = axes[a]
            mine = digit(*axes[a])
            theirs[a] = lax.rem(mine + offset, size)
            source[a] = lax.rem(mine + size - offset, size)
            place[axis] = place.get(axis, lax.axis_index(axis)) + (theirs[a] - mine) * stride
        found.append((place, theirs, source))
    return found


def greet(peers):
    barrier = pltpu.get_barrier_semaphore()
    for device, _, _ in peers:
        pl.semaphore_signal(barrier, inc=1, device_id=device, device_id_type=MESH)
    return lambda: pl.semaphore_wait(barrier, len(peers))


class Links:
    def __init__(self, send, recv):
        self.send, self.recv, self.count, self.started = send, recv, 0, []

    def copy(self, n, src, dst, place):
        return pltpu.make_async_remote_copy(
            src_ref=src,
            dst_ref=dst,
            send_sem=self.send.at[n],
            recv_sem=self.recv.at[n],
            device_id=place,
            device_id_type=MESH,
        )

    def start(self, src, dst, place, lands):
        n = self.count
        self.count += 1
        out = self.copy(n, src, dst, place)
        out.start()
        self.started.append(out)
        return self.copy(n, lands, lands, place).wait_recv

    def drain(self):
        for out in self.started:
            out.wait_send()


def gather_kernel(axes, roles, *refs):
    masters, w_ref = refs[:5], refs[5]
    held, (stage, block, local, send, recv) = refs[6:11], refs[11:]
    far, near, own = roles
    line, plane, chip = others(axes, (far,)), others(axes, near), others(axes, (own,))
    arrived = greet(line + plane + chip)
    loads = [pltpu.make_async_copy(m, h, local.at[n]) for n, (m, h) in enumerate(zip(masters, held))]
    for load in loads:
        load.start()
    stage[...] = jnp.zeros_like(stage)
    for load in loads:
        load.wait()
    qkv, out, up, down, norm = held
    rd, ro = qkv.shape[0], out.shape[0]
    at = 0
    for part, height in ((qkv, rd), (up, rd), (down, rd), (out, ro), (norm, ro)):
        stage[at : at + height, : part.shape[1]] = part[...]
        at += height
    block[...] = stage[...].astype(bf16)
    mine = {a: digit(*axes[a]) for a in range(4)}
    at = lambda digits: w_ref.at[tuple({**mine, **digits}[a] for a in range(4))]
    keep = pltpu.make_async_copy(block, at({}), local.at[0])
    keep.start()
    arrived()
    links = Links(send, recv)
    first = [links.start(block, at({}), place, at(source)) for place, _, source in line]

    def onward(src, digits):
        dst = at(digits)
        waits = [
            (links.start(src, dst, place, at({**digits, **source})), {**digits, **source})
            for place, _, source in plane
        ]
        return waits, [links.start(src, dst, place, at({**digits, **source})) for place, _, source in chip]

    second, third = onward(block, {})
    for wait, (_, _, source) in zip(first, line):
        wait()
        waits, more = onward(at(source), source)
        second += waits
        third += more
    for wait, digits in second:
        wait()
        third += [
            links.start(at(digits), at(digits), place, at({**digits, **source})) for place, _, source in chip
        ]
    for wait in third:
        wait()
    links.drain()
    keep.wait()


def gather(axes, roles, rows, masters, cid=0):
    sizes = [size for _, _, size in axes]
    copies = math.prod(sizes)
    return pl.pallas_call(
        functools.partial(gather_kernel, axes, roles),
        out_shape=jax.ShapeDtypeStruct(tuple(sizes) + (rows, 128), bf16),
        in_specs=[HBM] * 5,
        out_specs=HBM,
        scratch_shapes=[pltpu.VMEM(m.shape, f32) for m in masters]
        + [
            pltpu.VMEM((rows, 128), f32),
            pltpu.VMEM((rows, 128), bf16),
            pltpu.SemaphoreType.DMA((5,)),
            pltpu.SemaphoreType.DMA((copies,)),
            pltpu.SemaphoreType.DMA((copies,)),
        ],
        compiler_params=pltpu.CompilerParams(
            collective_id=cid, has_side_effects=True, vmem_limit_bytes=62 * 1024 * 1024
        ),
    )(*masters)


def scatter_kernel(axes, roles, g_ref, red_ref, sq_ref, *scratch):
    held, from_chip, partial, from_plane, passed, from_line, sq_chip, sq_all, local, send, recv = scratch
    far, near, own = roles
    line, plane, chip = others(axes, (far,)), others(axes, near), others(axes, (own,))
    every = others(axes, tuple(sorted((far,) + near)))
    ready = greet(chip + every)
    mine = {a: digit(*axes[a]) for a in range(4)}
    pick = lambda digits: g_ref.at[tuple(digits.get(a, slice(None)) for a in range(4))]
    pieces = [theirs for _, theirs, _ in line] + [{far: mine[far]}]
    loads = []
    for k, piece in enumerate(pieces):
        loads.append(pltpu.make_async_copy(pick({**piece, own: mine[own]}), held.at[k], local.at[k]))
        loads[-1].start()
    ready()
    links = Links(send, recv)
    first = [
        [
            links.start(pick({**piece, **theirs}), from_chip.at[k, n], place, from_chip.at[k, n])
            for n, (place, theirs, _) in enumerate(chip)
        ]
        for k, piece in enumerate(pieces)
    ]
    second = []
    inner = lambda digits: tuple(digits[a] for a in near)
    for k in range(len(pieces)):
        loads[k].wait()
        total = held[k].astype(f32)
        for n, wait in enumerate(first[k]):
            wait()
            total = total + from_chip[k, n].astype(f32)
        partial[k] = total.astype(bf16)
        second.append(
            [
                links.start(partial.at[(k,) + inner(theirs)], from_plane.at[k, n], place, from_plane.at[k, n])
                for n, (place, theirs, _) in enumerate(plane)
            ]
        )
    third = []
    for k in range(len(pieces)):
        total = partial[(k,) + inner(mine)].astype(f32)
        for n, wait in enumerate(second[k]):
            wait()
            total = total + from_plane[k, n].astype(f32)
        if k < len(line):
            passed[k] = total.astype(bf16)
            third.append(links.start(passed.at[k], from_line.at[k], line[k][0], from_line.at[k]))
    for n, wait in enumerate(third):
        wait()
        total = total + from_line[n].astype(f32)
    red_ref[...] = total
    square = total * total
    fold = square[0:8]
    for r in range(8, square.shape[0], 8):
        fold = fold + square[r : r + 8]
    fold = jnp.sum(fold, axis=0, keepdims=True)
    for group, peers, ref in (((own,), chip, sq_chip), (tuple(sorted((far,) + near)), every, sq_all)):
        at = lambda digits: ref.at[tuple(digits[a] for a in group)]
        ref[tuple(mine[a] for a in group)] = fold
        waits = [links.start(at(mine), at(mine), place, at(source)) for place, _, source in peers]
        for wait in waits:
            wait()
        fold = 0.0
        for index in itertools.product(*(range(axes[a][2]) for a in group)):
            fold = fold + ref[index]
    sq_ref[...] = fold
    links.drain()


def scatter(axes, roles, grads, cid=1):
    sizes = [size for _, _, size in axes]
    far, near, own = roles
    block = grads.shape[-2:]
    spread = tuple(sizes[a] for a in range(4) if a in near) + block
    nf, np_, no = sizes[far], math.prod(sizes[a] for a in near), sizes[own]
    least = lambda n: max(n, 1)
    copies = nf * (no - 1) + nf * (np_ - 1) + (nf - 1) + (no - 1) + (nf * np_ - 1)
    together = tuple(sizes[a] for a in sorted((far,) + near))
    return pl.pallas_call(
        functools.partial(scatter_kernel, axes, roles),
        out_shape=(jax.ShapeDtypeStruct(block, f32), jax.ShapeDtypeStruct((1, 128), f32)),
        in_specs=[HBM],
        out_specs=(WHOLE, WHOLE),
        scratch_shapes=[
            pltpu.VMEM((nf,) + spread, bf16),
            pltpu.VMEM((nf, least(no - 1)) + spread, bf16),
            pltpu.VMEM((nf,) + spread, bf16),
            pltpu.VMEM((nf, least(np_ - 1)) + block, bf16),
            pltpu.VMEM((least(nf - 1),) + block, bf16),
            pltpu.VMEM((least(nf - 1),) + block, bf16),
            pltpu.VMEM((no, 1, 128), f32),
            pltpu.VMEM(together + (1, 128), f32),
            pltpu.SemaphoreType.DMA((nf,)),
            pltpu.SemaphoreType.DMA((copies,)),
            pltpu.SemaphoreType.DMA((copies,)),
        ],
        compiler_params=pltpu.CompilerParams(
            collective_id=cid, has_side_effects=True, vmem_limit_bytes=62 * 1024 * 1024
        ),
    )(grads)


def adam(weight, first, second, grad, factor, rate, decay):
    clipped = grad * factor
    first_new = BETA_ONE * first + (1.0 - BETA_ONE) * clipped
    second_new = BETA_TWO * second + (1.0 - BETA_TWO) * clipped * clipped
    direction = (
        first_new
        / (1.0 - BETA_ONE**STEP)
        / (jnp.sqrt(second_new / (1.0 - BETA_TWO**STEP)) + ADAM_EPS)
    )
    return weight - rate * (direction + decay * weight), first_new, second_new


def update_kernel(*refs):
    held = refs[-18:-1]
    copies = [pltpu.make_async_copy(src, dst, refs[-1].at[n]) for n, (src, dst) in enumerate(zip(refs, held))]
    for copy in copies:
        copy.start()
    for copy in copies:
        copy.wait()
    (red, sq, *params), outs = held, refs[17:-18]
    rd, ro = params[0].shape[0], params[1].shape[0]
    norm = jnp.sqrt(jnp.sum(sq[...], keepdims=True))
    outs[0][...] = norm
    factor = jnp.minimum(1.0, CLIP_NORM / norm)
    rows = (0, 3 * rd, rd, 2 * rd, 3 * rd + ro)
    rates = (0.1, 0.5, 0.1, 0.1, 0.5)
    decays = (DECAY, DECAY, DECAY, DECAY, 0.0)
    for w in range(5):
        height, width = params[w].shape
        grad = red[rows[w] : rows[w] + height, :width]
        new, first_new, second_new = adam(
            params[w][...], params[5 + w][...], params[10 + w][...], grad, factor, rates[w], decays[w]
        )
        outs[1 + 3 * w][...] = new
        outs[2 + 3 * w][...] = first_new
        outs[3 + 3 * w][...] = second_new
        outs[16 + w][...] = grad
        outs[21 + w][...] = new.astype(bf16)


def update(red, sq, params):
    like = lambda p, dtype: jax.ShapeDtypeStruct(p.shape, dtype)
    shapes = [jax.ShapeDtypeStruct((1, 1), f32)]
    shapes += [like(p, f32) for p in params[:5] for _ in range(3)]
    shapes += [like(p, f32) for p in params[:5]]
    shapes += [like(p, bf16) for p in params[:5]]
    return pl.pallas_call(
        update_kernel,
        out_shape=shapes,
        in_specs=[HBM] * 17,
        out_specs=[WHOLE] * len(shapes),
        scratch_shapes=[pltpu.VMEM(a.shape, f32) for a in (red, sq, *params)] + [pltpu.SemaphoreType.DMA((17,))],
        compiler_params=pltpu.CompilerParams(vmem_limit_bytes=62 * 1024 * 1024),
    )(red, sq, *params)


def per_device(n_dp, n_head, tokens, cotangent, lengths, *params):
    masters = params[:5]
    rd, ro = masters[0].shape[0], masters[1].shape[0]
    rows = -(-(3 * rd + 2 * ro) // 16) * 16
    axes, roles = factors(n_dp, n_head)
    weights = gather(axes, roles, rows, masters).reshape(n_head, n_dp, rows, 128)
    mixed, input_grad, grads = layer(lengths, weights, tokens, cotangent, rd, ro)
    grads = grads.reshape(tuple(size for _, _, size in axes) + (rows, 128))
    red, sq = scatter(axes, roles, grads)
    outs = update(red, sq, params)
    return (mixed, input_grad, outs[0].reshape(()), *outs[1:])


def solution(mesh):
    both, split, lens = P(("dp", "head"), None), P("dp", "head"), P("dp", None)
    weight = (split, both, split, split, both)
    return jax.shard_map(
        functools.partial(per_device, mesh.shape["dp"], mesh.shape["head"]),
        mesh=mesh,
        in_specs=(both, both, lens) + weight * 3,
        out_specs=(both, both, P())
        + tuple(spec for spec in weight for _ in range(3))
        + weight
        + weight,
        check_vma=False,
    )
```

```python
import functools
import itertools
import math

import jax
import jax.numpy as jnp
from jax import lax
from jax.experimental import pallas as pl
from jax.experimental.pallas import tpu as pltpu
from jax.sharding import PartitionSpec as P

MAX_LEN = 1024
STEP = 5
NORM_EPS = 1e-05
CLIP_NORM = 0.25
BETA_ONE = 0.5
BETA_TWO = 0.5
ADAM_EPS = 1e-08
DECAY = 0.1
HEADS = 4
HD = 32
D = 128
FF = 512
B = 256
CAP = 48
CHUNK = 256
GROUP = 8
TAIL = 6
SIDE = 4
WIDE = SIDE * B
BIG = 2.0**100
PDF_SHIFT = math.log2(4.0 / math.sqrt(2.0 * math.pi))
LIMIT = 88.0
MASKED = -1e30
SCALE = HD**-0.5 / math.log(2.0)
f32 = jnp.float32
bf16 = jnp.bfloat16
MESH = pl.DeviceIdType.MESH
HBM = pl.BlockSpec(memory_space=pltpu.HBM)
WHOLE = pl.BlockSpec(memory_space=pltpu.VMEM)


def mm(a, b):
    return lax.dot_general(a, b, (((1,), (0,)), ((), ())), preferred_element_type=f32)


def mm_nt(a, b):
    return lax.dot_general(a, b, (((1,), (1,)), ((), ())), preferred_element_type=f32)


def stats(value):
    mean = jnp.mean(value, axis=0, keepdims=True)
    centred = value - mean
    spread = jnp.mean(centred * centred, axis=0, keepdims=True)
    rate = lax.rsqrt(spread + NORM_EPS)
    return centred * rate, rate


def norm_back(grad, normed, rate, gain):
    scaled = grad * gain
    inner = jnp.mean(scaled, axis=0, keepdims=True)
    along = jnp.mean(scaled * normed, axis=0, keepdims=True)
    return rate * (scaled - inner - normed * along)


def split3(value):
    one = value.astype(bf16).astype(f32)
    two = (value - one).astype(bf16).astype(f32)
    return one, two, value - one - two


def lane_fold(value):
    out = value[:, :128]
    for j in range(1, value.shape[1] // 128):
        out = out + value[:, j * 128 : (j + 1) * 128]
    return out


def together(steps, tiles):
    def pair(p, carry):
        running = [steps(p, half) for half in range(SIDE)]
        while running:
            running = [r for r in running if next(r, "done") != "done"]
        return carry

    lax.fori_loop(0, tiles // SIDE, pair, 0)


def layer_kernel(
    rd,
    ro,
    lengths_hbm,
    w_hbm,
    tokens_hbm,
    cot_hbm,
    mixed_hbm,
    igrad_hbm,
    grads_hbm,
    uq,
    uk,
    lengths,
    w_ref,
    tokens,
    cot,
    loads,
    stores,
    bounds,
    wqkv_t,
    wqkv,
    wout,
    wout_t,
    wup,
    wup_t,
    wdown,
    wdown_t,
    gains,
    stage,
    qf,
    kf,
    vf,
    kt,
    vt,
    dof,
    probs,
    turn_a,
    turn_b,
    acc,
    dk_acc,
    dv_acc,
    resid_grad,
    first,
    cot_s,
    heads_s,
    second_s,
    low_s,
    hidden_s,
    pre_s,
    causal,
    qn,
    kn,
    g_qkv,
    g_out,
    g_up,
    g_down,
    g_norm,
    g_stage,
):
    n_head, n_dp, rp = w_ref.shape[:3]
    tiles = tokens.shape[0] // B
    row = lax.rem(lax.axis_index("head"), n_head)
    load = [
        pltpu.make_async_copy(src, dst, loads.at[n])
        for n, (src, dst) in enumerate(((lengths_hbm, lengths), (w_hbm, w_ref), (tokens_hbm, tokens), (cot_hbm, cot)))
    ]
    for copy in load:
        copy.start()
    load[0].wait()

    starts, ends = [], []
    at = jnp.int32(0)
    for s in range(lengths.shape[1]):
        starts.append(at)
        at = at + lengths[row, s]
        ends.append(at)
    place = lax.broadcasted_iota(jnp.int32, (8, B), 0)
    start_v = jnp.zeros((8, B), jnp.int32)
    end_v = jnp.zeros((8, B), jnp.int32)
    for s in range(8):
        start_v = jnp.where(place == s, starts[s], start_v)
        end_v = jnp.where(place == s, ends[s], end_v)

    def blank(t, carry):
        uq[t] = 0
        uk[t] = 0
        return carry

    def list_q(i, n):
        low = jnp.int32(0)
        for s in range(1, 8):
            low = jnp.where(starts[s] <= i * B, starts[s], low)

        def list_k(j, n):
            uq[n] = i
            uk[n] = j
            return n + 1

        return lax.fori_loop(lax.div(low, B), i + 1, list_k, n)

    blank(0, 0)
    units = lax.fori_loop(0, tiles, list_q, jnp.int32(1))
    lax.fori_loop(units, units + GROUP, blank, 0)
    listed = jnp.minimum(units - 1, CAP)
    steps = lax.div(listed + GROUP - 1 - TAIL, GROUP)
    tail = jnp.where(listed > GROUP * steps, 1, 0)
    last = GROUP * steps + TAIL * tail

    def in_steps(step):
        def whole(p, carry):
            for u in range(GROUP):
                step(GROUP * p + 1 + u, u % 2)
            return carry

        def short(p, carry):
            for u in range(TAIL):
                step(GROUP * steps + 1 + u, u % 2)
            return carry

        lax.fori_loop(0, steps, whole, 0)
        lax.fori_loop(0, tail, short, 0)


    key_i = lax.broadcasted_iota(jnp.int32, (B, B), 0)
    query_i = lax.broadcasted_iota(jnp.int32, (B, B), 1)
    allowed = key_i <= query_i
    causal[0] = jnp.full((B, B), jnp.inf, bf16)
    causal[1] = jnp.where(allowed, jnp.inf, 0.0).astype(bf16)
    causal[2] = jnp.zeros((B, B), bf16)
    for ref in (qn, kn, g_qkv, g_out, g_up, g_down, g_norm, cot_s, heads_s, second_s, low_s, hidden_s, pre_s):
        ref[...] = jnp.zeros_like(ref)

    load[1].wait()
    for h in range(n_head):
        stage[...] = jnp.concatenate([w_ref[h, d].astype(f32) for d in range(n_dp)], axis=0)
        pick = lambda lo, n: jnp.concatenate(
            [stage[d * rp + lo : d * rp + lo + n] for d in range(n_dp)], axis=0
        )
        q = pick(0, rd)
        wqkv_t[h] = q.T[: 3 * HD].astype(bf16)
        wqkv[:, h * 3 * HD : (h + 1) * 3 * HD] = q[:, : 3 * HD].astype(bf16)
        u = pick(rd, rd)
        wup[:, h * 128 : (h + 1) * 128] = u.astype(bf16)
        wup_t[h * 128 : (h + 1) * 128] = (0.5 * u.T).astype(bf16)
        u = pick(2 * rd, rd)
        wdown[:, h * 128 : (h + 1) * 128] = u.astype(bf16)
        wdown_t[h * 128 : (h + 1) * 128] = (0.5 * u.T).astype(bf16)
        for d in range(n_dp):
            at = (d * n_head + h) * ro
            g_out[at : at + ro] = stage[d * rp + 3 * rd : d * rp + 3 * rd + ro]
            gains[at : at + ro] = stage[d * rp + 3 * rd + ro : d * rp + 3 * rd + 2 * ro]
    wo = g_out[...]
    wout[...] = wo.astype(bf16)
    wout_t[...] = wo.T.astype(bf16)
    g_out[...] = jnp.zeros_like(g_out)
    gain1, shift1 = gains[:, 0:1], gains[:, 1:2]
    gain2, shift2 = gains[:, 2:3], gains[:, 3:4]

    def project(p, half):
        i = SIDE * p + half
        x = tokens[pl.ds(pl.multiple_of(i * B, B), B), :].T.astype(f32)
        yield
        n1, _ = stats(x)
        f = (n1 * gain1 + shift1).astype(bf16)
        first[p, :, half * B : (half + 1) * B] = f
        yield
        where_t = i * B + lax.broadcasted_iota(jnp.int32, (8, B), 1)
        inside = ((where_t >= start_v) & (where_t < end_v)).astype(f32)
        zeros8 = jnp.zeros((8, B), f32)
        ones8 = jnp.ones((8, B), f32)
        key_side = jnp.concatenate([inside, ones8], axis=0).astype(bf16)
        query_side = jnp.concatenate([(1.0 - inside) * -BIG, zeros8], axis=0).astype(bf16)
        value_side = jnp.concatenate([ones8, zeros8], axis=0).astype(bf16)
        for h in range(HEADS):
            packed = mm(wqkv_t[h], f).astype(bf16)
            yield
            q, k, v = (packed[n * HD : (n + 1) * HD] for n in range(3))
            squares = packed.astype(f32)
            squares = squares * squares
            qn[h] = jnp.maximum(qn[h], jnp.sum(squares[:HD], axis=0, keepdims=True))
            kn[h] = jnp.maximum(kn[h], jnp.sum(squares[HD : 2 * HD], axis=0, keepdims=True))
            qf[h, i, :HD] = q
            qf[h, i, HD:] = query_side
            kf[h, i] = k
            vf[h, i, :HD] = v
            vf[h, i, HD:] = value_side
            kt[h, i] = jnp.concatenate([k, key_side], axis=0).T
            vt[h, i] = jnp.concatenate([v, value_side], axis=0).T
            acc[h, i] = jnp.zeros_like(acc[h, i])
            dk_acc[h, i] = jnp.zeros_like(dk_acc[h, i])
            dv_acc[h, i] = jnp.zeros_like(dv_acc[h, i])
            yield

    load[2].wait()
    together(project, tiles)

    bound = jnp.float32(0.0)
    for h in range(HEADS):
        bound = jnp.maximum(bound, jnp.max(qn[h]) * jnp.max(kn[h]))

    def scores(h, i, j):
        return mm(kt[h, j], qf[h, i])

    @pl.when(jnp.logical_not(bound * SCALE**2 <= LIMIT * LIMIT))
    def _():
        bounds[...] = jnp.full_like(bounds, MASKED)

        def top(t, carry):
            i, j = uq[t], uk[t]
            masked = jnp.where(allowed | (i != j), 0.0, MASKED)
            for h in range(HEADS):
                s = scores(h, i, j) + masked
                bounds[h, i] = jnp.maximum(bounds[h, i], jnp.max(s, axis=0, keepdims=True))
            return carry

        lax.fori_loop(1, units, top, 0)

        def shift(i, carry):
            for h in range(HEADS):
                one, two, three = split3(-bounds[h, i])
                r = lax.broadcasted_iota(jnp.int32, (16, B), 0)
                old = qf[h, i, HD : HD + 16].astype(f32)
                new = jnp.where(r == 8, one, jnp.where(r == 9, two, jnp.where(r == 10, three, old)))
                qf[h, i, HD : HD + 16] = new.astype(bf16)
            return carry

        lax.fori_loop(0, tiles, shift, 0)

    def weigh(t, slot, *kept_too):
        i, j = uq[t], uk[t]
        cut = causal[jnp.where(t >= units, 2, jnp.where(i == j, 1, 0))]
        for h in range(HEADS):
            p = jnp.minimum(jnp.exp2(scores(h, i, j) * SCALE).astype(bf16), cut)
            for ref in (probs.at[slot], *kept_too):
                ref[h] = p

    def weighted(t, block):
        i, j = uq[t], uk[t]
        for h in range(HEADS):
            acc[h, i] += mm(vf[h, j, : HD + 8], block[h])

    def forward(t, turn):
        weigh(t, t - 1, turns[turn])
        weighted(t - 1, turns[1 - turn])

    def forward_rest(t, carry):
        weigh(t, CAP)
        weighted(t, probs.at[CAP])
        return carry

    turns = (turn_a, turn_b)
    turn_b[...] = jnp.zeros_like(turn_b)
    in_steps(forward)
    weighted(last, turn_b)
    lax.fori_loop(CAP + 1, units, forward_rest, 0)

    def feed_grads():
        g_down[...] += mm_nt(hidden_s[...], cot_s[...])
        g_up[...] += mm_nt(pre_s[...], second_s[...])
        g_out[...] += mm_nt(heads_s[...], low_s[...])

    def write_tile(i, result, hbm):
        at = pl.ds(pl.multiple_of(i * B, B), B)
        return pltpu.make_async_copy(result.at[at], hbm.at[at], stores.at[i])

    def wait_tiles(result, hbm):
        def wait_tile(i, carry):
            write_tile(i, result, hbm).wait()
            return carry

        lax.fori_loop(0, tiles, wait_tile, 0)

    def feed(p, half):
        i = SIDE * p + half
        at = pl.ds(pl.multiple_of(i * B, B), B)
        lanes = slice(half * B, (half + 1) * B)
        if half == 0:
            feed_grads()
        outs, inv = [], []
        for h in range(HEADS):
            r = 1.0 / acc[h, i, HD : HD + 1]
            inv.append(r)
            outs.append(acc[h, i, :HD] * r)
            acc[h, i] = jnp.zeros_like(acc[h, i])
        heads = jnp.concatenate(outs, axis=0).astype(bf16)
        x = tokens[at, :].T.astype(f32)
        c16 = cot[at, :].T
        c32 = c16.astype(f32)
        yield
        resid = x + mm(wout_t[...], heads)
        yield
        n2, rate2 = stats(resid)
        second = (n2 * gain2 + shift2).astype(bf16)
        yield
        heads_s[:, lanes] = heads
        cot_s[:, lanes] = c16
        second_s[:, lanes] = second
        for c in range(0, FF, CHUNK):
            rows = slice(c, c + CHUNK)
            half_pre = mm(wup_t[rows], second)
            half_back = mm(wdown_t[rows], c16)
            yield
            twice_cdf = 1.0 + lax.erf(half_pre * 2.0**0.5)
            slope = half_pre * jnp.exp2(half_pre * half_pre * (-2.0 / math.log(2.0)) + PDF_SHIFT)
            hidden_s[rows, lanes] = (half_pre * twice_cdf).astype(bf16)
            pre_s[rows, lanes] = (half_back * (twice_cdf + slope)).astype(bf16)
            yield
        second_in = mm(wup[...], pre_s[:, lanes])
        yield
        cot[at, :] = (resid + mm(wdown[...], hidden_s[:, lanes])).astype(bf16).T
        g_norm[2] += lane_fold(second_in * n2)
        g_norm[3] += lane_fold(second_in)
        rg = c32 + norm_back(second_in, n2, rate2, gain2)
        low = rg.astype(bf16)
        yield
        hg = mm(wout[...], low).astype(bf16).astype(f32)
        resid_grad[i] = rg
        low_s[:, lanes] = low
        yield
        r8 = lax.broadcasted_iota(jnp.int32, (16, B), 0)
        for h in range(HEADS):
            do16 = (hg[h * HD : (h + 1) * HD] * inv[h]).astype(bf16)
            do = do16.astype(f32)
            delta = jnp.sum(do * outs[h], axis=0, keepdims=True)
            one, two, three = split3(-delta)
            extra = jnp.where(r8 == 0, one, jnp.where(r8 == 1, two, jnp.where(r8 == 2, three, 0.0)))
            dof[h, i, :HD] = do16
            dof[h, i, HD:] = extra.astype(bf16)
        write_tile(i, cot, mixed_hbm).start()

    load[3].wait()
    together(feed, tiles)
    feed_grads()

    def pushed(t, slot, block):
        i, j = uq[t], uk[t]
        for h in range(HEADS):
            w = probs[slot, h]
            pg = mm(vt[h, j], dof[h, i])
            block[h] = (w.astype(f32) * pg).astype(bf16)
            dv_acc[h, j] += mm_nt(dof[h, i, :HD], w)

    def pulled(t, block):
        i, j = uq[t], uk[t]
        for h in range(HEADS):
            acc[h, i, :HD] += mm(kf[h, j], block[h])
            dk_acc[h, j] += mm_nt(qf[h, i, :HD], block[h])

    def backward(t, turn):
        pushed(t, t - 1, turns[turn])
        pulled(t - 1, turns[1 - turn])

    def backward_rest(t, carry):
        weigh(t, CAP)
        pushed(t, CAP, turn_a)
        pulled(t, turn_a)
        return carry

    turn_b[...] = jnp.zeros_like(turn_b)
    in_steps(backward)
    pulled(last, turn_b)
    lax.fori_loop(CAP + 1, units, backward_rest, 0)

    wait_tiles(cot, mixed_hbm)

    def finish(p, half):
        i = SIDE * p + half
        at = pl.ds(pl.multiple_of(i * B, B), B)
        lanes = slice(half * B, (half + 1) * B)
        rows = []
        for h in range(HEADS):
            rows += [acc[h, i, :HD] * HD**-0.5, dk_acc[h, i] * HD**-0.5, dv_acc[h, i]]
        packed_grad = jnp.concatenate(rows, axis=0).astype(bf16)
        hidden_s[: 3 * D, lanes] = packed_grad
        yield
        first_in = mm(wqkv[...], packed_grad)
        if half == SIDE - 1:
            g_qkv[...] += mm_nt(hidden_s[: 3 * D, :], first[p])
        x = tokens[at, :].T.astype(f32)
        yield
        n1, rate1 = stats(x)
        yield
        g_norm[0] += lane_fold(first_in * n1)
        g_norm[1] += lane_fold(first_in)
        out = resid_grad[i] + norm_back(first_in, n1, rate1, gain1)
        yield
        tokens[at, :] = out.astype(bf16).T
        write_tile(i, tokens, igrad_hbm).start()

    together(finish, tiles)

    lane = lax.broadcasted_iota(jnp.int32, (D, 128), 1)
    norm = jnp.zeros((D, 128), f32)
    for c in range(4):
        norm = jnp.where(lane == c, jnp.sum(g_norm[c], axis=1, keepdims=True), norm)
    gains[...] = norm
    g_stage[...] = jnp.zeros_like(g_stage)
    for h in range(n_head):
        cols = slice(h * 128, (h + 1) * 128)
        qkv = g_qkv[h * 3 * HD : (h + 1) * 3 * HD].T
        up, down = g_up[cols].T, g_down[cols].T
        for d in range(n_dp):
            rows = slice(d * rd, (d + 1) * rd)
            at = (d * n_head + h) * ro
            g_stage[0:rd, : 3 * HD] = qkv[rows]
            g_stage[rd : 2 * rd] = up[rows]
            g_stage[2 * rd : 3 * rd] = down[rows]
            g_stage[3 * rd : 3 * rd + ro] = g_out[at : at + ro]
            g_stage[3 * rd + ro : 3 * rd + 2 * ro] = gains[at : at + ro]
            w_ref[h, d] = g_stage[...].astype(bf16)
    out = pltpu.make_async_copy(w_ref, grads_hbm, loads.at[0])
    out.start()
    wait_tiles(tokens, igrad_hbm)
    out.wait()


def layer(lengths, weights, tokens, cot, rd, ro):
    n_head, n_dp, rp = weights.shape[:3]
    tiles = tokens.shape[0] // B
    listed = tiles * (MAX_LEN // B + 1) + GROUP + 1
    vmem = lambda shape, dtype: pltpu.VMEM(shape, dtype)
    scratch = [
        pltpu.SMEM((listed,), jnp.int32),
        pltpu.SMEM((listed,), jnp.int32),
        pltpu.SMEM(lengths.shape, jnp.int32),
        vmem(weights.shape, bf16),
        vmem(tokens.shape, bf16),
        vmem(tokens.shape, bf16),
        pltpu.SemaphoreType.DMA((4,)),
        pltpu.SemaphoreType.DMA((tiles,)),
        vmem((HEADS, tiles, 1, B), f32),
        vmem((HEADS, 3 * HD, D), bf16),
        vmem((D, 3 * D), bf16),
        vmem((D, D), bf16),
        vmem((D, D), bf16),
        vmem((D, FF), bf16),
        vmem((FF, D), bf16),
        vmem((D, FF), bf16),
        vmem((FF, D), bf16),
        vmem((D, 128), f32),
        vmem((n_dp * rp, 128), f32),
        vmem((HEADS, tiles, 48, B), bf16),
        vmem((HEADS, tiles, HD, B), bf16),
        vmem((HEADS, tiles, 48, B), bf16),
        vmem((HEADS, tiles, B, 48), bf16),
        vmem((HEADS, tiles, B, 48), bf16),
        vmem((HEADS, tiles, 48, B), bf16),
        vmem((CAP + 1, HEADS, B, B), bf16),
        vmem((HEADS, B, B), bf16),
        vmem((HEADS, B, B), bf16),
        vmem((HEADS, tiles, HD + 8, B), f32),
        vmem((HEADS, tiles, HD, B), f32),
        vmem((HEADS, tiles, HD, B), f32),
        vmem((tiles, D, B), f32),
        vmem((tiles // SIDE, D, WIDE), bf16),
        vmem((D, WIDE), bf16),
        vmem((D, WIDE), bf16),
        vmem((D, WIDE), bf16),
        vmem((D, WIDE), bf16),
        vmem((FF, WIDE), bf16),
        vmem((FF, WIDE), bf16),
        vmem((3, B, B), bf16),
        vmem((HEADS, 1, B), f32),
        vmem((HEADS, 1, B), f32),
        vmem((3 * D, D), f32),
        vmem((D, D), f32),
        vmem((FF, D), f32),
        vmem((FF, D), f32),
        vmem((4, D, 128), f32),
        vmem((rp, 128), f32),
    ]
    return pl.pallas_call(
        functools.partial(layer_kernel, rd, ro),
        out_shape=(
            jax.ShapeDtypeStruct(tokens.shape, bf16),
            jax.ShapeDtypeStruct(tokens.shape, bf16),
            jax.ShapeDtypeStruct((n_head, n_dp, rp, 128), bf16),
        ),
        in_specs=[HBM] * 4,
        out_specs=(HBM, HBM, HBM),
        scratch_shapes=scratch,
        compiler_params=pltpu.CompilerParams(vmem_limit_bytes=63 * 1024 * 1024),
    )(lengths, weights, tokens, cot)


def factors(n_dp, n_head):
    if (n_dp, n_head) == (8, 4):
        return (("head", 2, 2), ("head", 1, 2), ("dp", 2, 4), ("dp", 1, 2)), (2, (0, 3), 1)
    own = 2 if n_dp % 2 == 0 else 1
    far = 4 if n_dp // own % 4 == 0 else 1
    near = n_dp // own // far
    return (("head", 1, n_head), ("dp", own * far, near), ("dp", own, far), ("dp", 1, own)), (2, (0, 1), 3)


def digit(axis, stride, size):
    return lax.rem(lax.div(lax.axis_index(axis), stride), size)


def others(axes, group):
    found = []
    for offsets in itertools.product(*(range(axes[a][2]) for a in group)):
        if not any(offsets):
            continue
        place, theirs, source = {}, {}, {}
        for a, offset in zip(group, offsets):
            axis, stride, size = axes[a]
            mine = digit(*axes[a])
            theirs[a] = lax.rem(mine + offset, size)
            source[a] = lax.rem(mine + size - offset, size)
            place[axis] = place.get(axis, lax.axis_index(axis)) + (theirs[a] - mine) * stride
        found.append((place, theirs, source))
    return found


def greet(peers):
    barrier = pltpu.get_barrier_semaphore()
    for device, _, _ in peers:
        pl.semaphore_signal(barrier, inc=1, device_id=device, device_id_type=MESH)
    return lambda: pl.semaphore_wait(barrier, len(peers))


class Links:
    def __init__(self, send, recv):
        self.send, self.recv, self.count, self.started = send, recv, 0, []

    def copy(self, n, src, dst, place):
        return pltpu.make_async_remote_copy(
            src_ref=src,
            dst_ref=dst,
            send_sem=self.send.at[n],
            recv_sem=self.recv.at[n],
            device_id=place,
            device_id_type=MESH,
        )

    def start(self, src, dst, place, lands):
        n = self.count
        self.count += 1
        out = self.copy(n, src, dst, place)
        out.start()
        self.started.append(out)
        return self.copy(n, lands, lands, place).wait_recv

    def drain(self):
        for out in self.started:
            out.wait_send()


def gather_kernel(axes, roles, *refs):
    masters, w_ref = refs[:5], refs[5]
    held, (stage, block, local, send, recv) = refs[6:11], refs[11:]
    far, near, own = roles
    line, plane, chip = others(axes, (far,)), others(axes, near), others(axes, (own,))
    arrived = greet(line + plane + chip)
    loads = [pltpu.make_async_copy(m, h, local.at[n]) for n, (m, h) in enumerate(zip(masters, held))]
    for load in loads:
        load.start()
    stage[...] = jnp.zeros_like(stage)
    for load in loads:
        load.wait()
    qkv, out, up, down, norm = held
    rd, ro = qkv.shape[0], out.shape[0]
    at = 0
    for part, height in ((qkv, rd), (up, rd), (down, rd), (out, ro), (norm, ro)):
        stage[at : at + height, : part.shape[1]] = part[...]
        at += height
    block[...] = stage[...].astype(bf16)
    mine = {a: digit(*axes[a]) for a in range(4)}
    at = lambda digits: w_ref.at[tuple({**mine, **digits}[a] for a in range(4))]
    keep = pltpu.make_async_copy(block, at({}), local.at[0])
    keep.start()
    arrived()
    links = Links(send, recv)
    first = [links.start(block, at({}), place, at(source)) for place, _, source in line]

    def onward(src, digits):
        dst = at(digits)
        waits = [
            (links.start(src, dst, place, at({**digits, **source})), {**digits, **source})
            for place, _, source in plane
        ]
        return waits, [links.start(src, dst, place, at({**digits, **source})) for place, _, source in chip]

    second, third = onward(block, {})
    for wait, (_, _, source) in zip(first, line):
        wait()
        waits, more = onward(at(source), source)
        second += waits
        third += more
    for wait, digits in second:
        wait()
        third += [
            links.start(at(digits), at(digits), place, at({**digits, **source})) for place, _, source in chip
        ]
    for wait in third:
        wait()
    links.drain()
    keep.wait()


def gather(axes, roles, rows, masters, cid=0):
    sizes = [size for _, _, size in axes]
    copies = math.prod(sizes)
    return pl.pallas_call(
        functools.partial(gather_kernel, axes, roles),
        out_shape=jax.ShapeDtypeStruct(tuple(sizes) + (rows, 128), bf16),
        in_specs=[HBM] * 5,
        out_specs=HBM,
        scratch_shapes=[pltpu.VMEM(m.shape, f32) for m in masters]
        + [
            pltpu.VMEM((rows, 128), f32),
            pltpu.VMEM((rows, 128), bf16),
            pltpu.SemaphoreType.DMA((5,)),
            pltpu.SemaphoreType.DMA((copies,)),
            pltpu.SemaphoreType.DMA((copies,)),
        ],
        compiler_params=pltpu.CompilerParams(
            collective_id=cid, has_side_effects=True, vmem_limit_bytes=62 * 1024 * 1024
        ),
    )(*masters)


def scatter_kernel(axes, roles, g_ref, red_ref, sq_ref, *scratch):
    held, from_chip, partial, from_plane, passed, from_line, sq_chip, sq_all, local, send, recv = scratch
    far, near, own = roles
    line, plane, chip = others(axes, (far,)), others(axes, near), others(axes, (own,))
    every = others(axes, tuple(sorted((far,) + near)))
    ready = greet(chip + every)
    mine = {a: digit(*axes[a]) for a in range(4)}
    pick = lambda digits: g_ref.at[tuple(digits.get(a, slice(None)) for a in range(4))]
    pieces = [theirs for _, theirs, _ in line] + [{far: mine[far]}]
    loads = []
    for k, piece in enumerate(pieces):
        loads.append(pltpu.make_async_copy(pick({**piece, own: mine[own]}), held.at[k], local.at[k]))
        loads[-1].start()
    ready()
    links = Links(send, recv)
    first = [
        [
            links.start(pick({**piece, **theirs}), from_chip.at[k, n], place, from_chip.at[k, n])
            for n, (place, theirs, _) in enumerate(chip)
        ]
        for k, piece in enumerate(pieces)
    ]
    second = []
    inner = lambda digits: tuple(digits[a] for a in near)
    for k in range(len(pieces)):
        loads[k].wait()
        total = held[k].astype(f32)
        for n, wait in enumerate(first[k]):
            wait()
            total = total + from_chip[k, n].astype(f32)
        partial[k] = total.astype(bf16)
        second.append(
            [
                links.start(partial.at[(k,) + inner(theirs)], from_plane.at[k, n], place, from_plane.at[k, n])
                for n, (place, theirs, _) in enumerate(plane)
            ]
        )
    third = []
    for k in range(len(pieces)):
        total = partial[(k,) + inner(mine)].astype(f32)
        for n, wait in enumerate(second[k]):
            wait()
            total = total + from_plane[k, n].astype(f32)
        if k < len(line):
            passed[k] = total.astype(bf16)
            third.append(links.start(passed.at[k], from_line.at[k], line[k][0], from_line.at[k]))
    for n, wait in enumerate(third):
        wait()
        total = total + from_line[n].astype(f32)
    red_ref[...] = total
    square = total * total
    fold = square[0:8]
    for r in range(8, square.shape[0], 8):
        fold = fold + square[r : r + 8]
    fold = jnp.sum(fold, axis=0, keepdims=True)
    for group, peers, ref in (((own,), chip, sq_chip), (tuple(sorted((far,) + near)), every, sq_all)):
        at = lambda digits: ref.at[tuple(digits[a] for a in group)]
        ref[tuple(mine[a] for a in group)] = fold
        waits = [links.start(at(mine), at(mine), place, at(source)) for place, _, source in peers]
        for wait in waits:
            wait()
        fold = 0.0
        for index in itertools.product(*(range(axes[a][2]) for a in group)):
            fold = fold + ref[index]
    sq_ref[...] = fold
    links.drain()


def scatter(axes, roles, grads, cid=1):
    sizes = [size for _, _, size in axes]
    far, near, own = roles
    block = grads.shape[-2:]
    spread = tuple(sizes[a] for a in range(4) if a in near) + block
    nf, np_, no = sizes[far], math.prod(sizes[a] for a in near), sizes[own]
    least = lambda n: max(n, 1)
    copies = nf * (no - 1) + nf * (np_ - 1) + (nf - 1) + (no - 1) + (nf * np_ - 1)
    together = tuple(sizes[a] for a in sorted((far,) + near))
    return pl.pallas_call(
        functools.partial(scatter_kernel, axes, roles),
        out_shape=(jax.ShapeDtypeStruct(block, f32), jax.ShapeDtypeStruct((1, 128), f32)),
        in_specs=[HBM],
        out_specs=(WHOLE, WHOLE),
        scratch_shapes=[
            pltpu.VMEM((nf,) + spread, bf16),
            pltpu.VMEM((nf, least(no - 1)) + spread, bf16),
            pltpu.VMEM((nf,) + spread, bf16),
            pltpu.VMEM((nf, least(np_ - 1)) + block, bf16),
            pltpu.VMEM((least(nf - 1),) + block, bf16),
            pltpu.VMEM((least(nf - 1),) + block, bf16),
            pltpu.VMEM((no, 1, 128), f32),
            pltpu.VMEM(together + (1, 128), f32),
            pltpu.SemaphoreType.DMA((nf,)),
            pltpu.SemaphoreType.DMA((copies,)),
            pltpu.SemaphoreType.DMA((copies,)),
        ],
        compiler_params=pltpu.CompilerParams(
            collective_id=cid, has_side_effects=True, vmem_limit_bytes=62 * 1024 * 1024
        ),
    )(grads)


def adam(weight, first, second, grad, factor, rate, decay):
    clipped = grad * factor
    first_new = BETA_ONE * first + (1.0 - BETA_ONE) * clipped
    second_new = BETA_TWO * second + (1.0 - BETA_TWO) * clipped * clipped
    direction = (
        first_new
        / (1.0 - BETA_ONE**STEP)
        / (jnp.sqrt(second_new / (1.0 - BETA_TWO**STEP)) + ADAM_EPS)
    )
    return weight - rate * (direction + decay * weight), first_new, second_new


def update_kernel(*refs):
    held = refs[-18:-1]
    copies = [pltpu.make_async_copy(src, dst, refs[-1].at[n]) for n, (src, dst) in enumerate(zip(refs, held))]
    for copy in copies:
        copy.start()
    for copy in copies:
        copy.wait()
    (red, sq, *params), outs = held, refs[17:-18]
    rd, ro = params[0].shape[0], params[1].shape[0]
    norm = jnp.sqrt(jnp.sum(sq[...], keepdims=True))
    outs[0][...] = norm
    factor = jnp.minimum(1.0, CLIP_NORM / norm)
    rows = (0, 3 * rd, rd, 2 * rd, 3 * rd + ro)
    rates = (0.1, 0.5, 0.1, 0.1, 0.5)
    decays = (DECAY, DECAY, DECAY, DECAY, 0.0)
    for w in range(5):
        height, width = params[w].shape
        grad = red[rows[w] : rows[w] + height, :width]
        new, first_new, second_new = adam(
            params[w][...], params[5 + w][...], params[10 + w][...], grad, factor, rates[w], decays[w]
        )
        outs[1 + 3 * w][...] = new
        outs[2 + 3 * w][...] = first_new
        outs[3 + 3 * w][...] = second_new
        outs[16 + w][...] = grad
        outs[21 + w][...] = new.astype(bf16)


def update(red, sq, params):
    like = lambda p, dtype: jax.ShapeDtypeStruct(p.shape, dtype)
    shapes = [jax.ShapeDtypeStruct((1, 1), f32)]
    shapes += [like(p, f32) for p in params[:5] for _ in range(3)]
    shapes += [like(p, f32) for p in params[:5]]
    shapes += [like(p, bf16) for p in params[:5]]
    return pl.pallas_call(
        update_kernel,
        out_shape=shapes,
        in_specs=[HBM] * 17,
        out_specs=[WHOLE] * len(shapes),
        scratch_shapes=[pltpu.VMEM(a.shape, f32) for a in (red, sq, *params)] + [pltpu.SemaphoreType.DMA((17,))],
        compiler_params=pltpu.CompilerParams(vmem_limit_bytes=62 * 1024 * 1024),
    )(red, sq, *params)


def per_device(n_dp, n_head, tokens, cotangent, lengths, *params):
    masters = params[:5]
    rd, ro = masters[0].shape[0], masters[1].shape[0]
    rows = -(-(3 * rd + 2 * ro) // 16) * 16
    axes, roles = factors(n_dp, n_head)
    weights = gather(axes, roles, rows, masters).reshape(n_head, n_dp, rows, 128)
    mixed, input_grad, grads = layer(lengths, weights, tokens, cotangent, rd, ro)
    grads = grads.reshape(tuple(size for _, _, size in axes) + (rows, 128))
    red, sq = scatter(axes, roles, grads)
    outs = update(red, sq, params)
    return (mixed, input_grad, outs[0].reshape(()), *outs[1:])


def solution(mesh):
    both, split, lens = P(("dp", "head"), None), P("dp", "head"), P("dp", None)
    weight = (split, both, split, split, both)
    return jax.shard_map(
        functools.partial(per_device, mesh.shape["dp"], mesh.shape["head"]),
        mesh=mesh,
        in_specs=(both, both, lens) + weight * 3,
        out_specs=(both, both, P())
        + tuple(spec for spec in weight for _ in range(3))
        + weight
        + weight,
        check_vma=False,
    )
```
